512 devices in a mesh: epoch: 4 (over x), batch: 32 (over y, z_lo), mem: 4 (over z_hi, core).
Axes of the slice: x: 4, y: 4, z: 16 (z_hi: 2, z_lo: 8; z = z_hi * 8 + z_lo), core: 2. Of those that a mesh axis runs over, the one named last changes fastest.
Arguments:
- node_memory: bfloat16 [65536, 512], P(('batch', 'mem')), may hold values from -3 to 3
- neighbour_ids: int32 [10, 65536], P(None, ('batch', 'mem')), may hold values from 0 to 511
- neighbour_ticks: int32 [10, 65536], P(None, ('batch', 'mem')), may hold values from 0 to 999
- source_ids: int32 [4, 2, 32768], P('epoch', None, ('batch', 'mem')), may hold values from 0 to 511
- target_ids: int32 [4, 2, 32768], P('epoch', None, ('batch', 'mem')), may hold values from 0 to 511, as said below
- negative_ids: int32 [4, 2, 32768], P('epoch', None, ('batch', 'mem')), may hold values from 0 to 511
- event_ticks: int32 [4, 2, 32768], P('epoch', None, ('batch', 'mem')), may hold values from 1000 to 4999
- gru_input: bfloat16 [512, 1536], replicated, may hold values from -0.25 to 0.25
- gru_state: bfloat16 [512, 1536], replicated, may hold values from -0.25 to 0.25
- decoder_weight: bfloat16 [512, 256], replicated, may hold values from -0.25 to 0.25
Outputs:
- memory_out: bfloat16 [4, 65536, 512], P('epoch', ('batch', 'mem'))
- decoder_out: float32 [4, 512, 256], P('epoch')
- logits_out: float32 [4, 4, 32768], P('epoch', None, ('batch', 'mem'))
The draws below stay inside these ranges and needn't reach their ends.
Inputs may be any that keep to these rules, and one draw needn't show every extreme that they name: `target_ids`: within one device's 256 events of one mini-batch the targets are distinct, and the last row of the block is among them.
All inputs are finite; a program needn't handle non-finite values.
Results may differ from the reference program's by a relative error of at most 0.0034.
Values may be sent and summed in bfloat16 or wider, within the bound.
A program may use at most 64 MiB of HBM per device.

```python
import jax
import jax.numpy as jnp
from jax import lax

M = 512
H = 256
K = 10
EV = 256
NODE_DEV = 512
BLOCKS = 128
EVENTS = 32768
NODES = 65536
N_EPOCH = 4


def draw_target_ids(key, part):
    key = jax.random.fold_in(key, 7)
    keys = jax.random.split(key, N_EPOCH * 2 * BLOCKS)

    def pick(single):
        first_key, second_key = jax.random.split(single)
        lower = jax.random.permutation(first_key, NODE_DEV - 1)[:EV - 1]
        chosen = jnp.concatenate([lower, jnp.full((1,), NODE_DEV - 1, jnp.int32)])
        order = jax.random.permutation(second_key, EV)
        return chosen[order]
    rows = jax.vmap(pick)(keys)
    return rows.reshape(N_EPOCH, 2, EVENTS).astype(jnp.int32)


def set_ends(result, stream_key, least, largest):
    longest = result.shape.index(max(result.shape))
    spots = []
    for shift in (0, 1):
        where = [jax.random.randint(jax.random.fold_in(stream_key, axis), (), 0, length) for axis, length in enumerate(result.shape)]
        where[longest] = (where[longest] + shift) % result.shape[longest]
        spots.append(tuple(where))
    return result.at[spots[0]].set(least).at[spots[1]].set(largest)


def shard_levels(key, shape, shards, least, top_value):
    loudness, own = 1.0, jax.random.fold_in(key, 6)
    for position, shards_of in shards:
        draws = jnp.exp(jax.random.uniform(jax.random.fold_in(own, position), (shards_of,), jnp.float32, least / len(shards), top_value / len(shards)))
        loudness = loudness * jnp.repeat(draws, shape[position] // shards_of).reshape([-1 if axis == position else 1 for axis in range(len(shape))])
    return loudness


def bell_draw(key, shape, scale, limit, cuts=(), kind=jnp.bfloat16):
    entries = scale * jax.random.normal(key, shape, jnp.float32)
    if cuts:
        entries = entries * shard_levels(key, shape, cuts, -0.22, 0.18)
    return jnp.clip(entries, -limit, limit).astype(kind)


def setup_inputs(seed: int = 0) -> dict:
    streams_of = jax.random.split(jax.random.key(seed), 11)
    node_memory = bell_draw(streams_of[0], (NODES, M), 0.5, 3.0, ((0, 128),))
    neighbour_ids = set_ends(jax.random.randint(streams_of[1], (K, NODES), 0, NODE_DEV), jax.random.fold_in(streams_of[1], 1), 0, NODE_DEV - 1).astype(jnp.int32)
    neighbour_ticks = set_ends(jax.random.randint(streams_of[2], (K, NODES), 0, 1000), jax.random.fold_in(streams_of[2], 1), 0, 999).astype(jnp.int32)
    source_ids = set_ends(jax.random.randint(streams_of[3], (N_EPOCH, 2, EVENTS), 0, NODE_DEV), jax.random.fold_in(streams_of[3], 1), 0, NODE_DEV - 1).astype(jnp.int32)
    target_ids = draw_target_ids(jax.random.fold_in(streams_of[10], 71), 0)
    negative_ids = set_ends(jax.random.randint(streams_of[5], (N_EPOCH, 2, EVENTS), 0, NODE_DEV), jax.random.fold_in(streams_of[5], 1), 0, NODE_DEV - 1).astype(jnp.int32)
    event_ticks = set_ends(jax.random.randint(streams_of[6], (N_EPOCH, 2, EVENTS), 1000, 5000), jax.random.fold_in(streams_of[6], 1), 1000, 4999).astype(jnp.int32)
    gru_input = bell_draw(streams_of[7], (M, 3 * M), M ** -0.5, 0.25)
    gru_state = bell_draw(streams_of[8], (M, 3 * M), M ** -0.5, 0.25)
    decoder_weight = bell_draw(streams_of[9], (M, H), M ** -0.5, 0.25)
    return dict(node_memory=node_memory, neighbour_ids=neighbour_ids, neighbour_ticks=neighbour_ticks, source_ids=source_ids, target_ids=target_ids, negative_ids=negative_ids, event_ticks=event_ticks, gru_input=gru_input, gru_state=gru_state, decoder_weight=decoder_weight)


tick_scale = 100.0
step_length = 4.0
epsilon = 1e-06

def fresh_memory(memory_block, near_table, near_times, source, target, ticks, gru_input, gru_state):
    width = memory_block.shape[1]
    source_rows = memory_block[source]
    target_rows = memory_block[target]
    near_ids = near_table[:, target]
    near_ticks = near_times[:, target]
    decay = tick_scale / (tick_scale + (ticks[None, :] - near_ticks).astype(jnp.float32))
    near_rows = memory_block[near_ids].astype(jnp.float32)
    aggregate = jnp.einsum('ke,kem->em', decay, near_rows) / lax.optimization_barrier(jnp.sum(decay, axis=0))[:, None]
    input_gates = jnp.dot(source_rows, gru_input, preferred_element_type=jnp.float32)
    state_gates = jnp.dot(target_rows, gru_state, preferred_element_type=jnp.float32)
    reset = jax.nn.sigmoid(input_gates[:, :width] + state_gates[:, :width])
    update = jax.nn.sigmoid(input_gates[:, width:2 * width] + state_gates[:, width:2 * width])
    candidate = jnp.tanh(input_gates[:, 2 * width:] + reset * state_gates[:, 2 * width:])
    fresh = ((1.0 - update) * candidate + update * target_rows.astype(jnp.float32)).astype(jnp.bfloat16)
    return (fresh, aggregate)

def link_terms(memory_block, source, target, negative, aggregate, decoder_bf):
    scale = 1.0 / jnp.sqrt(jnp.float32(decoder_bf.shape[1]))
    source_rows = memory_block[source]
    target_rows = memory_block[target]
    negative_rows = memory_block[negative]
    target_embed = (0.5 * (target_rows.astype(jnp.float32) + aggregate)).astype(jnp.bfloat16)
    proj_source = jnp.dot(source_rows, decoder_bf, preferred_element_type=jnp.float32)
    proj_target = jnp.dot(target_embed, decoder_bf, preferred_element_type=jnp.float32)
    proj_negative = jnp.dot(negative_rows, decoder_bf, preferred_element_type=jnp.float32)
    positive = lax.optimization_barrier(jnp.sum(proj_source * proj_target, axis=1)) * scale
    negative_logit = lax.optimization_barrier(jnp.sum(proj_source * proj_negative, axis=1)) * scale
    grad_positive = -jax.nn.sigmoid(-positive) * scale
    grad_negative = jax.nn.sigmoid(negative_logit) * scale
    delta_source = (grad_positive[:, None] * proj_target + grad_negative[:, None] * proj_negative).astype(jnp.bfloat16)
    delta_target = (grad_positive[:, None] * proj_source).astype(jnp.bfloat16)
    delta_negative = (grad_negative[:, None] * proj_source).astype(jnp.bfloat16)
    gradient = jnp.dot(source_rows.T, delta_source, preferred_element_type=jnp.float32)
    gradient = gradient + jnp.dot(target_embed.T, delta_target, preferred_element_type=jnp.float32)
    gradient = gradient + jnp.dot(negative_rows.T, delta_negative, preferred_element_type=jnp.float32)
    return (positive, negative_logit, gradient)

def reference(node_memory, neighbour_ids, neighbour_ticks, source_ids, target_ids, negative_ids, event_ticks, gru_input, gru_state, decoder_weight):
    blocks_memory = node_memory.reshape(BLOCKS, NODE_DEV, M)
    near_table = neighbour_ids.reshape(K, BLOCKS, NODE_DEV).transpose(1, 0, 2)
    near_times = neighbour_ticks.reshape(K, BLOCKS, NODE_DEV).transpose(1, 0, 2)

    def run_batch(memory_blocks, trainer, batch_index, master):
        decoder_bf = master.astype(jnp.bfloat16)
        source = source_ids[trainer, batch_index].reshape(BLOCKS, EV)
        target = target_ids[trainer, batch_index].reshape(BLOCKS, EV)
        negative = negative_ids[trainer, batch_index].reshape(BLOCKS, EV)
        ticks = event_ticks[trainer, batch_index].reshape(BLOCKS, EV)

        def one_block(items):
            block, table, times, src, tgt, neg, tck = items
            fresh, aggregate = fresh_memory(block, table, times, src, tgt, tck, gru_input, gru_state)
            updated = block.at[tgt].set(fresh)
            positive, negative_logit, gradient = link_terms(block, src, tgt, neg, aggregate, decoder_bf)
            return (updated, positive, negative_logit, gradient)
        updated, positive, negative_logit, gradient = lax.map(one_block, (memory_blocks, near_table, near_times, source, target, negative, ticks))
        total = lax.optimization_barrier(jnp.sum(gradient, axis=0))
        step = total / jnp.sqrt(jnp.sum(total * total) + epsilon)
        return (updated, positive.reshape(EVENTS), negative_logit.reshape(EVENTS), master - step_length * step)
    start = decoder_weight.astype(jnp.float32)
    first = [run_batch(blocks_memory, trainer, 0, start) for trainer in range(N_EPOCH)]
    memories = []
    decoders = []
    logit_rows = []
    for trainer in range(N_EPOCH):
        handed = first[(trainer - 1) % N_EPOCH][0]
        updated, positive, negative_logit, master = run_batch(handed, trainer, 1, first[trainer][3])
        memories.append(updated.reshape(NODES, M))
        decoders.append(master)
        logit_rows.append(jnp.stack([first[trainer][1], first[trainer][2], positive, negative_logit]))
    return (jnp.stack(memories), jnp.stack(decoders), jnp.stack(logit_rows))
```

```python
import jax
import jax.numpy as jnp
from jax import lax
from jax.experimental import pallas as pl
from jax.experimental.pallas import tpu as pltpu
from jax.sharding import PartitionSpec as P

tick_scale = 100.0
step_length = 4.0
epsilon = 1e-06


def passed_along(array, axis, by):
    length = lax.axis_size(axis)
    return lax.ppermute(array, axis, [(i, (i + by) % length) for i in range(length)])


def fresh_memory(memory_block, near_table, near_times, source, target, ticks, gru_input, gru_state):
    width = memory_block.shape[1]
    source_rows = jnp.take(memory_block, source, axis=0)
    target_rows = jnp.take(memory_block, target, axis=0)
    near_ids = jnp.take(near_table, target, axis=1)
    near_ticks = jnp.take(near_times, target, axis=1)
    decay = tick_scale / (tick_scale + (ticks[None, :] - near_ticks).astype(jnp.float32))
    summed = jnp.zeros((target.shape[0], width), jnp.float32)
    for slot in range(near_ids.shape[0]):
        near_rows = jnp.take(memory_block, near_ids[slot], axis=0)
        summed = summed + decay[slot][:, None] * near_rows.astype(jnp.float32)
    aggregate = summed / jnp.sum(decay, axis=0)[:, None]
    input_gates = jnp.dot(source_rows, gru_input, preferred_element_type=jnp.float32)
    state_gates = jnp.dot(target_rows, gru_state, preferred_element_type=jnp.float32)
    reset = jax.nn.sigmoid(input_gates[:, :width] + state_gates[:, :width])
    update = jax.nn.sigmoid(input_gates[:, width : 2 * width] + state_gates[:, width : 2 * width])
    candidate = jnp.tanh(input_gates[:, 2 * width :] + reset * state_gates[:, 2 * width :])
    fresh = ((1.0 - update) * candidate + update * target_rows.astype(jnp.float32)).astype(
        jnp.bfloat16
    )
    return (fresh, aggregate)


def link_terms(memory_block, source, target, negative, aggregate, decoder_bf):
    scale = 1.0 / jnp.sqrt(jnp.float32(decoder_bf.shape[1]))
    source_rows = jnp.take(memory_block, source, axis=0)
    target_rows = jnp.take(memory_block, target, axis=0)
    negative_rows = jnp.take(memory_block, negative, axis=0)
    target_embed = (0.5 * (target_rows.astype(jnp.float32) + aggregate)).astype(jnp.bfloat16)
    stacked = jnp.concatenate([source_rows, target_embed, negative_rows], axis=0)
    projected = jnp.dot(stacked, decoder_bf, preferred_element_type=jnp.float32)
    count = source.shape[0]
    proj_source = projected[:count]
    proj_target = projected[count : 2 * count]
    proj_negative = projected[2 * count :]
    positive = jnp.sum(proj_source * proj_target, axis=1) * scale
    negative_logit = jnp.sum(proj_source * proj_negative, axis=1) * scale
    grad_positive = -jax.nn.sigmoid(-positive) * scale
    grad_negative = jax.nn.sigmoid(negative_logit) * scale
    delta_source = (
        grad_positive[:, None] * proj_target + grad_negative[:, None] * proj_negative
    ).astype(jnp.bfloat16)
    delta_target = (grad_positive[:, None] * proj_source).astype(jnp.bfloat16)
    delta_negative = (grad_negative[:, None] * proj_source).astype(jnp.bfloat16)
    deltas = jnp.concatenate([delta_source, delta_target, delta_negative], axis=0)
    gradient = lax.dot_general(
        stacked, deltas, (((0,), (0,)), ((), ())), preferred_element_type=jnp.float32
    )
    return (positive, negative_logit, gradient)


MESH = pl.DeviceIdType.MESH
near_peers = [(y, c) for y in range(4) for c in range(2) if (y, c) != (0, 0)]
ring = 16


def place():
    batch, mem = lax.axis_index("batch"), lax.axis_index("mem")
    return batch // 8, (mem // 2) * 8 + batch % 8, mem % 2


def device_at(y, z, core):
    return {"batch": y * 8 + z % 8, "mem": (z // 8) * 2 + core}


def sum_kernel(
    gradient,
    total,
    rounded,
    near_in,
    piece,
    far_in,
    all_parts,
    joined,
    near_send,
    near_recv,
    far_send,
    far_recv,
    back_send,
    back_recv,
    last_send,
    last_recv,
):
    y, z, core = place()
    rows = 64
    near = [(dy * 2 + dc, (y + dy) % 4, (core + dc) % 2) for dy, dc in near_peers]
    barrier = pltpu.get_barrier_semaphore()
    for _, to_y, to_core in near:
        pl.semaphore_signal(
            barrier, 1, device_id=device_at(to_y, z, to_core), device_id_type=MESH
        )
    for step in range(1, ring):
        pl.semaphore_signal(
            barrier, 1, device_id=device_at(y, (z + step) % ring, core), device_id_type=MESH
        )
    rounded[...] = gradient[...].astype(jnp.bfloat16)
    pl.semaphore_wait(barrier, len(near) + ring - 1)

    near_copies = []
    for slot, to_y, to_core in near:
        row = pl.multiple_of((to_y * 2 + to_core) * rows, rows)
        copy = pltpu.make_async_remote_copy(
            src_ref=rounded.at[pl.ds(row, rows)],
            dst_ref=near_in.at[slot],
            send_sem=near_send.at[slot],
            recv_sem=near_recv.at[slot],
            device_id=device_at(to_y, z, to_core),
            device_id_type=MESH,
        )
        copy.start()
        near_copies.append((slot, copy))
    own = pl.multiple_of((y * 2 + core) * rows, rows)
    value = gradient[pl.ds(own, rows), :]
    for slot, copy in near_copies:
        copy.wait_recv()
        value = value + near_in[slot].astype(jnp.float32)
    for part in range(ring):
        row, column = (part % 8) * 8, (part // 8) * 128
        piece[part] = value[row : row + 8, column : column + 128]

    far_copies = []
    for step in range(1, ring):
        to_z = (z + step) % ring
        copy = pltpu.make_async_remote_copy(
            src_ref=piece.at[to_z],
            dst_ref=far_in.at[step],
            send_sem=far_send.at[step],
            recv_sem=far_recv.at[step],
            device_id=device_at(y, to_z, core),
            device_id_type=MESH,
        )
        copy.start()
        far_copies.append(copy)
    part_total = piece[z]
    for step, copy in enumerate(far_copies, 1):
        copy.wait_recv()
        part_total = part_total + far_in[step]
    all_parts[z] = part_total

    back_copies = []
    for step in range(1, ring):
        copy = pltpu.make_async_remote_copy(
            src_ref=all_parts.at[z],
            dst_ref=all_parts.at[z],
            send_sem=back_send.at[step],
            recv_sem=back_recv.at[step],
            device_id=device_at(y, (z + step) % ring, core),
            device_id_type=MESH,
        )
        copy.start()
        back_copies.append(copy)
    for copy in back_copies:
        copy.wait_recv()
    for part in range(ring):
        row, column = (part % 8) * 8, (part // 8) * 128
        joined[pl.ds(pl.multiple_of(own + row, 8), 8), column : column + 128] = all_parts[part]
    rounded_own = joined[pl.ds(own, rows), :].astype(jnp.bfloat16)
    total[pl.ds(own, rows), :] = rounded_own

    last_copies = []
    for slot, to_y, to_core in near:
        copy = pltpu.make_async_remote_copy(
            src_ref=total.at[pl.ds(own, rows)],
            dst_ref=total.at[pl.ds(own, rows)],
            send_sem=last_send.at[slot],
            recv_sem=last_recv.at[slot],
            device_id=device_at(to_y, z, to_core),
            device_id_type=MESH,
        )
        copy.start()
        last_copies.append(copy)
    for copy in last_copies:
        copy.wait_recv()
    for _, copy in near_copies:
        copy.wait_send()
    for copy in far_copies + back_copies + last_copies:
        copy.wait_send()


def summed_over_trainer(gradient, collective_id):
    height, width = gradient.shape
    dma = pltpu.SemaphoreType.DMA
    return pl.pallas_call(
        sum_kernel,
        out_shape=jax.ShapeDtypeStruct((height, width), jnp.bfloat16),
        in_specs=[pl.BlockSpec(memory_space=pltpu.VMEM)],
        out_specs=pl.BlockSpec(memory_space=pltpu.VMEM),
        scratch_shapes=[
            pltpu.VMEM((height, width), jnp.bfloat16),
            pltpu.VMEM((8, height // 8, width), jnp.bfloat16),
            pltpu.VMEM((ring, 8, 128), jnp.float32),
            pltpu.VMEM((ring, 8, 128), jnp.float32),
            pltpu.VMEM((ring, 8, 128), jnp.float32),
            pltpu.VMEM((height, width), jnp.float32),
            dma((8,)),
            dma((8,)),
            dma((ring,)),
            dma((ring,)),
            dma((ring,)),
            dma((ring,)),
            dma((8,)),
            dma((8,)),
        ],
        compiler_params=pltpu.CompilerParams(collective_id=collective_id, has_side_effects=True),
    )(gradient)


def take_step(master, gradient, collective_id):
    total = summed_over_trainer(gradient, collective_id).astype(jnp.float32)
    return master - step_length * total / jnp.sqrt(jnp.sum(total * total) + epsilon)


def on_device(
    node_memory,
    neighbour_ids,
    neighbour_ticks,
    source_ids,
    target_ids,
    negative_ids,
    event_ticks,
    gru_input,
    gru_state,
    decoder_weight,
):
    master = decoder_weight.astype(jnp.float32)
    first_fresh, first_aggregate = fresh_memory(
        node_memory,
        neighbour_ids,
        neighbour_ticks,
        source_ids[0, 0],
        target_ids[0, 0],
        event_ticks[0, 0],
        gru_input,
        gru_state,
    )
    first_positive, first_negative, first_gradient = link_terms(
        node_memory,
        source_ids[0, 0],
        target_ids[0, 0],
        negative_ids[0, 0],
        first_aggregate,
        master.astype(jnp.bfloat16),
    )
    first_memory = node_memory.at[target_ids[0, 0]].set(first_fresh)
    second_memory = passed_along(first_memory, "epoch", 1)
    master = take_step(master, first_gradient, 0)
    second_fresh, second_aggregate = fresh_memory(
        second_memory,
        neighbour_ids,
        neighbour_ticks,
        source_ids[0, 1],
        target_ids[0, 1],
        event_ticks[0, 1],
        gru_input,
        gru_state,
    )
    final_memory = second_memory.at[target_ids[0, 1]].set(second_fresh)
    second_positive, second_negative, second_gradient = link_terms(
        second_memory,
        source_ids[0, 1],
        target_ids[0, 1],
        negative_ids[0, 1],
        second_aggregate,
        master.astype(jnp.bfloat16),
    )
    master = take_step(master, second_gradient, 1)
    logit_rows = jnp.stack([first_positive, first_negative, second_positive, second_negative])
    return (final_memory[None], master[None], logit_rows[None])


def solution(mesh):
    in_specs = (
        P(("batch", "mem"), None),
        P(None, ("batch", "mem")),
        P(None, ("batch", "mem")),
        P("epoch", None, ("batch", "mem")),
        P("epoch", None, ("batch", "mem")),
        P("epoch", None, ("batch", "mem")),
        P("epoch", None, ("batch", "mem")),
        P(),
        P(),
        P(),
    )
    out_specs = (
        P("epoch", ("batch", "mem"), None),
        P("epoch", None, None),
        P("epoch", None, ("batch", "mem")),
    )
    return jax.shard_map(
        on_device, mesh=mesh, in_specs=in_specs, out_specs=out_specs, check_vma=False
    )
```

```python
import jax
import jax.numpy as jnp
from jax import lax
from jax.experimental import pallas as pl
from jax.experimental.pallas import tpu as pltpu
from jax.sharding import PartitionSpec as P

MESH = pl.DeviceIdType.MESH
bf16, f32 = jnp.bfloat16, jnp.float32
tick_scale = 100.0
step_length = 4.0
epsilon = 1e-06
near_count, far_count = 16, 8


def matmul(a, b):
    return jnp.dot(a, b, preferred_element_type=f32)


def matmul_nt(a, b):
    return lax.dot_general(a, b, (((1,), (1,)), ((), ())), preferred_element_type=f32)


def device_at(y, z, core):
    return {"batch": y * 8 + z % 8, "mem": (z // 8) * 2 + core}


class Place:
    def __init__(self):
        self.epoch = lax.axis_index("epoch")
        batch, mem = lax.axis_index("batch"), lax.axis_index("mem")
        self.y, self.core = batch // 8, mem % 2
        z = (mem // 2) * 8 + batch % 8
        self.pair, self.side = z // 2, z % 2
        self.piece = (self.y * 2 + self.core) * 2 + self.side

    def near(self, step):
        y, core = (self.y + step // 4) % 4, (self.core + (step // 2) % 2) % 2
        side = (self.side + step % 2) % 2
        return device_at(y, self.pair * 2 + side, core), (y * 2 + core) * 2 + side

    def far(self, step):
        return device_at(self.y, ((self.pair + step) % far_count) * 2 + self.side, self.core)

    def next_epoch(self):
        return {"epoch": (self.epoch + 1) % 4}

    def last_epoch(self):
        return {"epoch": (self.epoch + 3) % 4}


near_steps = sorted(range(1, near_count), key=lambda k: -(min(k // 4, 4 - k // 4) + k % 2))
far_steps = (4, 3, 5, 2, 6, 1, 7)


class TrainerSum:
    def __init__(self, place, gradient, rounded, near_in, far_in, total, sems):
        self.place, self.gradient, self.rounded = place, gradient, rounded
        self.near_in, self.far_in, self.total, self.sems = near_in, far_in, total, sems
        self.own = pl.ds(pl.multiple_of(place.piece * 16, 16), 16)
        self.copies = []

    def send(self, src, dst, stage, step, device):
        copy = pltpu.make_async_remote_copy(
            src_ref=src,
            dst_ref=dst,
            send_sem=self.sems.at[2 * stage, step],
            recv_sem=self.sems.at[2 * stage + 1, step],
            device_id=device,
            device_id_type=MESH,
        )
        copy.start()
        self.copies.append(copy)
        return copy

    def scatter(self):
        self.pending = []
        for step in near_steps:
            device, piece = self.place.near(step)
            rows = pl.ds(pl.multiple_of(piece * 16, 16), 16)
            copy = self.send(self.rounded.at[rows], self.near_in.at[step], 0, step, device)
            self.pending.append((step, copy))

    def exchange(self):
        value = self.gradient[self.own, :]
        for step, copy in reversed(self.pending):
            copy.wait_recv()
            value = value + self.near_in[step].astype(f32)
        slot = self.far_in.at[self.place.pair]
        slot[...] = value.astype(bf16)
        self.pending = [
            self.send(slot, slot, 1, step, self.place.far(step)) for step in far_steps
        ]

    def gather(self):
        for copy in self.pending:
            copy.wait_recv()
        value = self.far_in[0].astype(f32)
        for slot in range(1, far_count):
            value = value + self.far_in[slot].astype(f32)
        self.total[self.own, :] = value.astype(bf16)
        rows = self.total.at[self.own]
        self.pending = [
            self.send(rows, rows, 2, step, self.place.near(step)[0]) for step in near_steps
        ]

    def arrive(self):
        for copy in self.pending:
            copy.wait_recv()

    def close(self):
        for copy in self.copies:
            copy.wait_send()


def column_picks(column, count):
    lanes = lax.broadcasted_iota(jnp.int32, (column.shape[0], count), 1).astype(f32)
    return jnp.where(column == lanes, 1.0, 0.0).astype(bf16)


def row_picks(row, count):
    names = lax.broadcasted_iota(jnp.int32, (count, row.shape[1]), 0).astype(f32)
    return jnp.where(row == names, 1.0, 0.0)


def neighbour_weights(target_picks, ticks, near_ids, near_times):
    def looked_up(table):
        low = (table & 255).astype(f32).astype(bf16)
        high = (table >> 8).astype(f32).astype(bf16)
        return matmul_nt(target_picks, low) + 256.0 * matmul_nt(target_picks, high)

    ids, times = looked_up(near_ids), looked_up(near_times)
    decay = tick_scale / (tick_scale + (ticks - times))
    decay = decay / jnp.sum(decay, axis=1, keepdims=True)
    events, nodes = target_picks.shape
    lanes = lax.broadcasted_iota(jnp.int32, (events, nodes), 1).astype(f32)
    weights = jnp.zeros((events, nodes), f32)
    for slot in range(near_ids.shape[0]):
        chosen = ids[:, slot : slot + 1] == lanes
        weights = weights + jnp.where(chosen, decay[:, slot : slot + 1], 0.0)
    return weights


def gather_events(memory, columns, near_ids, near_times, stacked, target_rows):
    source, target, negative, ticks = columns
    events, nodes = source.shape[0], memory.shape[0]
    target_picks = column_picks(target, nodes)
    stacked[0:events, :] = matmul(column_picks(source, nodes), memory[...]).astype(bf16)
    stacked[2 * events :, :] = matmul(column_picks(negative, nodes), memory[...]).astype(bf16)
    rows = matmul(target_picks, memory[...])
    target_rows[...] = rows.astype(bf16)
    weights = neighbour_weights(target_picks, ticks, near_ids, near_times)
    high = weights.astype(bf16)
    low = (weights - high.astype(f32)).astype(bf16)
    aggregate = matmul(high, memory[...]) + matmul(low, memory[...])
    stacked[events : 2 * events, :] = (0.5 * (rows + aggregate)).astype(bf16)


def link_gradient(stacked, projection, logits, row, deltas, gradient, rounded):
    events = stacked.shape[0] // 3
    scale = 1.0 / projection.shape[0] ** 0.5
    projected = matmul_nt(projection, stacked[...])
    source = projected[:, :events]
    target = projected[:, events : 2 * events]
    negative = projected[:, 2 * events :]
    positive = jnp.sum(source * target, axis=0, keepdims=True) * scale
    negative_logit = jnp.sum(source * negative, axis=0, keepdims=True) * scale
    logits[0, row : row + 1, :] = positive
    logits[0, row + 1 : row + 2, :] = negative_logit
    grad_positive = -jax.nn.sigmoid(-positive) * scale
    grad_negative = jax.nn.sigmoid(negative_logit) * scale
    deltas[:, :events] = (grad_positive * target + grad_negative * negative).astype(bf16)
    deltas[:, events : 2 * events] = (grad_positive * source).astype(bf16)
    deltas[:, 2 * events :] = (grad_negative * source).astype(bf16)
    value = matmul(deltas[...], stacked[...])
    gradient[...] = value
    rounded[...] = value.astype(bf16)


def fresh_rows(source_rows, target_rows, gru_input, gru_state):
    width = source_rows.shape[1]

    def gate(weights, rows, part):
        return matmul(rows, weights[:, part * width : (part + 1) * width])

    reset = jax.nn.sigmoid(gate(gru_input, source_rows, 0) + gate(gru_state, target_rows, 0))
    candidate = jnp.tanh(
        gate(gru_input, source_rows, 2) + reset * gate(gru_state, target_rows, 2)
    )
    update = jax.nn.sigmoid(gate(gru_input, source_rows, 1) + gate(gru_state, target_rows, 1))
    return ((1.0 - update) * candidate + update * target_rows.astype(f32)).astype(bf16)


def replaced(memory, target_row, fresh):
    picks = row_picks(target_row, memory.shape[0])
    hit = jnp.sum(picks, axis=1, keepdims=True)
    placed = matmul(picks.astype(bf16), fresh)
    return jnp.where(hit > 0.5, placed, memory[...].astype(f32)).astype(bf16)


def stepped(master, total):
    total = total[...].astype(f32)
    return master - step_length * total / jnp.sqrt(jnp.sum(total * total) + epsilon)


def window_kernel(
    memory_hbm,
    near_ids_hbm,
    near_times_hbm,
    source_ids_hbm,
    target_ids_hbm,
    negative_ids_hbm,
    event_ticks_hbm,
    gru_input_hbm,
    gru_state_hbm,
    decoder_hbm,
    memory_out,
    decoder_out,
    logits_out,
    memory,
    near_ids,
    near_times,
    source_ids,
    target_ids,
    negative_ids,
    event_ticks,
    gru_input,
    gru_state,
    decoder,
    handed_source,
    handed_target,
    handed_memory,
    stacked,
    target_rows,
    deltas,
    master,
    gradient,
    rounded,
    near_in,
    far_in,
    total,
    load_sems,
    hand_sems,
    sum_sems,
):
    loads = [
        pltpu.make_async_copy(stored, held, load_sems.at[slot])
        for slot, (stored, held) in enumerate(
            (
                (source_ids_hbm, source_ids),
                (target_ids_hbm, target_ids),
                (negative_ids_hbm, negative_ids),
                (event_ticks_hbm, event_ticks),
                (near_ids_hbm, near_ids),
                (near_times_hbm, near_times),
                (decoder_hbm, decoder),
                (memory_hbm, memory),
                (gru_input_hbm, gru_input),
                (gru_state_hbm, gru_state),
            )
        )
    ]
    for load in loads:
        load.start()
    place = Place()
    barrier = pltpu.get_barrier_semaphore()
    greeted = [place.near(step)[0] for step in near_steps]
    greeted += [place.far(step) for step in far_steps]
    greeted += [place.next_epoch(), place.last_epoch()]
    for device in greeted:
        pl.semaphore_signal(barrier, 1, device_id=device, device_id_type=MESH)

    for load in loads[:8]:
        load.wait()
    ids = jnp.concatenate(
        [source_ids[0], target_ids[0], negative_ids[0], event_ticks[0]], axis=0
    ).astype(f32)
    columns = ids.T
    first_columns = [columns[:, 2 * kind : 2 * kind + 1] for kind in range(4)]
    second_columns = [columns[:, 2 * kind + 1 : 2 * kind + 2] for kind in range(4)]
    master[...] = decoder[...].astype(f32).T
    near_id_table, near_time_table = near_ids[...], near_times[...]

    gather_events(memory, first_columns, near_id_table, near_time_table, stacked, target_rows)
    link_gradient(
        stacked, master[...].astype(bf16), logits_out, 0, deltas, gradient, rounded.at[0]
    )
    pl.semaphore_wait(barrier, len(greeted))

    hands = []
    for slot, (kept, handed) in enumerate(
        ((source_ids, handed_source), (target_ids, handed_target))
    ):
        copy = pltpu.make_async_remote_copy(
            src_ref=kept.at[0],
            dst_ref=handed,
            send_sem=hand_sems.at[0, slot],
            recv_sem=hand_sems.at[1, slot],
            device_id=place.next_epoch(),
            device_id_type=MESH,
        )
        copy.start()
        hands.append(copy)
    sums = [
        TrainerSum(
            place,
            gradient,
            rounded.at[batch],
            near_in.at[batch],
            far_in.at[batch],
            total.at[batch],
            sum_sems.at[batch],
        )
        for batch in range(2)
    ]
    sums[0].scatter()
    for hand in hands:
        hand.wait_recv()
    for load in loads[8:]:
        load.wait()
    handed_rows = jnp.concatenate(
        [handed_source[...], handed_target[...], handed_source[...], handed_target[...]], axis=0
    ).astype(f32)
    handed_columns = handed_rows.T
    nodes = memory.shape[0]
    source = matmul(column_picks(handed_columns[:, 0:1], nodes), memory[...]).astype(bf16)
    target = matmul(column_picks(handed_columns[:, 2:3], nodes), memory[...]).astype(bf16)
    fresh = fresh_rows(source, target, gru_input, gru_state)
    sums[0].exchange()

    handed_memory[...] = replaced(memory, handed_rows[2:3, :], fresh)
    gather_events(
        handed_memory, second_columns, near_id_table, near_time_table, stacked, target_rows
    )
    sums[0].gather()
    sums[0].arrive()

    master[...] = stepped(master[...], total.at[0])
    link_gradient(
        stacked, master[...].astype(bf16), logits_out, 2, deltas, gradient, rounded.at[1]
    )
    sums[1].scatter()
    events = target_rows.shape[0]
    fresh = fresh_rows(stacked[0:events, :], target_rows[...], gru_input, gru_state)
    sums[1].exchange()
    memory_out[0] = replaced(handed_memory, ids[3:4, :], fresh)
    sums[1].gather()
    sums[1].arrive()
    decoder_out[0] = stepped(master[...], total.at[1]).T
    for hand in hands:
        hand.wait_send()
    for each in sums:
        each.close()


def on_device(
    node_memory,
    neighbour_ids,
    neighbour_ticks,
    source_ids,
    target_ids,
    negative_ids,
    event_ticks,
    gru_input,
    gru_state,
    decoder_weight,
):
    nodes, width = node_memory.shape
    hidden = decoder_weight.shape[1]
    batches, events = source_ids.shape[1:]
    vmem, dma = pltpu.VMEM, pltpu.SemaphoreType.DMA
    held = pl.BlockSpec(memory_space=vmem)
    return pl.pallas_call(
        window_kernel,
        out_shape=(
            jax.ShapeDtypeStruct((1, nodes, width), bf16),
            jax.ShapeDtypeStruct((1, width, hidden), f32),
            jax.ShapeDtypeStruct((1, 2 * batches, events), f32),
        ),
        in_specs=[pl.BlockSpec(memory_space=pltpu.HBM)] * 10,
        out_specs=(held, held, held),
        scratch_shapes=[
            vmem(node_memory.shape, bf16),
            vmem(neighbour_ids.shape, jnp.int32),
            vmem(neighbour_ticks.shape, jnp.int32),
            vmem(source_ids.shape, jnp.int32),
            vmem(target_ids.shape, jnp.int32),
            vmem(negative_ids.shape, jnp.int32),
            vmem(event_ticks.shape, jnp.int32),
            vmem(gru_input.shape, bf16),
            vmem(gru_state.shape, bf16),
            vmem(decoder_weight.shape, bf16),
            vmem((batches, events), jnp.int32),
            vmem((batches, events), jnp.int32),
            vmem((nodes, width), bf16),
            vmem((3 * events, width), bf16),
            vmem((events, width), bf16),
            vmem((hidden, 3 * events), bf16),
            vmem((hidden, width), f32),
            vmem((hidden, width), f32),
            vmem((batches, hidden, width), bf16),
            vmem((batches, near_count, hidden // near_count, width), bf16),
            vmem((batches, far_count, hidden // near_count, width), bf16),
            vmem((batches, hidden, width), bf16),
            dma((10,)),
            dma((2, 2)),
            dma((batches, 6, near_count)),
        ],
        compiler_params=pltpu.CompilerParams(
            collective_id=0, has_side_effects=True, vmem_limit_bytes=60 * 2**20
        ),
        name="window",
    )(
        node_memory,
        neighbour_ids,
        neighbour_ticks,
        source_ids,
        target_ids,
        negative_ids,
        event_ticks,
        gru_input,
        gru_state,
        decoder_weight,
    )


def solution(mesh):
    in_specs = (
        P(("batch", "mem"), None),
        P(None, ("batch", "mem")),
        P(None, ("batch", "mem")),
        P("epoch", None, ("batch", "mem")),
        P("epoch", None, ("batch", "mem")),
        P("epoch", None, ("batch", "mem")),
        P("epoch", None, ("batch", "mem")),
        P(),
        P(),
        P(),
    )
    out_specs = (
        P("epoch", ("batch", "mem"), None),
        P("epoch", None, None),
        P("epoch", None, ("batch", "mem")),
    )
    return jax.shard_map(
        on_device, mesh=mesh, in_specs=in_specs, out_specs=out_specs, check_vma=False
    )
```

```python
import jax
import jax.numpy as jnp
from jax import lax
from jax.experimental import pallas as pl
from jax.experimental.pallas import tpu as pltpu
from jax.sharding import PartitionSpec as P

MESH = pl.DeviceIdType.MESH
bf16, f32 = jnp.bfloat16, jnp.float32
tick_scale = 100.0
step_length = 4.0
epsilon = 1e-06
near_count, far_count = 16, 8


def matmul(a, b):
    return jnp.dot(a, b, preferred_element_type=f32)


def matmul_nt(a, b):
    return lax.dot_general(a, b, (((1,), (1,)), ((), ())), preferred_element_type=f32)


def device_at(y, z, core):
    return {"batch": y * 8 + z % 8, "mem": (z // 8) * 2 + core}


class Place:
    def __init__(self):
        self.epoch = lax.axis_index("epoch")
        batch, mem = lax.axis_index("batch"), lax.axis_index("mem")
        self.y, self.core = batch // 8, mem % 2
        z = (mem // 2) * 8 + batch % 8
        self.pair, self.side = z // 2, z % 2
        self.piece = (self.y * 2 + self.core) * 2 + self.side

    def near(self, step):
        y, core = (self.y + step // 4) % 4, (self.core + (step // 2) % 2) % 2
        side = (self.side + step % 2) % 2
        return device_at(y, self.pair * 2 + side, core), (y * 2 + core) * 2 + side

    def far(self, step):
        return device_at(self.y, ((self.pair + step) % far_count) * 2 + self.side, self.core)

    def next_epoch(self):
        return {"epoch": (self.epoch + 1) % 4}

    def last_epoch(self):
        return {"epoch": (self.epoch + 3) % 4}


near_steps = sorted(range(1, near_count), key=lambda k: -(min(k // 4, 4 - k // 4) + k % 2))
far_steps = (4, 3, 5, 2, 6, 1, 7)


class TrainerSum:
    def __init__(self, place, gradient, rounded, near_in, far_in, total, sems):
        self.place, self.gradient, self.rounded = place, gradient, rounded
        self.near_in, self.far_in, self.total, self.sems = near_in, far_in, total, sems
        self.own = pl.ds(pl.multiple_of(place.piece * 16, 16), 16)
        self.copies = []

    def send(self, src, dst, stage, step, device):
        copy = pltpu.make_async_remote_copy(
            src_ref=src,
            dst_ref=dst,
            send_sem=self.sems.at[2 * stage, step],
            recv_sem=self.sems.at[2 * stage + 1, step],
            device_id=device,
            device_id_type=MESH,
        )
        copy.start()
        self.copies.append(copy)
        return copy

    def scatter(self):
        self.pending = []
        for step in near_steps:
            device, piece = self.place.near(step)
            rows = pl.ds(pl.multiple_of(piece * 16, 16), 16)
            copy = self.send(self.rounded.at[rows], self.near_in.at[step], 0, step, device)
            self.pending.append((step, copy))

    def exchange(self):
        value = self.gradient[self.own, :]
        for step, copy in reversed(self.pending):
            copy.wait_recv()
            value = value + self.near_in[step].astype(f32)
        slot = self.far_in.at[self.place.pair]
        slot[...] = value.astype(bf16)
        self.pending = [
            self.send(slot, slot, 1, step, self.place.far(step)) for step in far_steps
        ]

    def gather(self):
        for copy in self.pending:
            copy.wait_recv()
        value = self.far_in[0].astype(f32)
        for slot in range(1, far_count):
            value = value + self.far_in[slot].astype(f32)
        self.total[self.own, :] = value.astype(bf16)
        rows = self.total.at[self.own]
        self.pending = [
            self.send(rows, rows, 2, step, self.place.near(step)[0]) for step in near_steps
        ]

    def arrive(self):
        for copy in self.pending:
            copy.wait_recv()

    def close(self):
        for copy in self.copies:
            copy.wait_send()


def column_picks(column, count):
    lanes = lax.broadcasted_iota(jnp.int32, (column.shape[0], count), 1).astype(f32)
    return jnp.where(column == lanes, 1.0, 0.0).astype(bf16)


def row_picks(row, count):
    names = lax.broadcasted_iota(jnp.int32, (count, row.shape[1]), 0).astype(f32)
    return jnp.where(row == names, 1.0, 0.0)


def neighbour_weights(target_picks, ticks, near_ids, near_times):
    def looked_up(table):
        low = (table & 255).astype(f32).astype(bf16)
        high = (table >> 8).astype(f32).astype(bf16)
        return matmul_nt(target_picks, low) + 256.0 * matmul_nt(target_picks, high)

    ids, times = looked_up(near_ids), looked_up(near_times)
    decay = tick_scale / (tick_scale + (ticks - times))
    decay = decay / jnp.sum(decay, axis=1, keepdims=True)
    events, nodes = target_picks.shape
    lanes = lax.broadcasted_iota(jnp.int32, (events, nodes), 1).astype(f32)
    weights = jnp.zeros((events, nodes), f32)
    for slot in range(near_ids.shape[0]):
        chosen = ids[:, slot : slot + 1] == lanes
        weights = weights + jnp.where(chosen, decay[:, slot : slot + 1], 0.0)
    return weights


def gather_events(memory, columns, near_ids, near_times, stacked, target_rows):
    source, target, negative, ticks = columns
    events, nodes = source.shape[0], memory.shape[0]
    target_picks = column_picks(target, nodes)
    stacked[0:events, :] = matmul(column_picks(source, nodes), memory[...]).astype(bf16)
    stacked[2 * events :, :] = matmul(column_picks(negative, nodes), memory[...]).astype(bf16)
    rows = matmul(target_picks, memory[...])
    target_rows[...] = rows.astype(bf16)
    weights = neighbour_weights(target_picks, ticks, near_ids, near_times)
    high = weights.astype(bf16)
    low = (weights - high.astype(f32)).astype(bf16)
    aggregate = matmul(high, memory[...]) + matmul(low, memory[...])
    stacked[events : 2 * events, :] = (0.5 * (rows + aggregate)).astype(bf16)


def link_gradient(stacked, projection, logits, row, deltas, gradient, rounded):
    events = stacked.shape[0] // 3
    scale = 1.0 / projection.shape[0] ** 0.5
    projected = matmul_nt(projection, stacked[...])
    source = projected[:, :events]
    target = projected[:, events : 2 * events]
    negative = projected[:, 2 * events :]
    positive = jnp.sum(source * target, axis=0, keepdims=True) * scale
    negative_logit = jnp.sum(source * negative, axis=0, keepdims=True) * scale
    logits[row : row + 1, :] = positive
    logits[row + 1 : row + 2, :] = negative_logit
    grad_positive = -jax.nn.sigmoid(-positive) * scale
    grad_negative = jax.nn.sigmoid(negative_logit) * scale
    deltas[:, :events] = (grad_positive * target + grad_negative * negative).astype(bf16)
    deltas[:, events : 2 * events] = (grad_positive * source).astype(bf16)
    deltas[:, 2 * events :] = (grad_negative * source).astype(bf16)
    value = matmul(deltas[...], stacked[...])
    gradient[...] = value
    rounded[...] = value.astype(bf16)


def fresh_rows(source_rows, target_rows, gru_input, gru_state):
    width = source_rows.shape[1]

    def gate(weights, rows, part):
        return matmul(rows, weights[:, part * width : (part + 1) * width])

    reset = jax.nn.sigmoid(gate(gru_input, source_rows, 0) + gate(gru_state, target_rows, 0))
    candidate = jnp.tanh(
        gate(gru_input, source_rows, 2) + reset * gate(gru_state, target_rows, 2)
    )
    update = jax.nn.sigmoid(gate(gru_input, source_rows, 1) + gate(gru_state, target_rows, 1))
    return ((1.0 - update) * candidate + update * target_rows.astype(f32)).astype(bf16)


def replaced(memory, target_row, fresh):
    picks = row_picks(target_row, memory.shape[0])
    hit = jnp.sum(picks, axis=1, keepdims=True)
    placed = matmul(picks.astype(bf16), fresh)
    return jnp.where(hit > 0.5, placed, memory[...].astype(f32)).astype(bf16)


def stepped(master, total):
    total = total[...].astype(f32)
    return master - step_length * total / jnp.sqrt(jnp.sum(total * total) + epsilon)


def window_kernel(
    memory_hbm,
    near_ids_hbm,
    near_times_hbm,
    source_ids_hbm,
    target_ids_hbm,
    negative_ids_hbm,
    event_ticks_hbm,
    gru_input_hbm,
    gru_state_hbm,
    decoder_hbm,
    memory_out,
    master,
    last_total,
    logits_out,
    memory,
    near_ids,
    near_times,
    source_ids,
    target_ids,
    negative_ids,
    event_ticks,
    gru_input,
    gru_state,
    decoder,
    handed_source,
    handed_target,
    handed_memory,
    stacked,
    target_rows,
    deltas,
    gradient,
    rounded,
    near_in,
    far_in,
    total,
    load_sems,
    hand_sems,
    sum_sems,
):
    loads = [
        pltpu.make_async_copy(stored, held, load_sems.at[slot])
        for slot, (stored, held) in enumerate(
            (
                (source_ids_hbm, source_ids),
                (target_ids_hbm, target_ids),
                (negative_ids_hbm, negative_ids),
                (event_ticks_hbm, event_ticks),
                (near_ids_hbm, near_ids),
                (near_times_hbm, near_times),
                (decoder_hbm, decoder),
                (memory_hbm, memory),
                (gru_input_hbm, gru_input),
                (gru_state_hbm, gru_state),
            )
        )
    ]
    for load in loads:
        load.start()
    place = Place()
    barrier = pltpu.get_barrier_semaphore()
    greeted = [place.near(step)[0] for step in near_steps]
    greeted += [place.far(step) for step in far_steps]
    greeted += [place.next_epoch(), place.last_epoch()]
    for device in greeted:
        pl.semaphore_signal(barrier, 1, device_id=device, device_id_type=MESH)

    for load in loads[:8]:
        load.wait()
    ids = jnp.concatenate(
        [source_ids[0], target_ids[0], negative_ids[0], event_ticks[0]], axis=0
    ).astype(f32)
    columns = ids.T
    first_columns = [columns[:, 2 * kind : 2 * kind + 1] for kind in range(4)]
    second_columns = [columns[:, 2 * kind + 1 : 2 * kind + 2] for kind in range(4)]
    master[...] = decoder[...].astype(f32).T
    near_id_table, near_time_table = near_ids[...], near_times[...]

    gather_events(memory, first_columns, near_id_table, near_time_table, stacked, target_rows)
    link_gradient(
        stacked, master[...].astype(bf16), logits_out, 0, deltas, gradient, rounded.at[0]
    )
    pl.semaphore_wait(barrier, len(greeted))

    hands = []
    for slot, (kept, handed) in enumerate(
        ((source_ids, handed_source), (target_ids, handed_target))
    ):
        copy = pltpu.make_async_remote_copy(
            src_ref=kept.at[0],
            dst_ref=handed,
            send_sem=hand_sems.at[0, slot],
            recv_sem=hand_sems.at[1, slot],
            device_id=place.next_epoch(),
            device_id_type=MESH,
        )
        copy.start()
        hands.append(copy)
    sums = [
        TrainerSum(
            place,
            gradient,
            rounded.at[batch],
            near_in.at[batch],
            far_in.at[batch],
            (total, last_total)[batch],
            sum_sems.at[batch],
        )
        for batch in range(2)
    ]
    sums[0].scatter()
    for hand in hands:
        hand.wait_recv()
    for load in loads[8:]:
        load.wait()
    handed_rows = jnp.concatenate(
        [handed_source[...], handed_target[...], handed_source[...], handed_target[...]], axis=0
    ).astype(f32)
    handed_columns = handed_rows.T
    nodes = memory.shape[0]
    source = matmul(column_picks(handed_columns[:, 0:1], nodes), memory[...]).astype(bf16)
    target = matmul(column_picks(handed_columns[:, 2:3], nodes), memory[...]).astype(bf16)
    fresh = fresh_rows(source, target, gru_input, gru_state)
    sums[0].exchange()

    handed_memory[...] = replaced(memory, handed_rows[2:3, :], fresh)
    gather_events(
        handed_memory, second_columns, near_id_table, near_time_table, stacked, target_rows
    )
    sums[0].gather()
    sums[0].arrive()

    master[...] = stepped(master[...], total)
    link_gradient(
        stacked, master[...].astype(bf16), logits_out, 2, deltas, gradient, rounded.at[1]
    )
    sums[1].scatter()
    events = target_rows.shape[0]
    fresh = fresh_rows(stacked[0:events, :], target_rows[...], gru_input, gru_state)
    sums[1].exchange()
    memory_out[...] = replaced(handed_memory, ids[3:4, :], fresh)
    sums[1].gather()
    sums[1].arrive()
    for hand in hands:
        hand.wait_send()
    for each in sums:
        each.close()


def results_kernel(memory, master, total, logits, memory_out, decoder_out, logits_out, decoder, sems):
    stores = [
        pltpu.make_async_copy(memory, memory_out.at[0], sems.at[0]),
        pltpu.make_async_copy(logits, logits_out.at[0], sems.at[1]),
        pltpu.make_async_copy(decoder, decoder_out.at[0], sems.at[2]),
    ]
    stores[0].start()
    stores[1].start()
    decoder[...] = stepped(master[...], total).T
    stores[2].start()
    for store in stores:
        store.wait()


def on_device(*given):
    node_memory, neighbour_ids, neighbour_ticks, source_ids, target_ids, negative_ids = given[:6]
    event_ticks, gru_input, gru_state, decoder_weight = given[6:]
    nodes, width = node_memory.shape
    hidden = decoder_weight.shape[1]
    batches, events = source_ids.shape[1:]
    vmem, dma = pltpu.VMEM, pltpu.SemaphoreType.DMA
    held = pl.BlockSpec(memory_space=vmem)
    kept = pl.pallas_call(
        window_kernel,
        out_shape=(
            vmem((nodes, width), bf16),
            vmem((hidden, width), f32),
            vmem((hidden, width), bf16),
            vmem((2 * batches, events), f32),
        ),
        in_specs=[pl.BlockSpec(memory_space=pltpu.HBM)] * 10,
        out_specs=(held,) * 4,
        scratch_shapes=[
            vmem(node_memory.shape, bf16),
            vmem(neighbour_ids.shape, jnp.int32),
            vmem(neighbour_ticks.shape, jnp.int32),
            vmem(source_ids.shape, jnp.int32),
            vmem(target_ids.shape, jnp.int32),
            vmem(negative_ids.shape, jnp.int32),
            vmem(event_ticks.shape, jnp.int32),
            vmem(gru_input.shape, bf16),
            vmem(gru_state.shape, bf16),
            vmem(decoder_weight.shape, bf16),
            vmem((batches, events), jnp.int32),
            vmem((batches, events), jnp.int32),
            vmem((nodes, width), bf16),
            vmem((3 * events, width), bf16),
            vmem((events, width), bf16),
            vmem((hidden, 3 * events), bf16),
            vmem((hidden, width), f32),
            vmem((batches, hidden, width), bf16),
            vmem((batches, near_count, hidden // near_count, width), bf16),
            vmem((batches, far_count, hidden // near_count, width), bf16),
            vmem((hidden, width), bf16),
            dma((10,)),
            dma((2, 2)),
            dma((batches, 6, near_count)),
        ],
        compiler_params=pltpu.CompilerParams(
            collective_id=0, has_side_effects=True, vmem_limit_bytes=50 * 2**20
        ),
        name="window",
    )(*(pltpu.with_memory_space_constraint(each, pltpu.HBM) for each in given))
    stored = pl.BlockSpec(memory_space=pltpu.HBM)
    return pl.pallas_call(
        results_kernel,
        out_shape=(
            jax.ShapeDtypeStruct((1, nodes, width), bf16),
            jax.ShapeDtypeStruct((1, width, hidden), f32),
            jax.ShapeDtypeStruct((1, 2 * batches, events), f32),
        ),
        in_specs=[held] * 4,
        out_specs=(stored,) * 3,
        scratch_shapes=[vmem((width, hidden), f32), dma((3,))],
        name="results",
    )(*kept)


def solution(mesh):
    in_specs = (
        P(("batch", "mem"), None),
        P(None, ("batch", "mem")),
        P(None, ("batch", "mem")),
        P("epoch", None, ("batch", "mem")),
        P("epoch", None, ("batch", "mem")),
        P("epoch", None, ("batch", "mem")),
        P("epoch", None, ("batch", "mem")),
        P(),
        P(),
        P(),
    )
    out_specs = (
        P("epoch", ("batch", "mem"), None),
        P("epoch", None, None),
        P("epoch", None, ("batch", "mem")),
    )
    return jax.shard_map(
        on_device, mesh=mesh, in_specs=in_specs, out_specs=out_specs, check_vma=False
    )
```

```python
import jax
import jax.numpy as jnp
from jax import lax
from jax.experimental import pallas as pl
from jax.experimental.pallas import tpu as pltpu
from jax.sharding import PartitionSpec as P

MESH = pl.DeviceIdType.MESH
bf16, f32 = jnp.bfloat16, jnp.float32
tick_scale = 100.0
step_length = 4.0
epsilon = 1e-06
near_count, far_count = 16, 8


def matmul(a, b):
    return jnp.dot(a, b, preferred_element_type=f32)


def matmul_nt(a, b):
    return lax.dot_general(a, b, (((1,), (1,)), ((), ())), preferred_element_type=f32)


def device_at(y, z, core):
    return {"batch": y * 8 + z % 8, "mem": (z // 8) * 2 + core}


class Place:
    def __init__(self):
        self.epoch = lax.axis_index("epoch")
        batch, mem = lax.axis_index("batch"), lax.axis_index("mem")
        self.y, self.core = batch // 8, mem % 2
        z = (mem // 2) * 8 + batch % 8
        self.pair, self.side = z // 2, z % 2
        self.piece = (self.y * 2 + self.core) * 2 + self.side

    def near(self, step):
        y, core = (self.y + step // 4) % 4, (self.core + (step // 2) % 2) % 2
        side = (self.side + step % 2) % 2
        return device_at(y, self.pair * 2 + side, core), (y * 2 + core) * 2 + side

    def far(self, step):
        return device_at(self.y, ((self.pair + step) % far_count) * 2 + self.side, self.core)

    def next_epoch(self):
        return {"epoch": (self.epoch + 1) % 4}

    def last_epoch(self):
        return {"epoch": (self.epoch + 3) % 4}


near_steps = sorted(range(1, near_count), key=lambda k: -(min(k // 4, 4 - k // 4) + k % 2))
far_steps = (4, 3, 5, 2, 6, 1, 7)


class TrainerSum:
    def __init__(self, place, gradient, rounded, near_in, far_in, total, sems):
        self.place, self.gradient, self.rounded = place, gradient, rounded
        self.near_in, self.far_in, self.total, self.sems = near_in, far_in, total, sems
        self.own = pl.ds(pl.multiple_of(place.piece * 16, 16), 16)
        self.copies = []

    def send(self, src, dst, stage, step, device):
        copy = pltpu.make_async_remote_copy(
            src_ref=src,
            dst_ref=dst,
            send_sem=self.sems.at[2 * stage, step],
            recv_sem=self.sems.at[2 * stage + 1, step],
            device_id=device,
            device_id_type=MESH,
        )
        copy.start()
        self.copies.append(copy)
        return copy

    def scatter(self):
        self.pending = []
        for step in near_steps:
            device, piece = self.place.near(step)
            rows = pl.ds(pl.multiple_of(piece * 16, 16), 16)
            copy = self.send(self.rounded.at[rows], self.near_in.at[step], 0, step, device)
            self.pending.append((step, copy))

    def exchange(self):
        value = self.gradient[self.own, :]
        for step, copy in reversed(self.pending):
            copy.wait_recv()
            value = value + self.near_in[step].astype(f32)
        slot = self.far_in.at[self.place.pair]
        slot[...] = value.astype(bf16)
        self.pending = [
            self.send(slot, slot, 1, step, self.place.far(step)) for step in far_steps
        ]

    def gather(self):
        for copy in self.pending:
            copy.wait_recv()
        value = self.far_in[0].astype(f32)
        for slot in range(1, far_count):
            value = value + self.far_in[slot].astype(f32)
        self.total[self.own, :] = value.astype(bf16)
        rows = self.total.at[self.own]
        self.pending = [
            self.send(rows, rows, 2, step, self.place.near(step)[0]) for step in near_steps
        ]

    def arrive(self):
        for copy in self.pending:
            copy.wait_recv()

    def close(self):
        for copy in self.copies:
            copy.wait_send()


def column_picks(column, count):
    lanes = lax.broadcasted_iota(jnp.int32, (column.shape[0], count), 1).astype(f32)
    return jnp.where(column == lanes, 1.0, 0.0).astype(bf16)


def row_picks(row, count):
    names = lax.broadcasted_iota(jnp.int32, (count, row.shape[1]), 0).astype(f32)
    return jnp.where(row == names, 1.0, 0.0)


def neighbour_weights(target_picks, ticks, near_ids, near_times):
    def looked_up(table):
        low = (table & 255).astype(f32).astype(bf16)
        high = (table >> 8).astype(f32).astype(bf16)
        return matmul_nt(target_picks, low) + 256.0 * matmul_nt(target_picks, high)

    ids, times = looked_up(near_ids), looked_up(near_times)
    decay = tick_scale / (tick_scale + (ticks - times))
    decay = decay / jnp.sum(decay, axis=1, keepdims=True)
    events, nodes = target_picks.shape
    lanes = lax.broadcasted_iota(jnp.int32, (events, nodes), 1).astype(f32)
    weights = jnp.zeros((events, nodes), f32)
    for slot in range(near_ids.shape[0]):
        chosen = ids[:, slot : slot + 1] == lanes
        weights = weights + jnp.where(chosen, decay[:, slot : slot + 1], 0.0)
    return weights


def gather_events(memory, columns, near_ids, near_times, stacked, target_rows):
    source, target, negative, ticks = columns
    events, nodes = source.shape[0], memory.shape[0]
    target_picks = column_picks(target, nodes)
    stacked[0:events, :] = matmul(column_picks(source, nodes), memory[...]).astype(bf16)
    stacked[2 * events :, :] = matmul(column_picks(negative, nodes), memory[...]).astype(bf16)
    rows = matmul(target_picks, memory[...])
    target_rows[...] = rows.astype(bf16)
    weights = neighbour_weights(target_picks, ticks, near_ids, near_times)
    high = weights.astype(bf16)
    low = (weights - high.astype(f32)).astype(bf16)
    aggregate = matmul(high, memory[...]) + matmul(low, memory[...])
    stacked[events : 2 * events, :] = (0.5 * (rows + aggregate)).astype(bf16)


def link_gradient(stacked, projection, logits, row, deltas, gradient, rounded):
    events = stacked.shape[0] // 3
    scale = 1.0 / projection.shape[0] ** 0.5
    projected = matmul_nt(projection, stacked[...])
    source = projected[:, :events]
    target = projected[:, events : 2 * events]
    negative = projected[:, 2 * events :]
    positive = jnp.sum(source * target, axis=0, keepdims=True) * scale
    negative_logit = jnp.sum(source * negative, axis=0, keepdims=True) * scale
    logits[row : row + 1, :] = positive
    logits[row + 1 : row + 2, :] = negative_logit
    grad_positive = -jax.nn.sigmoid(-positive) * scale
    grad_negative = jax.nn.sigmoid(negative_logit) * scale
    deltas[:, :events] = (grad_positive * target + grad_negative * negative).astype(bf16)
    deltas[:, events : 2 * events] = (grad_positive * source).astype(bf16)
    deltas[:, 2 * events :] = (grad_negative * source).astype(bf16)
    value = matmul(deltas[...], stacked[...])
    gradient[...] = value
    rounded[...] = value.astype(bf16)


def fresh_rows(source_rows, target_rows, gru_input, gru_state):
    width = source_rows.shape[1]

    def gate(weights, rows, part):
        return matmul(rows, weights[:, part * width : (part + 1) * width])

    reset = jax.nn.sigmoid(gate(gru_input, source_rows, 0) + gate(gru_state, target_rows, 0))
    candidate = jnp.tanh(
        gate(gru_input, source_rows, 2) + reset * gate(gru_state, target_rows, 2)
    )
    update = jax.nn.sigmoid(gate(gru_input, source_rows, 1) + gate(gru_state, target_rows, 1))
    return ((1.0 - update) * candidate + update * target_rows.astype(f32)).astype(bf16)


def replaced(memory, target_row, fresh):
    picks = row_picks(target_row, memory.shape[0])
    hit = jnp.sum(picks, axis=1, keepdims=True)
    placed = matmul(picks.astype(bf16), fresh)
    return jnp.where(hit > 0.5, placed, memory[...].astype(f32)).astype(bf16)


def stepped(master, total):
    total = total[...].astype(f32)
    return master - step_length * total / jnp.sqrt(jnp.sum(total * total) + epsilon)


def window_kernel(
    memory_hbm,
    near_ids_hbm,
    near_times_hbm,
    source_ids_hbm,
    target_ids_hbm,
    negative_ids_hbm,
    event_ticks_hbm,
    gru_input_hbm,
    gru_state_hbm,
    decoder_hbm,
    memory_out,
    master,
    last_total,
    logits_out,
    memory,
    near_ids,
    near_times,
    source_ids,
    target_ids,
    negative_ids,
    event_ticks,
    gru_input,
    gru_state,
    decoder,
    handed_source,
    handed_target,
    handed_memory,
    stacked,
    target_rows,
    deltas,
    gradient,
    rounded,
    near_in,
    far_in,
    total,
    load_sems,
    hand_sems,
    sum_sems,
):
    place = Place()
    barrier = pltpu.get_barrier_semaphore()
    greeted = [place.far(step) for step in far_steps]
    greeted += [place.near(step)[0] for step in near_steps]
    greeted += [place.next_epoch(), place.last_epoch()]
    loads = [
        pltpu.make_async_copy(stored, held, load_sems.at[slot])
        for slot, (stored, held) in enumerate(
            (
                (memory_hbm, memory),
                (source_ids_hbm, source_ids),
                (target_ids_hbm, target_ids),
                (negative_ids_hbm, negative_ids),
                (event_ticks_hbm, event_ticks),
                (near_ids_hbm, near_ids),
                (near_times_hbm, near_times),
                (decoder_hbm, decoder),
                (gru_input_hbm, gru_input),
                (gru_state_hbm, gru_state),
            )
        )
    ]
    for load in loads[:8]:
        load.start()
    for device in greeted:
        pl.semaphore_signal(barrier, 1, device_id=device, device_id_type=MESH)
    for load in loads[:8]:
        load.wait()
    for load in loads[8:]:
        load.start()

    ids = jnp.concatenate(
        [source_ids[0], target_ids[0], negative_ids[0], event_ticks[0]], axis=0
    ).astype(f32)
    columns = ids.T
    first_columns = [columns[:, 2 * kind : 2 * kind + 1] for kind in range(4)]
    second_columns = [columns[:, 2 * kind + 1 : 2 * kind + 2] for kind in range(4)]
    master[...] = decoder[...].astype(f32).T
    near_id_table, near_time_table = near_ids[...], near_times[...]

    gather_events(memory, first_columns, near_id_table, near_time_table, stacked, target_rows)
    link_gradient(
        stacked, master[...].astype(bf16), logits_out, 0, deltas, gradient, rounded.at[0]
    )
    pl.semaphore_wait(barrier, len(greeted))

    hands = []
    for slot, (kept, handed) in enumerate(
        ((source_ids, handed_source), (target_ids, handed_target))
    ):
        copy = pltpu.make_async_remote_copy(
            src_ref=kept.at[0],
            dst_ref=handed,
            send_sem=hand_sems.at[0, slot],
            recv_sem=hand_sems.at[1, slot],
            device_id=place.next_epoch(),
            device_id_type=MESH,
        )
        copy.start()
        hands.append(copy)
    sums = [
        TrainerSum(
            place,
            gradient,
            rounded.at[batch],
            near_in.at[batch],
            far_in.at[batch],
            (total, last_total)[batch],
            sum_sems.at[batch],
        )
        for batch in range(2)
    ]
    sums[0].scatter()
    for hand in hands:
        hand.wait_recv()
    for load in loads[8:]:
        load.wait()
    handed_rows = jnp.concatenate(
        [handed_source[...], handed_target[...], handed_source[...], handed_target[...]], axis=0
    ).astype(f32)
    handed_columns = handed_rows.T
    nodes = memory.shape[0]
    source = matmul(column_picks(handed_columns[:, 0:1], nodes), memory[...]).astype(bf16)
    target = matmul(column_picks(handed_columns[:, 2:3], nodes), memory[...]).astype(bf16)
    fresh = fresh_rows(source, target, gru_input, gru_state)
    sums[0].exchange()

    handed_memory[...] = replaced(memory, handed_rows[2:3, :], fresh)
    gather_events(
        handed_memory, second_columns, near_id_table, near_time_table, stacked, target_rows
    )
    sums[0].gather()
    sums[0].arrive()

    master[...] = stepped(master[...], total)
    link_gradient(
        stacked, master[...].astype(bf16), logits_out, 2, deltas, gradient, rounded.at[1]
    )
    sums[1].scatter()
    events = target_rows.shape[0]
    fresh = fresh_rows(stacked[0:events, :], target_rows[...], gru_input, gru_state)
    sums[1].exchange()
    memory_out[...] = replaced(handed_memory, ids[3:4, :], fresh)
    sums[1].gather()
    sums[1].arrive()
    for hand in hands:
        hand.wait_send()
    for each in sums:
        each.close()


def results_kernel(memory, master, total, logits, memory_out, decoder_out, logits_out, decoder, sems):
    stores = [
        pltpu.make_async_copy(memory, memory_out.at[0], sems.at[0]),
        pltpu.make_async_copy(logits, logits_out.at[0], sems.at[1]),
        pltpu.make_async_copy(decoder, decoder_out.at[0], sems.at[2]),
    ]
    stores[0].start()
    stores[1].start()
    decoder[...] = stepped(master[...], total).T
    stores[2].start()
    for store in stores:
        store.wait()


def on_device(*given):
    node_memory, neighbour_ids, neighbour_ticks, source_ids, target_ids, negative_ids = given[:6]
    event_ticks, gru_input, gru_state, decoder_weight = given[6:]
    nodes, width = node_memory.shape
    hidden = decoder_weight.shape[1]
    batches, events = source_ids.shape[1:]
    vmem, dma = pltpu.VMEM, pltpu.SemaphoreType.DMA
    held = pl.BlockSpec(memory_space=vmem)
    kept = pl.pallas_call(
        window_kernel,
        out_shape=(
            vmem((nodes, width), bf16),
            vmem((hidden, width), f32),
            vmem((hidden, width), bf16),
            vmem((2 * batches, events), f32),
        ),
        in_specs=[pl.BlockSpec(memory_space=pltpu.HBM)] * 10,
        out_specs=(held,) * 4,
        scratch_shapes=[
            vmem(node_memory.shape, bf16),
            vmem(neighbour_ids.shape, jnp.int32),
            vmem(neighbour_ticks.shape, jnp.int32),
            vmem(source_ids.shape, jnp.int32),
            vmem(target_ids.shape, jnp.int32),
            vmem(negative_ids.shape, jnp.int32),
            vmem(event_ticks.shape, jnp.int32),
            vmem(gru_input.shape, bf16),
            vmem(gru_state.shape, bf16),
            vmem(decoder_weight.shape, bf16),
            vmem((batches, events), jnp.int32),
            vmem((batches, events), jnp.int32),
            vmem((nodes, width), bf16),
            vmem((3 * events, width), bf16),
            vmem((events, width), bf16),
            vmem((hidden, 3 * events), bf16),
            vmem((hidden, width), f32),
            vmem((batches, hidden, width), bf16),
            vmem((batches, near_count, hidden // near_count, width), bf16),
            vmem((batches, far_count, hidden // near_count, width), bf16),
            vmem((hidden, width), bf16),
            dma((10,)),
            dma((2, 2)),
            dma((batches, 6, near_count)),
        ],
        compiler_params=pltpu.CompilerParams(
            collective_id=0, has_side_effects=True, vmem_limit_bytes=50 * 2**20
        ),
        name="window",
    )(*(pltpu.with_memory_space_constraint(each, pltpu.HBM) for each in given))
    stored = pl.BlockSpec(memory_space=pltpu.HBM)
    return pl.pallas_call(
        results_kernel,
        out_shape=(
            jax.ShapeDtypeStruct((1, nodes, width), bf16),
            jax.ShapeDtypeStruct((1, width, hidden), f32),
            jax.ShapeDtypeStruct((1, 2 * batches, events), f32),
        ),
        in_specs=[held] * 4,
        out_specs=(stored,) * 3,
        scratch_shapes=[vmem((width, hidden), f32), dma((3,))],
        compiler_params=pltpu.CompilerParams(vmem_limit_bytes=8 * 2**20),
        name="results",
    )(*(pltpu.with_memory_space_constraint(each, pltpu.VMEM) for each in kept))


def solution(mesh):
    in_specs = (
        P(("batch", "mem"), None),
        P(None, ("batch", "mem")),
        P(None, ("batch", "mem")),
        P("epoch", None, ("batch", "mem")),
        P("epoch", None, ("batch", "mem")),
        P("epoch", None, ("batch", "mem")),
        P("epoch", None, ("batch", "mem")),
        P(),
        P(),
        P(),
    )
    out_specs = (
        P("epoch", ("batch", "mem"), None),
        P("epoch", None, None),
        P("epoch", None, ("batch", "mem")),
    )
    return jax.shard_map(
        on_device, mesh=mesh, in_specs=in_specs, out_specs=out_specs, check_vma=False
    )
```

```python
import jax
import jax.numpy as jnp
from jax import lax
from jax.experimental import pallas as pl
from jax.experimental.pallas import tpu as pltpu
from jax.sharding import PartitionSpec as P

MESH = pl.DeviceIdType.MESH
bf16, f32 = jnp.bfloat16, jnp.float32
tick_scale = 100.0
step_length = 4.0
epsilon = 1e-06
near_count, far_count = 16, 8
half = far_count // 2


def matmul(a, b):
    return jnp.dot(a, b, preferred_element_type=f32)


def matmul_nt(a, b):
    return lax.dot_general(a, b, (((1,), (1,)), ((), ())), preferred_element_type=f32)


def device_at(y, z, core):
    return {"batch": y * 8 + z % 8, "mem": (z // 8) * 2 + core}


class Place:
    def __init__(self):
        self.epoch = lax.axis_index("epoch")
        batch, mem = lax.axis_index("batch"), lax.axis_index("mem")
        self.y, self.core = batch // 8, mem % 2
        z = (mem // 2) * 8 + batch % 8
        self.pair, self.side = z // 2, z % 2
        self.piece = (self.y * 2 + self.core) * 2 + self.side

    def near(self, step):
        y, core = (self.y + step // 4) % 4, (self.core + (step // 2) % 2) % 2
        side = (self.side + step % 2) % 2
        return device_at(y, self.pair * 2 + side, core), (y * 2 + core) * 2 + side

    def far_pair(self, step):
        return (self.pair + step + far_count) % far_count

    def far(self, step):
        return device_at(self.y, self.far_pair(step) * 2 + self.side, self.core)

    def mirror(self):
        return device_at(self.y, (far_count - 1 - self.pair) * 2 + self.side, self.core)

    def next_epoch(self):
        return {"epoch": (self.epoch + 1) % 4}

    def last_epoch(self):
        return {"epoch": (self.epoch + 3) % 4}


near_steps = sorted(range(1, near_count), key=lambda k: -(min(k // 4, 4 - k // 4) + k % 2))
far_steps = (4, 3, 5, 2, 6, 1, 7)


class TrainerSum:
    def __init__(self, place, gradient, rounded, near_in, far_in, half_sum, total, sems):
        self.place, self.gradient, self.rounded = place, gradient, rounded
        self.near_in, self.far_in, self.half_sum = near_in, far_in, half_sum
        self.total, self.sems = total, sems
        self.own = pl.ds(pl.multiple_of(place.piece * 16, 16), 16)
        self.copies = []

    def copy_of(self, src, dst, stage, step, device):
        return pltpu.make_async_remote_copy(
            src_ref=src,
            dst_ref=dst,
            send_sem=self.sems.at[2 * stage, step],
            recv_sem=self.sems.at[2 * stage + 1, step],
            device_id=device,
            device_id_type=MESH,
        )

    def send(self, src, dst, stage, step, device):
        copy = self.copy_of(src, dst, stage, step, device)
        copy.start()
        self.copies.append(copy)
        return copy

    def scatter(self):
        self.pending = []
        for step in near_steps:
            device, piece = self.place.near(step)
            rows = pl.ds(pl.multiple_of(piece * 16, 16), 16)
            copy = self.send(self.rounded.at[rows], self.near_in.at[step], 0, step, device)
            self.pending.append((step, copy))

    def exchange(self):
        value = self.gradient[self.own, :]
        for step, copy in reversed(self.pending):
            copy.wait_recv()
            value = value + self.near_in[step].astype(f32)
        place = self.place
        self.far_in[place.pair] = value.astype(bf16)
        for step in far_steps:

            @pl.when((place.pair >= half) | (place.far_pair(step) < half))
            def _(step=step):
                self.far_copy(step).start()

    def far_copy(self, step):
        slot = self.far_in.at[self.place.pair]
        return self.copy_of(slot, slot, 1, step, self.place.far(step))

    def bridge_copy(self):
        return self.copy_of(self.half_sum, self.half_sum, 1, 0, self.place.mirror())

    def bridge(self, greeting):
        place = self.place

        @pl.when(place.pair < half)
        def _():
            for step in far_steps:

                @pl.when(place.far_pair(-step) < half)
                def _(step=step):
                    self.far_copy(step).wait_recv()

            value = self.far_in[0].astype(f32)
            for slot in range(1, half):
                value = value + self.far_in[slot].astype(f32)
            self.half_sum[...] = value.astype(bf16)
            if greeting is not None:
                pl.semaphore_wait(greeting, 1)
            self.bridge_copy().start()

    def gather(self):
        place = self.place
        for step in far_steps:

            @pl.when(place.far_pair(-step) >= half)
            def _(step=step):
                self.far_copy(step).wait_recv()

        @pl.when(place.pair >= half)
        def _():
            self.bridge_copy().wait_recv()

        value = self.half_sum[...].astype(f32)
        for slot in range(half, far_count):
            value = value + self.far_in[slot].astype(f32)
        self.total[self.own, :] = value.astype(bf16)
        rows = self.total.at[self.own]
        self.pending = [
            self.send(rows, rows, 2, step, self.place.near(step)[0]) for step in near_steps
        ]

    def arrive(self):
        for copy in self.pending:
            copy.wait_recv()

    def close(self):
        place = self.place
        for copy in self.copies:
            copy.wait_send()
        for step in far_steps:

            @pl.when((place.pair >= half) | (place.far_pair(step) < half))
            def _(step=step):
                self.far_copy(step).wait_send()

        @pl.when(place.pair < half)
        def _():
            self.bridge_copy().wait_send()


def column_picks(column, count):
    lanes = lax.broadcasted_iota(jnp.int32, (column.shape[0], count), 1).astype(f32)
    return jnp.where(column == lanes, 1.0, 0.0).astype(bf16)


def row_picks(row, count):
    names = lax.broadcasted_iota(jnp.int32, (count, row.shape[1]), 0).astype(f32)
    return jnp.where(row == names, 1.0, 0.0)


def neighbour_weights(target_picks, ticks, near_ids, near_times):
    def looked_up(table):
        low = (table & 255).astype(f32).astype(bf16)
        high = (table >> 8).astype(f32).astype(bf16)
        return matmul_nt(target_picks, low) + 256.0 * matmul_nt(target_picks, high)

    ids, times = looked_up(near_ids), looked_up(near_times)
    decay = tick_scale / (tick_scale + (ticks - times))
    decay = decay / jnp.sum(decay, axis=1, keepdims=True)
    events, nodes = target_picks.shape
    lanes = lax.broadcasted_iota(jnp.int32, (events, nodes), 1).astype(f32)
    weights = jnp.zeros((events, nodes), f32)
    for slot in range(near_ids.shape[0]):
        chosen = ids[:, slot : slot + 1] == lanes
        weights = weights + jnp.where(chosen, decay[:, slot : slot + 1], 0.0)
    return weights


def gather_events(memory, columns, near_ids, near_times, stacked, target_rows):
    source, target, negative, ticks = columns
    events, nodes = source.shape[0], memory.shape[0]
    target_picks = column_picks(target, nodes)
    stacked[0:events, :] = matmul(column_picks(source, nodes), memory[...]).astype(bf16)
    stacked[2 * events :, :] = matmul(column_picks(negative, nodes), memory[...]).astype(bf16)
    rows = matmul(target_picks, memory[...])
    target_rows[...] = rows.astype(bf16)
    weights = neighbour_weights(target_picks, ticks, near_ids, near_times)
    high = weights.astype(bf16)
    low = (weights - high.astype(f32)).astype(bf16)
    aggregate = matmul(high, memory[...]) + matmul(low, memory[...])
    stacked[events : 2 * events, :] = (0.5 * (rows + aggregate)).astype(bf16)


def link_gradient(stacked, projection, logits, row, deltas, gradient, rounded):
    events = stacked.shape[0] // 3
    scale = 1.0 / projection.shape[0] ** 0.5
    projected = matmul_nt(projection, stacked[...])
    source = projected[:, :events]
    target = projected[:, events : 2 * events]
    negative = projected[:, 2 * events :]
    positive = jnp.sum(source * target, axis=0, keepdims=True) * scale
    negative_logit = jnp.sum(source * negative, axis=0, keepdims=True) * scale
    logits[row : row + 1, :] = positive
    logits[row + 1 : row + 2, :] = negative_logit
    grad_positive = -jax.nn.sigmoid(-positive) * scale
    grad_negative = jax.nn.sigmoid(negative_logit) * scale
    deltas[:, :events] = (grad_positive * target + grad_negative * negative).astype(bf16)
    deltas[:, events : 2 * events] = (grad_positive * source).astype(bf16)
    deltas[:, 2 * events :] = (grad_negative * source).astype(bf16)
    value = matmul(deltas[...], stacked[...])
    gradient[...] = value
    rounded[...] = value.astype(bf16)


def fresh_rows(source_rows, target_rows, gru_input, gru_state):
    width = source_rows.shape[1]

    def gate(weights, rows, part):
        return matmul(rows, weights[:, part * width : (part + 1) * width])

    reset = jax.nn.sigmoid(gate(gru_input, source_rows, 0) + gate(gru_state, target_rows, 0))
    candidate = jnp.tanh(
        gate(gru_input, source_rows, 2) + reset * gate(gru_state, target_rows, 2)
    )
    update = jax.nn.sigmoid(gate(gru_input, source_rows, 1) + gate(gru_state, target_rows, 1))
    return ((1.0 - update) * candidate + update * target_rows.astype(f32)).astype(bf16)


def replaced(memory, target_row, fresh):
    picks = row_picks(target_row, memory.shape[0])
    hit = jnp.sum(picks, axis=1, keepdims=True)
    placed = matmul(picks.astype(bf16), fresh)
    return jnp.where(hit > 0.5, placed, memory[...].astype(f32)).astype(bf16)


def stepped(master, total):
    total = total[...].astype(f32)
    return master - step_length * total / jnp.sqrt(jnp.sum(total * total) + epsilon)


def window_kernel(
    memory_hbm,
    near_ids_hbm,
    near_times_hbm,
    source_ids_hbm,
    target_ids_hbm,
    negative_ids_hbm,
    event_ticks_hbm,
    gru_input_hbm,
    gru_state_hbm,
    decoder_hbm,
    memory_out,
    master,
    last_total,
    logits_out,
    memory,
    near_ids,
    near_times,
    source_ids,
    target_ids,
    negative_ids,
    event_ticks,
    gru_input,
    gru_state,
    decoder,
    handed_source,
    handed_target,
    handed_memory,
    stacked,
    target_rows,
    deltas,
    gradient,
    rounded,
    near_in,
    far_in,
    half_sums,
    total,
    load_sems,
    hand_sems,
    sum_sems,
    greeting,
):
    place = Place()
    barrier = pltpu.get_barrier_semaphore()
    greeted = [place.near(step)[0] for step in near_steps]
    greeted += [place.next_epoch(), place.last_epoch()]
    loads = [
        pltpu.make_async_copy(stored, held, load_sems.at[slot])
        for slot, (stored, held) in enumerate(
            (
                (memory_hbm, memory),
                (source_ids_hbm, source_ids),
                (target_ids_hbm, target_ids),
                (negative_ids_hbm, negative_ids),
                (event_ticks_hbm, event_ticks),
                (near_ids_hbm, near_ids),
                (near_times_hbm, near_times),
                (decoder_hbm, decoder),
                (gru_input_hbm, gru_input),
                (gru_state_hbm, gru_state),
            )
        )
    ]
    for load in loads[:8]:
        load.start()
    for step in far_steps:

        @pl.when((place.pair < half) | (place.far_pair(step) >= half))
        def _(step=step):
            pl.semaphore_signal(barrier, 1, device_id=place.far(step), device_id_type=MESH)

    for device in greeted:
        pl.semaphore_signal(barrier, 1, device_id=device, device_id_type=MESH)
    for load in loads[:8]:
        load.wait()
    for load in loads[8:]:
        load.start()

    ids = jnp.concatenate(
        [source_ids[0], target_ids[0], negative_ids[0], event_ticks[0]], axis=0
    ).astype(f32)
    columns = ids.T
    first_columns = [columns[:, 2 * kind : 2 * kind + 1] for kind in range(4)]
    second_columns = [columns[:, 2 * kind + 1 : 2 * kind + 2] for kind in range(4)]
    master[...] = decoder[...].astype(f32).T
    near_id_table, near_time_table = near_ids[...], near_times[...]

    gather_events(memory, first_columns, near_id_table, near_time_table, stacked, target_rows)
    link_gradient(
        stacked, master[...].astype(bf16), logits_out, 0, deltas, gradient, rounded.at[0]
    )
    pl.semaphore_wait(barrier, len(greeted) + half - 1 + half * (place.pair // half))

    @pl.when(place.pair >= half)
    def _():
        pl.semaphore_signal(greeting, 1, device_id=place.mirror(), device_id_type=MESH)


    hands = []
    for slot, (kept, handed) in enumerate(
        ((source_ids, handed_source), (target_ids, handed_target))
    ):
        copy = pltpu.make_async_remote_copy(
            src_ref=kept.at[0],
            dst_ref=handed,
            send_sem=hand_sems.at[0, slot],
            recv_sem=hand_sems.at[1, slot],
            device_id=place.next_epoch(),
            device_id_type=MESH,
        )
        copy.start()
        hands.append(copy)
    sums = [
        TrainerSum(
            place,
            gradient,
            rounded.at[batch],
            near_in.at[batch],
            far_in.at[batch],
            half_sums.at[batch],
            (total, last_total)[batch],
            sum_sems.at[batch],
        )
        for batch in range(2)
    ]
    sums[0].scatter()
    for hand in hands:
        hand.wait_recv()
    for load in loads[8:]:
        load.wait()
    handed_rows = jnp.concatenate(
        [handed_source[...], handed_target[...], handed_source[...], handed_target[...]], axis=0
    ).astype(f32)
    handed_columns = handed_rows.T
    nodes = memory.shape[0]
    source = matmul(column_picks(handed_columns[:, 0:1], nodes), memory[...]).astype(bf16)
    target = matmul(column_picks(handed_columns[:, 2:3], nodes), memory[...]).astype(bf16)
    fresh = fresh_rows(source, target, gru_input, gru_state)
    sums[0].exchange()

    handed_memory[...] = replaced(memory, handed_rows[2:3, :], fresh)
    gather_events(
        handed_memory, second_columns, near_id_table, near_time_table, stacked, target_rows
    )
    sums[0].bridge(greeting)
    sums[0].gather()
    sums[0].arrive()

    master[...] = stepped(master[...], total)
    link_gradient(
        stacked, master[...].astype(bf16), logits_out, 2, deltas, gradient, rounded.at[1]
    )
    sums[1].scatter()
    events = target_rows.shape[0]
    fresh = fresh_rows(stacked[0:events, :], target_rows[...], gru_input, gru_state)
    sums[1].exchange()
    memory_out[...] = replaced(handed_memory, ids[3:4, :], fresh)
    sums[1].bridge(None)
    sums[1].gather()
    sums[1].arrive()
    for hand in hands:
        hand.wait_send()
    for each in sums:
        each.close()


def results_kernel(memory, master, total, logits, memory_out, decoder_out, logits_out, decoder, sems):
    stores = [
        pltpu.make_async_copy(memory, memory_out.at[0], sems.at[0]),
        pltpu.make_async_copy(logits, logits_out.at[0], sems.at[1]),
        pltpu.make_async_copy(decoder, decoder_out.at[0], sems.at[2]),
    ]
    stores[0].start()
    stores[1].start()
    decoder[...] = stepped(master[...], total).T
    stores[2].start()
    for store in stores:
        store.wait()


def on_device(*given):
    node_memory, neighbour_ids, neighbour_ticks, source_ids, target_ids, negative_ids = given[:6]
    event_ticks, gru_input, gru_state, decoder_weight = given[6:]
    nodes, width = node_memory.shape
    hidden = decoder_weight.shape[1]
    batches, events = source_ids.shape[1:]
    vmem, dma = pltpu.VMEM, pltpu.SemaphoreType.DMA
    held = pl.BlockSpec(memory_space=vmem)
    kept = pl.pallas_call(
        window_kernel,
        out_shape=(
            vmem((nodes, width), bf16),
            vmem((hidden, width), f32),
            vmem((hidden, width), bf16),
            vmem((2 * batches, events), f32),
        ),
        in_specs=[pl.BlockSpec(memory_space=pltpu.HBM)] * 10,
        out_specs=(held,) * 4,
        scratch_shapes=[
            vmem(node_memory.shape, bf16),
            vmem(neighbour_ids.shape, jnp.int32),
            vmem(neighbour_ticks.shape, jnp.int32),
            vmem(source_ids.shape, jnp.int32),
            vmem(target_ids.shape, jnp.int32),
            vmem(negative_ids.shape, jnp.int32),
            vmem(event_ticks.shape, jnp.int32),
            vmem(gru_input.shape, bf16),
            vmem(gru_state.shape, bf16),
            vmem(decoder_weight.shape, bf16),
            vmem((batches, events), jnp.int32),
            vmem((batches, events), jnp.int32),
            vmem((nodes, width), bf16),
            vmem((3 * events, width), bf16),
            vmem((events, width), bf16),
            vmem((hidden, 3 * events), bf16),
            vmem((hidden, width), f32),
            vmem((batches, hidden, width), bf16),
            vmem((batches, near_count, hidden // near_count, width), bf16),
            vmem((batches, far_count, hidden // near_count, width), bf16),
            vmem((batches, hidden // near_count, width), bf16),
            vmem((hidden, width), bf16),
            dma((10,)),
            dma((2, 2)),
            dma((batches, 6, near_count)),
            pltpu.SemaphoreType.REGULAR,
        ],
        compiler_params=pltpu.CompilerParams(
            collective_id=0, has_side_effects=True, vmem_limit_bytes=50 * 2**20
        ),
        name="window",
    )(*(pltpu.with_memory_space_constraint(each, pltpu.HBM) for each in given))
    stored = pl.BlockSpec(memory_space=pltpu.HBM)
    return pl.pallas_call(
        results_kernel,
        out_shape=(
            jax.ShapeDtypeStruct((1, nodes, width), bf16),
            jax.ShapeDtypeStruct((1, width, hidden), f32),
            jax.ShapeDtypeStruct((1, 2 * batches, events), f32),
        ),
        in_specs=[held] * 4,
        out_specs=(stored,) * 3,
        scratch_shapes=[vmem((width, hidden), f32), dma((3,))],
        compiler_params=pltpu.CompilerParams(vmem_limit_bytes=8 * 2**20),
        name="results",
    )(*(pltpu.with_memory_space_constraint(each, pltpu.VMEM) for each in kept))


def solution(mesh):
    in_specs = (
        P(("batch", "mem"), None),
        P(None, ("batch", "mem")),
        P(None, ("batch", "mem")),
        P("epoch", None, ("batch", "mem")),
        P("epoch", None, ("batch", "mem")),
        P("epoch", None, ("batch", "mem")),
        P("epoch", None, ("batch", "mem")),
        P(),
        P(),
        P(),
    )
    out_specs = (
        P("epoch", ("batch", "mem"), None),
        P("epoch", None, None),
        P("epoch", None, ("batch", "mem")),
    )
    return jax.shard_map(
        on_device, mesh=mesh, in_specs=in_specs, out_specs=out_specs, check_vma=False
    )
```

```python
import jax
import jax.numpy as jnp
from jax import lax
from jax.experimental import pallas as pl
from jax.experimental.pallas import tpu as pltpu
from jax.sharding import PartitionSpec as P

MESH = pl.DeviceIdType.MESH
bf16, f32 = jnp.bfloat16, jnp.float32
tick_scale = 100.0
step_length = 4.0
epsilon = 1e-06
near_count, far_count = 16, 8
half = far_count // 2


def matmul(a, b):
    return jnp.dot(a, b, preferred_element_type=f32)


def matmul_nt(a, b):
    return lax.dot_general(a, b, (((1,), (1,)), ((), ())), preferred_element_type=f32)


def device_at(y, z, core):
    return {"batch": y * 8 + z % 8, "mem": (z // 8) * 2 + core}


class Place:
    def __init__(self):
        self.epoch = lax.axis_index("epoch")
        batch, mem = lax.axis_index("batch"), lax.axis_index("mem")
        self.y, self.core = batch // 8, mem % 2
        z = (mem // 2) * 8 + batch % 8
        self.pair, self.side = z // 2, z % 2
        self.piece = (self.y * 2 + self.core) * 2 + self.side

    def near(self, step):
        y, core = (self.y + step // 4) % 4, (self.core + (step // 2) % 2) % 2
        side = (self.side + step % 2) % 2
        return device_at(y, self.pair * 2 + side, core), (y * 2 + core) * 2 + side

    def far_pair(self, step):
        return (self.pair + step + far_count) % far_count

    def far(self, step):
        return device_at(self.y, self.far_pair(step) * 2 + self.side, self.core)

    def mirror(self):
        return device_at(self.y, (far_count - 1 - self.pair) * 2 + self.side, self.core)

    def next_epoch(self):
        return {"epoch": (self.epoch + 1) % 4}

    def last_epoch(self):
        return {"epoch": (self.epoch + 3) % 4}


near_steps = sorted(range(1, near_count), key=lambda k: -(min(k // 4, 4 - k // 4) + k % 2))
far_steps = (4, 3, 5, 2, 6, 1, 7)


class TrainerSum:
    def __init__(
        self, place, gradient, rounded, near_in, far_in, half_sum, total, sems, greetings, chain
    ):
        self.place, self.gradient, self.rounded = place, gradient, rounded
        self.near_in, self.far_in, self.half_sum = near_in, far_in, half_sum
        self.total, self.sems, self.greetings = total, sems, greetings
        self.chained = chain is not None
        if self.chained:
            self.chain_in, self.chain_out, self.running = (chain.at[slot] for slot in range(3))
        self.own = pl.ds(pl.multiple_of(place.piece * 16, 16), 16)
        self.copies = []

    def copy_of(self, src, dst, stage, step, device):
        return pltpu.make_async_remote_copy(
            src_ref=src,
            dst_ref=dst,
            send_sem=self.sems.at[2 * stage, step],
            recv_sem=self.sems.at[2 * stage + 1, step],
            device_id=device,
            device_id_type=MESH,
        )

    def send(self, src, dst, stage, step, device):
        copy = self.copy_of(src, dst, stage, step, device)
        copy.start()
        self.copies.append(copy)
        return copy

    def scatter(self):
        self.pending = []
        for step in near_steps:
            device, piece = self.place.near(step)
            rows = pl.ds(pl.multiple_of(piece * 16, 16), 16)
            copy = self.send(self.rounded.at[rows], self.near_in.at[step], 0, step, device)
            self.pending.append((step, copy))

    def exchange(self):
        value = self.gradient[self.own, :]
        for step, copy in reversed(self.pending):
            copy.wait_recv()
            value = value + self.near_in[step].astype(f32)
        place = self.place
        self.far_in[place.pair] = value.astype(bf16)
        if not self.chained:
            for step in range(2, half):

                @pl.when(place.pair + step < half)
                def _(step=step):
                    pl.semaphore_wait(self.greetings.at[step], 1)

        for step in far_steps:

            @pl.when(self.sends_far(step))
            def _(step=step):
                self.far_copy(step).start()

    def sends_far(self, step):
        pair, peer = self.place.pair, self.place.far_pair(step)
        return (pair >= half) | (peer < (pair if self.chained else half))

    def far_copy(self, step):
        slot = self.far_in.at[self.place.pair]
        return self.copy_of(slot, slot, 1, step, self.place.far(step))

    def bridge_copy(self):
        return self.copy_of(self.half_sum, self.half_sum, 1, 0, self.place.mirror())

    def chain_copy(self):
        return self.copy_of(self.chain_out, self.chain_in, 2, 0, self.place.far(1))

    def bridge(self):
        place = self.place

        @pl.when(place.pair < half)
        def _():
            if self.chained:
                self.chain_out[...] = self.far_in[place.pair].astype(f32)

                @pl.when(place.pair > 0)
                def _():
                    self.chain_copy().wait_recv()
                    self.chain_out[...] += self.chain_in[...]

                @pl.when(place.pair < half - 1)
                def _():
                    pl.semaphore_wait(self.greetings.at[1], 1)
                    self.chain_copy().start()

                self.running[...] = self.chain_out[...]
                for pair in range(1, half):

                    @pl.when(place.pair < pair)
                    def _(pair=pair):
                        self.arrived_from(pair)
                        self.running[...] += self.far_in[pair].astype(f32)

                self.half_sum[...] = self.running[...].astype(bf16)
                pl.semaphore_wait(self.greetings.at[0], 1)
            else:
                for step in far_steps:

                    @pl.when(place.far_pair(-step) < half)
                    def _(step=step):
                        self.far_copy(step).wait_recv()

                value = self.far_in[0].astype(f32)
                for slot in range(1, half):
                    value = value + self.far_in[slot].astype(f32)
                self.half_sum[...] = value.astype(bf16)
            self.bridge_copy().start()

    def arrived_from(self, pair):
        step = (self.place.pair - pair + far_count) % far_count
        slot = self.far_in.at[pair]
        self.copy_of(slot, slot, 1, step, self.place.far(1)).wait_recv()

    def gather(self):
        place = self.place
        for step in far_steps:

            @pl.when(place.far_pair(-step) >= half)
            def _(step=step):
                self.far_copy(step).wait_recv()

        @pl.when(place.pair >= half)
        def _():
            self.bridge_copy().wait_recv()

        value = self.half_sum[...].astype(f32)
        for slot in range(half, far_count):
            value = value + self.far_in[slot].astype(f32)
        self.total[self.own, :] = value.astype(bf16)
        rows = self.total.at[self.own]
        self.pending = [
            self.send(rows, rows, 2, step, self.place.near(step)[0]) for step in near_steps
        ]

    def arrive(self):
        for copy in self.pending:
            copy.wait_recv()

    def close(self):
        place = self.place
        for copy in self.copies:
            copy.wait_send()
        for step in far_steps:

            @pl.when(self.sends_far(step))
            def _(step=step):
                self.far_copy(step).wait_send()

        @pl.when(place.pair < half)
        def _():
            self.bridge_copy().wait_send()

        if self.chained:

            @pl.when(place.pair < half - 1)
            def _():
                self.chain_copy().wait_send()


def column_picks(column, count):
    lanes = lax.broadcasted_iota(jnp.int32, (column.shape[0], count), 1).astype(f32)
    return jnp.where(column == lanes, 1.0, 0.0).astype(bf16)


def row_picks(row, count):
    names = lax.broadcasted_iota(jnp.int32, (count, row.shape[1]), 0).astype(f32)
    return jnp.where(row == names, 1.0, 0.0)


def neighbour_weights(target_picks, ticks, near_ids, near_times):
    def looked_up(table):
        low = (table & 255).astype(f32).astype(bf16)
        high = (table >> 8).astype(f32).astype(bf16)
        return matmul_nt(target_picks, low) + 256.0 * matmul_nt(target_picks, high)

    ids, times = looked_up(near_ids), looked_up(near_times)
    decay = tick_scale / (tick_scale + (ticks - times))
    decay = decay / jnp.sum(decay, axis=1, keepdims=True)
    events, nodes = target_picks.shape
    lanes = lax.broadcasted_iota(jnp.int32, (events, nodes), 1).astype(f32)
    weights = jnp.zeros((events, nodes), f32)
    for slot in range(near_ids.shape[0]):
        chosen = ids[:, slot : slot + 1] == lanes
        weights = weights + jnp.where(chosen, decay[:, slot : slot + 1], 0.0)
    return weights


def gather_events(memory, columns, near_ids, near_times, stacked, target_rows):
    source, target, negative, ticks = columns
    events, nodes = source.shape[0], memory.shape[0]
    target_picks = column_picks(target, nodes)
    stacked[0:events, :] = matmul(column_picks(source, nodes), memory[...]).astype(bf16)
    stacked[2 * events :, :] = matmul(column_picks(negative, nodes), memory[...]).astype(bf16)
    rows = matmul(target_picks, memory[...])
    target_rows[...] = rows.astype(bf16)
    weights = neighbour_weights(target_picks, ticks, near_ids, near_times)
    high = weights.astype(bf16)
    low = (weights - high.astype(f32)).astype(bf16)
    aggregate = matmul(high, memory[...]) + matmul(low, memory[...])
    stacked[events : 2 * events, :] = (0.5 * (rows + aggregate)).astype(bf16)


def link_gradient(stacked, projection, logits, row, deltas, gradient, rounded):
    events = stacked.shape[0] // 3
    scale = 1.0 / projection.shape[0] ** 0.5
    projected = matmul_nt(projection, stacked[...])
    source = projected[:, :events]
    target = projected[:, events : 2 * events]
    negative = projected[:, 2 * events :]
    positive = jnp.sum(source * target, axis=0, keepdims=True) * scale
    negative_logit = jnp.sum(source * negative, axis=0, keepdims=True) * scale
    logits[row : row + 1, :] = positive
    logits[row + 1 : row + 2, :] = negative_logit
    grad_positive = -jax.nn.sigmoid(-positive) * scale
    grad_negative = jax.nn.sigmoid(negative_logit) * scale
    deltas[:, :events] = (grad_positive * target + grad_negative * negative).astype(bf16)
    deltas[:, events : 2 * events] = (grad_positive * source).astype(bf16)
    deltas[:, 2 * events :] = (grad_negative * source).astype(bf16)
    value = matmul(deltas[...], stacked[...])
    gradient[...] = value
    rounded[...] = value.astype(bf16)


def fresh_rows(source_rows, target_rows, gru_input, gru_state):
    width = source_rows.shape[1]

    def gate(weights, rows, part):
        return matmul(rows, weights[:, part * width : (part + 1) * width])

    reset = jax.nn.sigmoid(gate(gru_input, source_rows, 0) + gate(gru_state, target_rows, 0))
    candidate = jnp.tanh(
        gate(gru_input, source_rows, 2) + reset * gate(gru_state, target_rows, 2)
    )
    update = jax.nn.sigmoid(gate(gru_input, source_rows, 1) + gate(gru_state, target_rows, 1))
    return ((1.0 - update) * candidate + update * target_rows.astype(f32)).astype(bf16)


def replaced(memory, target_row, fresh):
    picks = row_picks(target_row, memory.shape[0])
    hit = jnp.sum(picks, axis=1, keepdims=True)
    placed = matmul(picks.astype(bf16), fresh)
    return jnp.where(hit > 0.5, placed, memory[...].astype(f32)).astype(bf16)


def stepped(master, total):
    total = total[...].astype(f32)
    return master - step_length * total / jnp.sqrt(jnp.sum(total * total) + epsilon)


def window_kernel(
    memory_hbm,
    near_ids_hbm,
    near_times_hbm,
    source_ids_hbm,
    target_ids_hbm,
    negative_ids_hbm,
    event_ticks_hbm,
    gru_input_hbm,
    gru_state_hbm,
    decoder_hbm,
    memory_out,
    master,
    last_total,
    logits_out,
    memory,
    near_ids,
    near_times,
    source_ids,
    target_ids,
    negative_ids,
    event_ticks,
    gru_input,
    gru_state,
    decoder,
    handed_source,
    handed_target,
    handed_memory,
    stacked,
    target_rows,
    deltas,
    gradient,
    rounded,
    near_in,
    far_in,
    half_sums,
    chain,
    total,
    load_sems,
    hand_sems,
    sum_sems,
    greetings,
):
    place = Place()
    barrier = pltpu.get_barrier_semaphore()
    greeted = [place.near(step)[0] for step in near_steps]
    greeted += [place.next_epoch(), place.last_epoch()]
    loads = [
        pltpu.make_async_copy(stored, held, load_sems.at[slot])
        for slot, (stored, held) in enumerate(
            (
                (memory_hbm, memory),
                (source_ids_hbm, source_ids),
                (target_ids_hbm, target_ids),
                (negative_ids_hbm, negative_ids),
                (event_ticks_hbm, event_ticks),
                (near_ids_hbm, near_ids),
                (near_times_hbm, near_times),
                (decoder_hbm, decoder),
                (gru_input_hbm, gru_input),
                (gru_state_hbm, gru_state),
            )
        )
    ]
    for load in loads[:8]:
        load.start()
    for step in far_steps:

        @pl.when(
            (place.far_pair(step) > place.pair)
            | ((place.pair >= half) & (place.far_pair(step) >= half))
        )
        def _(step=step):
            pl.semaphore_signal(barrier, 1, device_id=place.far(step), device_id_type=MESH)

    for device in greeted:
        pl.semaphore_signal(barrier, 1, device_id=device, device_id_type=MESH)
    for load in loads[:8]:
        load.wait()
    for load in loads[8:]:
        load.start()

    ids = jnp.concatenate(
        [source_ids[0], target_ids[0], negative_ids[0], event_ticks[0]], axis=0
    ).astype(f32)
    columns = ids.T
    first_columns = [columns[:, 2 * kind : 2 * kind + 1] for kind in range(4)]
    second_columns = [columns[:, 2 * kind + 1 : 2 * kind + 2] for kind in range(4)]
    master[...] = decoder[...].astype(f32).T
    near_id_table, near_time_table = near_ids[...], near_times[...]

    gather_events(memory, first_columns, near_id_table, near_time_table, stacked, target_rows)
    link_gradient(
        stacked, master[...].astype(bf16), logits_out, 0, deltas, gradient, rounded.at[0]
    )
    late = place.pair // half
    earlier = (1 - late) * place.pair + late * (far_count - 1)
    pl.semaphore_wait(barrier, len(greeted) + earlier)

    @pl.when(place.pair >= half)
    def _():
        pl.semaphore_signal(greetings.at[0], 1, device_id=place.mirror(), device_id_type=MESH)

    for step in range(1, half):

        @pl.when((place.pair < half) & (place.pair >= step))
        def _(step=step):
            pl.semaphore_signal(
                greetings.at[step], 1, device_id=place.far(-step), device_id_type=MESH
            )


    hands = []
    for slot, (kept, handed) in enumerate(
        ((source_ids, handed_source), (target_ids, handed_target))
    ):
        copy = pltpu.make_async_remote_copy(
            src_ref=kept.at[0],
            dst_ref=handed,
            send_sem=hand_sems.at[0, slot],
            recv_sem=hand_sems.at[1, slot],
            device_id=place.next_epoch(),
            device_id_type=MESH,
        )
        copy.start()
        hands.append(copy)
    sums = [
        TrainerSum(
            place,
            gradient,
            rounded.at[batch],
            near_in.at[batch],
            far_in.at[batch],
            half_sums.at[batch],
            (total, last_total)[batch],
            sum_sems.at[batch],
            greetings,
            (chain, None)[batch],
        )
        for batch in range(2)
    ]
    sums[0].scatter()
    for hand in hands:
        hand.wait_recv()
    for load in loads[8:]:
        load.wait()
    handed_rows = jnp.concatenate(
        [handed_source[...], handed_target[...], handed_source[...], handed_target[...]], axis=0
    ).astype(f32)
    handed_columns = handed_rows.T
    nodes = memory.shape[0]
    source = matmul(column_picks(handed_columns[:, 0:1], nodes), memory[...]).astype(bf16)
    target = matmul(column_picks(handed_columns[:, 2:3], nodes), memory[...]).astype(bf16)
    fresh = fresh_rows(source, target, gru_input, gru_state)
    sums[0].exchange()

    handed_memory[...] = replaced(memory, handed_rows[2:3, :], fresh)
    gather_events(
        handed_memory, second_columns, near_id_table, near_time_table, stacked, target_rows
    )
    sums[0].bridge()
    sums[0].gather()
    sums[0].arrive()

    master[...] = stepped(master[...], total)
    link_gradient(
        stacked, master[...].astype(bf16), logits_out, 2, deltas, gradient, rounded.at[1]
    )
    sums[1].scatter()
    events = target_rows.shape[0]
    fresh = fresh_rows(stacked[0:events, :], target_rows[...], gru_input, gru_state)
    sums[1].exchange()
    memory_out[...] = replaced(handed_memory, ids[3:4, :], fresh)
    sums[1].bridge()
    sums[1].gather()
    sums[1].arrive()
    for hand in hands:
        hand.wait_send()
    for each in sums:
        each.close()


def results_kernel(memory, master, total, logits, memory_out, decoder_out, logits_out, decoder, sems):
    stores = [
        pltpu.make_async_copy(memory, memory_out.at[0], sems.at[0]),
        pltpu.make_async_copy(logits, logits_out.at[0], sems.at[1]),
        pltpu.make_async_copy(decoder, decoder_out.at[0], sems.at[2]),
    ]
    stores[0].start()
    stores[1].start()
    decoder[...] = stepped(master[...], total).T
    stores[2].start()
    for store in stores:
        store.wait()


def on_device(*given):
    node_memory, neighbour_ids, neighbour_ticks, source_ids, target_ids, negative_ids = given[:6]
    event_ticks, gru_input, gru_state, decoder_weight = given[6:]
    nodes, width = node_memory.shape
    hidden = decoder_weight.shape[1]
    batches, events = source_ids.shape[1:]
    vmem, dma = pltpu.VMEM, pltpu.SemaphoreType.DMA
    held = pl.BlockSpec(memory_space=vmem)
    kept = pl.pallas_call(
        window_kernel,
        out_shape=(
            vmem((nodes, width), bf16),
            vmem((hidden, width), f32),
            vmem((hidden, width), bf16),
            vmem((2 * batches, events), f32),
        ),
        in_specs=[pl.BlockSpec(memory_space=pltpu.HBM)] * 10,
        out_specs=(held,) * 4,
        scratch_shapes=[
            vmem(node_memory.shape, bf16),
            vmem(neighbour_ids.shape, jnp.int32),
            vmem(neighbour_ticks.shape, jnp.int32),
            vmem(source_ids.shape, jnp.int32),
            vmem(target_ids.shape, jnp.int32),
            vmem(negative_ids.shape, jnp.int32),
            vmem(event_ticks.shape, jnp.int32),
            vmem(gru_input.shape, bf16),
            vmem(gru_state.shape, bf16),
            vmem(decoder_weight.shape, bf16),
            vmem((batches, events), jnp.int32),
            vmem((batches, events), jnp.int32),
            vmem((nodes, width), bf16),
            vmem((3 * events, width), bf16),
            vmem((events, width), bf16),
            vmem((hidden, 3 * events), bf16),
            vmem((hidden, width), f32),
            vmem((batches, hidden, width), bf16),
            vmem((batches, near_count, hidden // near_count, width), bf16),
            vmem((batches, far_count, hidden // near_count, width), bf16),
            vmem((batches, hidden // near_count, width), bf16),
            vmem((3, hidden // near_count, width), f32),
            vmem((hidden, width), bf16),
            dma((10,)),
            dma((2, 2)),
            dma((batches, 6, near_count)),
            pltpu.SemaphoreType.REGULAR((half,)),
        ],
        compiler_params=pltpu.CompilerParams(
            collective_id=0, has_side_effects=True, vmem_limit_bytes=50 * 2**20
        ),
        name="window",
    )(*(pltpu.with_memory_space_constraint(each, pltpu.HBM) for each in given))
    stored = pl.BlockSpec(memory_space=pltpu.HBM)
    return pl.pallas_call(
        results_kernel,
        out_shape=(
            jax.ShapeDtypeStruct((1, nodes, width), bf16),
            jax.ShapeDtypeStruct((1, width, hidden), f32),
            jax.ShapeDtypeStruct((1, 2 * batches, events), f32),
        ),
        in_specs=[held] * 4,
        out_specs=(stored,) * 3,
        scratch_shapes=[vmem((width, hidden), f32), dma((3,))],
        compiler_params=pltpu.CompilerParams(vmem_limit_bytes=8 * 2**20),
        name="results",
    )(*(pltpu.with_memory_space_constraint(each, pltpu.VMEM) for each in kept))


def solution(mesh):
    in_specs = (
        P(("batch", "mem"), None),
        P(None, ("batch", "mem")),
        P(None, ("batch", "mem")),
        P("epoch", None, ("batch", "mem")),
        P("epoch", None, ("batch", "mem")),
        P("epoch", None, ("batch", "mem")),
        P("epoch", None, ("batch", "mem")),
        P(),
        P(),
        P(),
    )
    out_specs = (
        P("epoch", ("batch", "mem"), None),
        P("epoch", None, None),
        P("epoch", None, ("batch", "mem")),
    )
    return jax.shard_map(
        on_device, mesh=mesh, in_specs=in_specs, out_specs=out_specs, check_vma=False
    )
```

```python
import jax
import jax.numpy as jnp
from jax import lax
from jax.experimental import pallas as pl
from jax.experimental.pallas import tpu as pltpu
from jax.sharding import PartitionSpec as P

MESH = pl.DeviceIdType.MESH
bf16, f32 = jnp.bfloat16, jnp.float32
tick_scale = 100.0
step_length = 4.0
epsilon = 1e-06
near_count, far_count = 16, 8
half = far_count // 2
near_out, early_out, late_out, bridge_out, back_out = range(5)


def matmul(a, b):
    return jnp.dot(a, b, preferred_element_type=f32)


def matmul_nt(a, b):
    return lax.dot_general(a, b, (((1,), (1,)), ((), ())), preferred_element_type=f32)


def device_at(y, z, core):
    return {"batch": y * 8 + z % 8, "mem": (z // 8) * 2 + core}


class Place:
    def __init__(self):
        self.epoch = lax.axis_index("epoch")
        batch, mem = lax.axis_index("batch"), lax.axis_index("mem")
        self.y, self.core = batch // 8, mem % 2
        z = (mem // 2) * 8 + batch % 8
        self.pair, self.side = z // 2, z % 2
        self.piece = (self.y * 2 + self.core) * 2 + self.side

    def near(self, step):
        y, core = (self.y + step // 4) % 4, (self.core + (step // 2) % 2) % 2
        side = (self.side + step % 2) % 2
        return device_at(y, self.pair * 2 + side, core), (y * 2 + core) * 2 + side

    def far_pair(self, step):
        return (self.pair + step + far_count) % far_count

    def far(self, step):
        return device_at(self.y, self.far_pair(step) * 2 + self.side, self.core)

    def mirror(self):
        return device_at(self.y, (far_count - 1 - self.pair) * 2 + self.side, self.core)

    def next_epoch(self):
        return {"epoch": (self.epoch + 1) % 4}

    def last_epoch(self):
        return {"epoch": (self.epoch + 3) % 4}


near_steps = sorted(range(1, near_count), key=lambda k: -(min(k // 4, 4 - k // 4) + k % 2))
far_steps = (4, 3, 5, 2, 6, 1, 7)


class TrainerSum:
    def __init__(self, place, gradient, rounded, near_in, far_in, half_sum, total, sems):
        self.place, self.gradient, self.rounded = place, gradient, rounded
        self.near_in, self.far_in, self.half_sum = near_in, far_in, half_sum
        self.total, self.sems = total, sems
        self.own = pl.ds(pl.multiple_of(place.piece * 16, 16), 16)

    def copy_of(self, src, dst, stage, device):
        return pltpu.make_async_remote_copy(
            src_ref=src,
            dst_ref=dst,
            send_sem=self.sems.at[0, stage],
            recv_sem=self.sems.at[1, stage],
            device_id=device,
            device_id_type=MESH,
        )

    def all_of(self, rows, stage):
        return self.copy_of(rows, rows, stage, self.place.mirror())

    def scatter(self):
        for step in near_steps:
            device, piece = self.place.near(step)
            rows = pl.ds(pl.multiple_of(piece * 16, 16), 16)
            self.copy_of(self.rounded.at[rows], self.near_in.at[step - 1], near_out, device).start()

    def exchange(self):
        self.all_of(self.near_in, near_out).wait_recv()
        value = self.gradient[self.own, :]
        for slot in range(near_count - 1):
            value = value + self.near_in[slot].astype(f32)
        place = self.place
        self.far_in[place.pair] = value.astype(bf16)
        slot = self.far_in.at[place.pair]
        for step in far_steps:

            @pl.when(place.pair >= half)
            def _(step=step):
                self.copy_of(slot, slot, late_out, place.far(step)).start()

            @pl.when((place.pair < half) & (place.far_pair(step) < half))
            def _(step=step):
                self.copy_of(slot, slot, early_out, place.far(step)).start()

    def bridge_copy(self):
        return self.copy_of(self.half_sum, self.half_sum, bridge_out, self.place.mirror())

    def bridge(self, greeting):
        @pl.when(self.place.pair < half)
        def _():
            self.all_of(self.far_in.at[: half - 1], early_out).wait_recv()
            value = self.far_in[0].astype(f32)
            for slot in range(1, half):
                value = value + self.far_in[slot].astype(f32)
            self.half_sum[...] = value.astype(bf16)
            if greeting is not None:
                pl.semaphore_wait(greeting, 1)
            self.bridge_copy().start()

    def gather(self):
        @pl.when(self.place.pair < half)
        def _():
            self.all_of(self.far_in.at[:half], late_out).wait_recv()

        @pl.when(self.place.pair >= half)
        def _():
            self.all_of(self.far_in.at[: half - 1], late_out).wait_recv()
            self.bridge_copy().wait_recv()

        value = self.half_sum[...].astype(f32)
        for slot in range(half, far_count):
            value = value + self.far_in[slot].astype(f32)
        self.total[self.own, :] = value.astype(bf16)
        rows = self.total.at[self.own]
        for step in near_steps:
            self.copy_of(rows, rows, back_out, self.place.near(step)[0]).start()

    def arrive(self):
        self.all_of(self.near_in, back_out).wait_recv()

    def close(self):
        self.all_of(self.near_in, near_out).wait_send()
        self.all_of(self.near_in, back_out).wait_send()

        @pl.when(self.place.pair < half)
        def _():
            self.all_of(self.far_in.at[: half - 1], early_out).wait_send()
            self.bridge_copy().wait_send()

        @pl.when(self.place.pair >= half)
        def _():
            self.all_of(self.far_in.at[: far_count - 1], late_out).wait_send()


def column_picks(column, count):
    lanes = lax.broadcasted_iota(jnp.int32, (column.shape[0], count), 1).astype(f32)
    return jnp.where(column == lanes, 1.0, 0.0).astype(bf16)


def row_picks(row, count):
    names = lax.broadcasted_iota(jnp.int32, (count, row.shape[1]), 0).astype(f32)
    return jnp.where(row == names, 1.0, 0.0)


def neighbour_weights(target_picks, ticks, near_ids, near_times):
    def looked_up(table):
        low = (table & 255).astype(f32).astype(bf16)
        high = (table >> 8).astype(f32).astype(bf16)
        return matmul_nt(target_picks, low) + 256.0 * matmul_nt(target_picks, high)

    ids, times = looked_up(near_ids), looked_up(near_times)
    decay = tick_scale / (tick_scale + (ticks - times))
    decay = decay / jnp.sum(decay, axis=1, keepdims=True)
    events, nodes = target_picks.shape
    lanes = lax.broadcasted_iota(jnp.int32, (events, nodes), 1).astype(f32)
    weights = jnp.zeros((events, nodes), f32)
    for slot in range(near_ids.shape[0]):
        chosen = ids[:, slot : slot + 1] == lanes
        weights = weights + jnp.where(chosen, decay[:, slot : slot + 1], 0.0)
    return weights


def gather_events(memory, columns, near_ids, near_times, picks, stacked, target_rows):
    source, target, negative, ticks = columns
    events, nodes = source.shape[0], memory.shape[0]
    target_picks = column_picks(target, nodes)
    picks[0:events, :] = column_picks(source, nodes)
    picks[events : 2 * events, :] = column_picks(negative, nodes)
    picks[2 * events :, :] = target_picks
    rows = matmul(picks[...], memory[...])
    stacked[0:events, :] = rows[0:events].astype(bf16)
    stacked[2 * events :, :] = rows[events : 2 * events].astype(bf16)
    rows = rows[2 * events :]
    target_rows[...] = rows.astype(bf16)
    weights = neighbour_weights(target_picks, ticks, near_ids, near_times)
    aggregate = matmul(weights.astype(bf16), memory[...])
    stacked[events : 2 * events, :] = (0.5 * (rows + aggregate)).astype(bf16)


def link_gradient(stacked, projection, logits, row, deltas, gradient, rounded):
    events = stacked.shape[0] // 3
    scale = 1.0 / projection.shape[0] ** 0.5
    projected = matmul_nt(projection, stacked[...])
    source = projected[:, :events]
    target = projected[:, events : 2 * events]
    negative = projected[:, 2 * events :]
    positive = jnp.sum(source * target, axis=0, keepdims=True) * scale
    negative_logit = jnp.sum(source * negative, axis=0, keepdims=True) * scale
    logits[row : row + 1, :] = positive
    logits[row + 1 : row + 2, :] = negative_logit
    grad_positive = -jax.nn.sigmoid(-positive) * scale
    grad_negative = jax.nn.sigmoid(negative_logit) * scale
    deltas[:, :events] = (grad_positive * target + grad_negative * negative).astype(bf16)
    deltas[:, events : 2 * events] = (grad_positive * source).astype(bf16)
    deltas[:, 2 * events :] = (grad_negative * source).astype(bf16)
    value = matmul(deltas[...], stacked[...])
    gradient[...] = value
    rounded[...] = value.astype(bf16)


def fresh_rows(source_rows, target_rows, gru_input, gru_state):
    width = source_rows.shape[1]

    def gate(weights, rows, part):
        return matmul(rows, weights[:, part * width : (part + 1) * width])

    reset = jax.nn.sigmoid(gate(gru_input, source_rows, 0) + gate(gru_state, target_rows, 0))
    candidate = jnp.tanh(
        gate(gru_input, source_rows, 2) + reset * gate(gru_state, target_rows, 2)
    )
    update = jax.nn.sigmoid(gate(gru_input, source_rows, 1) + gate(gru_state, target_rows, 1))
    return ((1.0 - update) * candidate + update * target_rows.astype(f32)).astype(bf16)


def replaced(memory, target_row, fresh):
    picks = row_picks(target_row, memory.shape[0])
    hit = jnp.sum(picks, axis=1, keepdims=True)
    placed = matmul(picks.astype(bf16), fresh)
    return jnp.where(hit > 0.5, placed, memory[...].astype(f32)).astype(bf16)


def stepped(master, total):
    total = total[...].astype(f32)
    return master - step_length * total / jnp.sqrt(jnp.sum(total * total) + epsilon)


def window_kernel(
    memory_hbm,
    near_ids_hbm,
    near_times_hbm,
    source_ids_hbm,
    target_ids_hbm,
    negative_ids_hbm,
    event_ticks_hbm,
    gru_input_hbm,
    gru_state_hbm,
    decoder_hbm,
    memory_out,
    master,
    last_total,
    logits_out,
    memory,
    near_ids,
    near_times,
    source_ids,
    target_ids,
    negative_ids,
    event_ticks,
    gru_input,
    gru_state,
    decoder,
    handed_source,
    handed_target,
    handed_memory,
    picks,
    stacked,
    target_rows,
    deltas,
    gradient,
    rounded,
    near_in,
    far_in,
    half_sums,
    total,
    load_sems,
    hand_sems,
    sum_sems,
    greeting,
):
    place = Place()
    barrier = pltpu.get_barrier_semaphore()
    greeted = [place.near(step)[0] for step in near_steps]
    greeted += [place.next_epoch(), place.last_epoch()]
    loads = [
        pltpu.make_async_copy(stored, held, load_sems.at[slot])
        for slot, (stored, held) in enumerate(
            (
                (memory_hbm, memory),
                (source_ids_hbm, source_ids),
                (target_ids_hbm, target_ids),
                (negative_ids_hbm, negative_ids),
                (event_ticks_hbm, event_ticks),
                (near_ids_hbm, near_ids),
                (near_times_hbm, near_times),
                (decoder_hbm, decoder),
                (gru_input_hbm, gru_input),
                (gru_state_hbm, gru_state),
            )
        )
    ]
    for load in loads[:8]:
        load.start()
    for step in far_steps:

        @pl.when((place.pair < half) | (place.far_pair(step) >= half))
        def _(step=step):
            pl.semaphore_signal(barrier, 1, device_id=place.far(step), device_id_type=MESH)

    for device in greeted:
        pl.semaphore_signal(barrier, 1, device_id=device, device_id_type=MESH)
    for load in loads[:8]:
        load.wait()
    for load in loads[8:]:
        load.start()

    ids = jnp.concatenate(
        [source_ids[0], target_ids[0], negative_ids[0], event_ticks[0]], axis=0
    ).astype(f32)
    columns = ids.T
    first_columns = [columns[:, 2 * kind : 2 * kind + 1] for kind in range(4)]
    second_columns = [columns[:, 2 * kind + 1 : 2 * kind + 2] for kind in range(4)]
    master[...] = decoder[...].astype(f32).T
    near_id_table, near_time_table = near_ids[...], near_times[...]

    gather_events(
        memory, first_columns, near_id_table, near_time_table, picks, stacked, target_rows
    )
    link_gradient(
        stacked, master[...].astype(bf16), logits_out, 0, deltas, gradient, rounded.at[0]
    )
    pl.semaphore_wait(barrier, len(greeted) + half - 1 + half * (place.pair // half))

    @pl.when(place.pair >= half)
    def _():
        pl.semaphore_signal(greeting, 1, device_id=place.mirror(), device_id_type=MESH)


    hands = []
    for slot, (kept, handed) in enumerate(
        ((source_ids, handed_source), (target_ids, handed_target))
    ):
        copy = pltpu.make_async_remote_copy(
            src_ref=kept.at[0],
            dst_ref=handed,
            send_sem=hand_sems.at[0, slot],
            recv_sem=hand_sems.at[1, slot],
            device_id=place.next_epoch(),
            device_id_type=MESH,
        )
        copy.start()
        hands.append(copy)
    sums = [
        TrainerSum(
            place,
            gradient,
            rounded.at[batch],
            near_in.at[batch],
            far_in.at[batch],
            half_sums.at[batch],
            (total, last_total)[batch],
            sum_sems.at[batch],
        )
        for batch in range(2)
    ]
    sums[0].scatter()
    for hand in hands:
        hand.wait_recv()
    for load in loads[8:]:
        load.wait()
    handed_rows = jnp.concatenate(
        [handed_source[...], handed_target[...], handed_source[...], handed_target[...]], axis=0
    ).astype(f32)
    handed_columns = handed_rows.T
    nodes = memory.shape[0]
    source = matmul(column_picks(handed_columns[:, 0:1], nodes), memory[...]).astype(bf16)
    target = matmul(column_picks(handed_columns[:, 2:3], nodes), memory[...]).astype(bf16)
    fresh = fresh_rows(source, target, gru_input, gru_state)
    sums[0].exchange()

    handed_memory[...] = replaced(memory, handed_rows[2:3, :], fresh)
    gather_events(
        handed_memory, second_columns, near_id_table, near_time_table, picks, stacked, target_rows
    )
    sums[0].bridge(greeting)
    sums[0].gather()
    sums[0].arrive()

    master[...] = stepped(master[...], total)
    link_gradient(
        stacked, master[...].astype(bf16), logits_out, 2, deltas, gradient, rounded.at[1]
    )
    sums[1].scatter()
    events = target_rows.shape[0]
    fresh = fresh_rows(stacked[0:events, :], target_rows[...], gru_input, gru_state)
    sums[1].exchange()
    memory_out[...] = replaced(handed_memory, ids[3:4, :], fresh)
    sums[1].bridge(None)
    sums[1].gather()
    sums[1].arrive()
    for hand in hands:
        hand.wait_send()
    for each in sums:
        each.close()


def results_kernel(memory, master, total, logits, memory_out, decoder_out, logits_out, decoder, sems):
    stores = [
        pltpu.make_async_copy(memory, memory_out.at[0], sems.at[0]),
        pltpu.make_async_copy(logits, logits_out.at[0], sems.at[1]),
        pltpu.make_async_copy(decoder, decoder_out.at[0], sems.at[2]),
    ]
    stores[0].start()
    stores[1].start()
    decoder[...] = stepped(master[...], total).T
    stores[2].start()
    for store in stores:
        store.wait()


def on_device(*given):
    node_memory, neighbour_ids, neighbour_ticks, source_ids, target_ids, negative_ids = given[:6]
    event_ticks, gru_input, gru_state, decoder_weight = given[6:]
    nodes, width = node_memory.shape
    hidden = decoder_weight.shape[1]
    batches, events = source_ids.shape[1:]
    vmem, dma = pltpu.VMEM, pltpu.SemaphoreType.DMA
    held = pl.BlockSpec(memory_space=vmem)
    kept = pl.pallas_call(
        window_kernel,
        out_shape=(
            vmem((nodes, width), bf16),
            vmem((hidden, width), f32),
            vmem((hidden, width), bf16),
            vmem((2 * batches, events), f32),
        ),
        in_specs=[pl.BlockSpec(memory_space=pltpu.HBM)] * 10,
        out_specs=(held,) * 4,
        scratch_shapes=[
            vmem(node_memory.shape, bf16),
            vmem(neighbour_ids.shape, jnp.int32),
            vmem(neighbour_ticks.shape, jnp.int32),
            vmem(source_ids.shape, jnp.int32),
            vmem(target_ids.shape, jnp.int32),
            vmem(negative_ids.shape, jnp.int32),
            vmem(event_ticks.shape, jnp.int32),
            vmem(gru_input.shape, bf16),
            vmem(gru_state.shape, bf16),
            vmem(decoder_weight.shape, bf16),
            vmem((batches, events), jnp.int32),
            vmem((batches, events), jnp.int32),
            vmem((nodes, width), bf16),
            vmem((3 * events, nodes), bf16),
            vmem((3 * events, width), bf16),
            vmem((events, width), bf16),
            vmem((hidden, 3 * events), bf16),
            vmem((hidden, width), f32),
            vmem((batches, hidden, width), bf16),
            vmem((batches, near_count - 1, hidden // near_count, width), bf16),
            vmem((batches, far_count, hidden // near_count, width), bf16),
            vmem((batches, hidden // near_count, width), bf16),
            vmem((hidden, width), bf16),
            dma((10,)),
            dma((2, 2)),
            dma((batches, 2, 5)),
            pltpu.SemaphoreType.REGULAR,
        ],
        compiler_params=pltpu.CompilerParams(
            collective_id=0, has_side_effects=True, vmem_limit_bytes=50 * 2**20
        ),
        name="window",
    )(*(pltpu.with_memory_space_constraint(each, pltpu.HBM) for each in given))
    stored = pl.BlockSpec(memory_space=pltpu.HBM)
    return pl.pallas_call(
        results_kernel,
        out_shape=(
            jax.ShapeDtypeStruct((1, nodes, width), bf16),
            jax.ShapeDtypeStruct((1, width, hidden), f32),
            jax.ShapeDtypeStruct((1, 2 * batches, events), f32),
        ),
        in_specs=[held] * 4,
        out_specs=(stored,) * 3,
        scratch_shapes=[vmem((width, hidden), f32), dma((3,))],
        compiler_params=pltpu.CompilerParams(vmem_limit_bytes=8 * 2**20),
        name="results",
    )(*(pltpu.with_memory_space_constraint(each, pltpu.VMEM) for each in kept))


def solution(mesh):
    in_specs = (
        P(("batch", "mem"), None),
        P(None, ("batch", "mem")),
        P(None, ("batch", "mem")),
        P("epoch", None, ("batch", "mem")),
        P("epoch", None, ("batch", "mem")),
        P("epoch", None, ("batch", "mem")),
        P("epoch", None, ("batch", "mem")),
        P(),
        P(),
        P(),
    )
    out_specs = (
        P("epoch", ("batch", "mem"), None),
        P("epoch", None, None),
        P("epoch", None, ("batch", "mem")),
    )
    return jax.shard_map(
        on_device, mesh=mesh, in_specs=in_specs, out_specs=out_specs, check_vma=False
    )
```

```python
import jax
import jax.numpy as jnp
from jax import lax
from jax.experimental import pallas as pl
from jax.experimental.pallas import tpu as pltpu
from jax.sharding import PartitionSpec as P

MESH = pl.DeviceIdType.MESH
bf16, f32 = jnp.bfloat16, jnp.float32
tick_scale = 100.0
step_length = 4.0
epsilon = 1e-06
near_count, far_count = 16, 8
half = far_count // 2
near_out, early_out, late_out, bridge_out, back_out = range(5)


def matmul(a, b):
    return jnp.dot(a, b, preferred_element_type=f32)


def matmul_nt(a, b):
    return lax.dot_general(a, b, (((1,), (1,)), ((), ())), preferred_element_type=f32)


def device_at(y, z, core):
    return {"batch": y * 8 + z % 8, "mem": (z // 8) * 2 + core}


class Place:
    def __init__(self):
        self.epoch = lax.axis_index("epoch")
        batch, mem = lax.axis_index("batch"), lax.axis_index("mem")
        self.y, self.core = batch // 8, mem % 2
        z = (mem // 2) * 8 + batch % 8
        self.pair, self.side = z // 2, z % 2
        self.piece = (self.y * 2 + self.core) * 2 + self.side

    def near(self, step):
        y, core = (self.y + step // 4) % 4, (self.core + (step // 2) % 2) % 2
        side = (self.side + step % 2) % 2
        return device_at(y, self.pair * 2 + side, core), (y * 2 + core) * 2 + side

    def far_pair(self, step):
        return (self.pair + step + far_count) % far_count

    def far(self, step):
        return device_at(self.y, self.far_pair(step) * 2 + self.side, self.core)

    def mirror(self):
        return device_at(self.y, (far_count - 1 - self.pair) * 2 + self.side, self.core)

    def next_epoch(self):
        return {"epoch": (self.epoch + 1) % 4}

    def last_epoch(self):
        return {"epoch": (self.epoch + 3) % 4}


near_steps = sorted(range(1, near_count), key=lambda k: -(min(k // 4, 4 - k // 4) + k % 2))
far_steps = (4, 3, 5, 2, 6, 1, 7)


class TrainerSum:
    def __init__(self, place, gradient, rounded, near_in, far_in, half_sum, total, sems):
        self.place, self.gradient, self.rounded = place, gradient, rounded
        self.near_in, self.far_in, self.half_sum = near_in, far_in, half_sum
        self.total, self.sems = total, sems
        self.own = pl.ds(pl.multiple_of(place.piece * 16, 16), 16)

    def copy_of(self, src, dst, stage, device):
        return pltpu.make_async_remote_copy(
            src_ref=src,
            dst_ref=dst,
            send_sem=self.sems.at[0, stage],
            recv_sem=self.sems.at[1, stage],
            device_id=device,
            device_id_type=MESH,
        )

    def all_of(self, rows, stage):
        return self.copy_of(rows, rows, stage, self.place.mirror())

    def scatter(self):
        for step in near_steps:
            device, piece = self.place.near(step)
            rows = pl.ds(pl.multiple_of(piece * 16, 16), 16)
            self.copy_of(self.rounded.at[rows], self.near_in.at[step - 1], near_out, device).start()

    def exchange(self):
        self.all_of(self.near_in, near_out).wait_recv()
        value = self.gradient[self.own, :]
        for slot in range(near_count - 1):
            value = value + self.near_in[slot].astype(f32)
        place = self.place
        self.far_in[place.pair] = value.astype(bf16)
        slot = self.far_in.at[place.pair]
        for step in far_steps:

            @pl.when(place.pair >= half)
            def _(step=step):
                self.copy_of(slot, slot, late_out, place.far(step)).start()

            @pl.when((place.pair < half) & (place.far_pair(step) < half))
            def _(step=step):
                self.copy_of(slot, slot, early_out, place.far(step)).start()

    def bridge_copy(self):
        return self.copy_of(self.half_sum, self.half_sum, bridge_out, self.place.mirror())

    def bridge(self, greeting):
        @pl.when(self.place.pair < half)
        def _():
            self.all_of(self.far_in.at[: half - 1], early_out).wait_recv()
            value = self.far_in[0].astype(f32)
            for slot in range(1, half):
                value = value + self.far_in[slot].astype(f32)
            self.half_sum[...] = value.astype(bf16)
            if greeting is not None:
                pl.semaphore_wait(greeting, 1)
            self.bridge_copy().start()

    def gather(self):
        @pl.when(self.place.pair < half)
        def _():
            self.all_of(self.far_in.at[:half], late_out).wait_recv()

        @pl.when(self.place.pair >= half)
        def _():
            self.all_of(self.far_in.at[: half - 1], late_out).wait_recv()
            self.bridge_copy().wait_recv()

        value = self.half_sum[...].astype(f32)
        for slot in range(half, far_count):
            value = value + self.far_in[slot].astype(f32)
        self.total[self.own, :] = value.astype(bf16)
        rows = self.total.at[self.own]
        for step in near_steps:
            self.copy_of(rows, rows, back_out, self.place.near(step)[0]).start()

    def arrive(self):
        self.all_of(self.near_in, back_out).wait_recv()

    def close(self):
        self.all_of(self.near_in, near_out).wait_send()
        self.all_of(self.near_in, back_out).wait_send()

        @pl.when(self.place.pair < half)
        def _():
            self.all_of(self.far_in.at[: half - 1], early_out).wait_send()
            self.bridge_copy().wait_send()

        @pl.when(self.place.pair >= half)
        def _():
            self.all_of(self.far_in.at[: far_count - 1], late_out).wait_send()


def column_picks(column, count):
    lanes = lax.broadcasted_iota(jnp.int32, (column.shape[0], count), 1).astype(f32)
    return jnp.where(column == lanes, 1.0, 0.0).astype(bf16)


def row_picks(row, count):
    names = lax.broadcasted_iota(jnp.int32, (count, row.shape[1]), 0).astype(f32)
    return jnp.where(row == names, 1.0, 0.0)


def fill_table(table, near_ids, near_times):
    table[...] = jnp.zeros_like(table)
    count = near_ids.shape[0]
    for part, value in enumerate((near_ids, near_ids, near_times, near_times)):
        value = value[...] >> 8 if part % 2 else value[...] & 255
        table[16 * part : 16 * part + count, :] = value.astype(f32).astype(bf16)


def neighbour_weights(found, count, ticks, nodes):
    ids = found[:, 0:count] + 256.0 * found[:, 16 : 16 + count]
    times = found[:, 32 : 32 + count] + 256.0 * found[:, 48 : 48 + count]
    decay = tick_scale / (tick_scale + (ticks - times))
    decay = decay / jnp.sum(decay, axis=1, keepdims=True)
    events = found.shape[0]
    lanes = lax.broadcasted_iota(jnp.int32, (events, nodes), 1).astype(f32)
    weights = jnp.zeros((events, nodes), f32)
    for slot in range(count):
        chosen = ids[:, slot : slot + 1] == lanes
        weights = weights + jnp.where(chosen, decay[:, slot : slot + 1], 0.0)
    return weights


def gather_events(memory, columns, table, count, picks, stacked, target_rows, ready):
    source, target, negative, ticks = columns
    events, nodes = source.shape[0], memory.shape[0]
    target_picks = column_picks(target, nodes)
    found = matmul_nt(target_picks, table[...])
    picks[2 * events :, :] = target_picks
    picks[0:events, :] = column_picks(source, nodes)
    picks[events : 2 * events, :] = column_picks(negative, nodes)
    ready()
    rows = matmul(picks[...], memory[...])
    weights = neighbour_weights(found, count, ticks, nodes).astype(bf16)
    stacked[0:events, :] = rows[0:events].astype(bf16)
    stacked[2 * events :, :] = rows[events : 2 * events].astype(bf16)
    rows = rows[2 * events :]
    target_rows[...] = rows.astype(bf16)
    aggregate = matmul(weights, memory[...])
    stacked[events : 2 * events, :] = (0.5 * (rows + aggregate)).astype(bf16)


def link_gradient(stacked, projection, logits, row, deltas, gradient, rounded):
    events = stacked.shape[0] // 3
    scale = 1.0 / projection.shape[0] ** 0.5
    projected = matmul_nt(projection, stacked[...])
    source = projected[:, :events]
    target = projected[:, events : 2 * events]
    negative = projected[:, 2 * events :]
    positive = jnp.sum(source * target, axis=0, keepdims=True) * scale
    negative_logit = jnp.sum(source * negative, axis=0, keepdims=True) * scale
    logits[row : row + 1, :] = positive
    logits[row + 1 : row + 2, :] = negative_logit
    grad_positive = -jax.nn.sigmoid(-positive) * scale
    grad_negative = jax.nn.sigmoid(negative_logit) * scale
    deltas[:, :events] = (grad_positive * target + grad_negative * negative).astype(bf16)
    deltas[:, events : 2 * events] = (grad_positive * source).astype(bf16)
    deltas[:, 2 * events :] = (grad_negative * source).astype(bf16)
    value = matmul(deltas[...], stacked[...])
    gradient[...] = value
    rounded[...] = value.astype(bf16)


def fresh_rows(source_rows, target_rows, gru_input, gru_state):
    width = source_rows.shape[1]

    def gate(weights, rows, part):
        return matmul(rows, weights[:, part * width : (part + 1) * width])

    reset = jax.nn.sigmoid(gate(gru_input, source_rows, 0) + gate(gru_state, target_rows, 0))
    candidate = jnp.tanh(
        gate(gru_input, source_rows, 2) + reset * gate(gru_state, target_rows, 2)
    )
    update = jax.nn.sigmoid(gate(gru_input, source_rows, 1) + gate(gru_state, target_rows, 1))
    return ((1.0 - update) * candidate + update * target_rows.astype(f32)).astype(bf16)


def replaced(memory, target_row, fresh):
    picks = row_picks(target_row, memory.shape[0])
    hit = jnp.sum(picks, axis=1, keepdims=True)
    placed = matmul(picks.astype(bf16), fresh)
    return jnp.where(hit > 0.5, placed, memory[...].astype(f32)).astype(bf16)


def step_scale(total):
    total = total[...].astype(f32)
    return step_length / jnp.sqrt(jnp.sum(total * total) + epsilon)


def stepped(master, total, scale):
    return master - scale * total.astype(f32)


def window_kernel(
    memory_hbm,
    near_ids_hbm,
    near_times_hbm,
    source_ids_hbm,
    target_ids_hbm,
    negative_ids_hbm,
    event_ticks_hbm,
    gru_input_hbm,
    gru_state_hbm,
    decoder_hbm,
    memory_out,
    master,
    last_total,
    logits_out,
    memory,
    near_ids,
    near_times,
    source_ids,
    target_ids,
    negative_ids,
    event_ticks,
    gru_input,
    gru_state,
    decoder,
    handed_source,
    handed_target,
    handed_memory,
    table,
    picks,
    stacked,
    target_rows,
    deltas,
    gradient,
    rounded,
    near_in,
    far_in,
    half_sums,
    total,
    load_sems,
    hand_sems,
    sum_sems,
    greeting,
):
    place = Place()
    barrier = pltpu.get_barrier_semaphore()
    greeted = [place.near(step)[0] for step in near_steps]
    greeted += [place.next_epoch(), place.last_epoch()]
    loads = [
        pltpu.make_async_copy(stored, held, load_sems.at[slot])
        for slot, (stored, held) in enumerate(
            (
                (source_ids_hbm, source_ids),
                (target_ids_hbm, target_ids),
                (negative_ids_hbm, negative_ids),
                (event_ticks_hbm, event_ticks),
                (near_ids_hbm, near_ids),
                (near_times_hbm, near_times),
                (memory_hbm, memory),
                (decoder_hbm, decoder),
                (gru_input_hbm, gru_input),
                (gru_state_hbm, gru_state),
            )
        )
    ]
    for load in loads[:8]:
        load.start()
    for step in far_steps:

        @pl.when((place.pair < half) | (place.far_pair(step) >= half))
        def _(step=step):
            pl.semaphore_signal(barrier, 1, device_id=place.far(step), device_id_type=MESH)

    for device in greeted:
        pl.semaphore_signal(barrier, 1, device_id=device, device_id_type=MESH)
    for load in loads[:6]:
        load.wait()

    ids = jnp.concatenate(
        [source_ids[0], target_ids[0], negative_ids[0], event_ticks[0]], axis=0
    ).astype(f32)
    columns = ids.T
    first_columns = [columns[:, 2 * kind : 2 * kind + 1] for kind in range(4)]
    second_columns = [columns[:, 2 * kind + 1 : 2 * kind + 2] for kind in range(4)]
    fill_table(table, near_ids, near_times)
    count = near_ids.shape[0]

    def loaded():
        for load in loads[6:8]:
            load.wait()
        for load in loads[8:]:
            load.start()
        master[...] = decoder[...].astype(f32).T

    gather_events(memory, first_columns, table, count, picks, stacked, target_rows, loaded)
    link_gradient(
        stacked, master[...].astype(bf16), logits_out, 0, deltas, gradient, rounded.at[0]
    )
    pl.semaphore_wait(barrier, len(greeted) + half - 1 + half * (place.pair // half))

    @pl.when(place.pair >= half)
    def _():
        pl.semaphore_signal(greeting, 1, device_id=place.mirror(), device_id_type=MESH)


    hands = []
    for slot, (kept, handed) in enumerate(
        ((source_ids, handed_source), (target_ids, handed_target))
    ):
        copy = pltpu.make_async_remote_copy(
            src_ref=kept.at[0],
            dst_ref=handed,
            send_sem=hand_sems.at[0, slot],
            recv_sem=hand_sems.at[1, slot],
            device_id=place.next_epoch(),
            device_id_type=MESH,
        )
        copy.start()
        hands.append(copy)
    sums = [
        TrainerSum(
            place,
            gradient,
            rounded.at[batch],
            near_in.at[batch],
            far_in.at[batch],
            half_sums.at[batch],
            (total, last_total)[batch],
            sum_sems.at[batch],
        )
        for batch in range(2)
    ]
    sums[0].scatter()
    for hand in hands:
        hand.wait_recv()
    for load in loads[8:]:
        load.wait()
    handed_rows = jnp.concatenate(
        [handed_source[...], handed_target[...], handed_source[...], handed_target[...]], axis=0
    ).astype(f32)
    handed_columns = handed_rows.T
    nodes = memory.shape[0]
    source = matmul(column_picks(handed_columns[:, 0:1], nodes), memory[...]).astype(bf16)
    target = matmul(column_picks(handed_columns[:, 2:3], nodes), memory[...]).astype(bf16)
    fresh = fresh_rows(source, target, gru_input, gru_state)
    sums[0].exchange()

    handed_memory[...] = replaced(memory, handed_rows[2:3, :], fresh)
    gather_events(
        handed_memory, second_columns, table, count, picks, stacked, target_rows, lambda: None
    )
    sums[0].bridge(greeting)
    sums[0].gather()
    sums[0].arrive()

    master[...] = stepped(master[...], total[...], step_scale(total))
    link_gradient(
        stacked, master[...].astype(bf16), logits_out, 2, deltas, gradient, rounded.at[1]
    )
    sums[1].scatter()
    events = target_rows.shape[0]
    fresh = fresh_rows(stacked[0:events, :], target_rows[...], gru_input, gru_state)
    sums[1].exchange()
    memory_out[...] = replaced(handed_memory, ids[3:4, :], fresh)
    sums[1].bridge(None)
    sums[1].gather()
    sums[1].arrive()
    for hand in hands:
        hand.wait_send()
    for each in sums:
        each.close()


def results_kernel(memory, master, total, logits, memory_out, decoder_out, logits_out, decoder, sems):
    stores = [
        pltpu.make_async_copy(memory, memory_out.at[0], sems.at[0]),
        pltpu.make_async_copy(logits, logits_out.at[0], sems.at[1]),
    ]
    for store in stores:
        store.start()
    scale = step_scale(total)
    parts = decoder.shape[0] // 128
    for part in range(parts):
        rows = slice(128 * part, 128 * (part + 1))
        decoder[rows, :] = stepped(master[:, rows], total[:, rows], scale).T
        stores.append(
            pltpu.make_async_copy(
                decoder.at[rows], decoder_out.at[0, rows], sems.at[2 + part]
            )
        )
        stores[-1].start()
    for store in stores:
        store.wait()


def on_device(*given):
    node_memory, neighbour_ids, neighbour_ticks, source_ids, target_ids, negative_ids = given[:6]
    event_ticks, gru_input, gru_state, decoder_weight = given[6:]
    nodes, width = node_memory.shape
    hidden = decoder_weight.shape[1]
    batches, events = source_ids.shape[1:]
    vmem, dma = pltpu.VMEM, pltpu.SemaphoreType.DMA
    held = pl.BlockSpec(memory_space=vmem)
    kept = pl.pallas_call(
        window_kernel,
        out_shape=(
            vmem((nodes, width), bf16),
            vmem((hidden, width), f32),
            vmem((hidden, width), bf16),
            vmem((2 * batches, events), f32),
        ),
        in_specs=[pl.BlockSpec(memory_space=pltpu.HBM)] * 10,
        out_specs=(held,) * 4,
        scratch_shapes=[
            vmem(node_memory.shape, bf16),
            vmem(neighbour_ids.shape, jnp.int32),
            vmem(neighbour_ticks.shape, jnp.int32),
            vmem(source_ids.shape, jnp.int32),
            vmem(target_ids.shape, jnp.int32),
            vmem(negative_ids.shape, jnp.int32),
            vmem(event_ticks.shape, jnp.int32),
            vmem(gru_input.shape, bf16),
            vmem(gru_state.shape, bf16),
            vmem(decoder_weight.shape, bf16),
            vmem((batches, events), jnp.int32),
            vmem((batches, events), jnp.int32),
            vmem((nodes, width), bf16),
            vmem((64, nodes), bf16),
            vmem((3 * events, nodes), bf16),
            vmem((3 * events, width), bf16),
            vmem((events, width), bf16),
            vmem((hidden, 3 * events), bf16),
            vmem((hidden, width), f32),
            vmem((batches, hidden, width), bf16),
            vmem((batches, near_count - 1, hidden // near_count, width), bf16),
            vmem((batches, far_count, hidden // near_count, width), bf16),
            vmem((batches, hidden // near_count, width), bf16),
            vmem((hidden, width), bf16),
            dma((10,)),
            dma((2, 2)),
            dma((batches, 2, 5)),
            pltpu.SemaphoreType.REGULAR,
        ],
        compiler_params=pltpu.CompilerParams(
            collective_id=0, has_side_effects=True, vmem_limit_bytes=50 * 2**20
        ),
        name="window",
    )(*(pltpu.with_memory_space_constraint(each, pltpu.HBM) for each in given))
    stored = pl.BlockSpec(memory_space=pltpu.HBM)
    return pl.pallas_call(
        results_kernel,
        out_shape=(
            jax.ShapeDtypeStruct((1, nodes, width), bf16),
            jax.ShapeDtypeStruct((1, width, hidden), f32),
            jax.ShapeDtypeStruct((1, 2 * batches, events), f32),
        ),
        in_specs=[held] * 4,
        out_specs=(stored,) * 3,
        scratch_shapes=[vmem((width, hidden), f32), dma((2 + width // 128,))],
        compiler_params=pltpu.CompilerParams(vmem_limit_bytes=8 * 2**20),
        name="results",
    )(*(pltpu.with_memory_space_constraint(each, pltpu.VMEM) for each in kept))


def solution(mesh):
    in_specs = (
        P(("batch", "mem"), None),
        P(None, ("batch", "mem")),
        P(None, ("batch", "mem")),
        P("epoch", None, ("batch", "mem")),
        P("epoch", None, ("batch", "mem")),
        P("epoch", None, ("batch", "mem")),
        P("epoch", None, ("batch", "mem")),
        P(),
        P(),
        P(),
    )
    out_specs = (
        P("epoch", ("batch", "mem"), None),
        P("epoch", None, None),
        P("epoch", None, ("batch", "mem")),
    )
    return jax.shard_map(
        on_device, mesh=mesh, in_specs=in_specs, out_specs=out_specs, check_vma=False
    )
```

```python
import jax
import jax.numpy as jnp
from jax import lax
from jax.experimental import pallas as pl
from jax.experimental.pallas import tpu as pltpu
from jax.sharding import PartitionSpec as P

MESH = pl.DeviceIdType.MESH
bf16, f32 = jnp.bfloat16, jnp.float32
tick_scale = 100.0
step_length = 4.0
epsilon = 1e-06
near_count, far_count = 16, 8
half = far_count // 2
near_out, early_out, late_out, bridge_out, back_out = range(5)


def matmul(a, b):
    return jnp.dot(a, b, preferred_element_type=f32)


def matmul_nt(a, b):
    return lax.dot_general(a, b, (((1,), (1,)), ((), ())), preferred_element_type=f32)


def device_at(y, z, core):
    return {"batch": y * 8 + z % 8, "mem": (z // 8) * 2 + core}


class Place:
    def __init__(self):
        self.epoch = lax.axis_index("epoch")
        batch, mem = lax.axis_index("batch"), lax.axis_index("mem")
        self.y, self.core = batch // 8, mem % 2
        z = (mem // 2) * 8 + batch % 8
        self.pair, self.side = z // 2, z % 2
        self.piece = (self.y * 2 + self.core) * 2 + self.side

    def near(self, step):
        y, core = (self.y + step // 4) % 4, (self.core + (step // 2) % 2) % 2
        side = (self.side + step % 2) % 2
        return device_at(y, self.pair * 2 + side, core), (y * 2 + core) * 2 + side

    def far_pair(self, step):
        return (self.pair + step + far_count) % far_count

    def at_pair(self, pair):
        return device_at(self.y, pair * 2 + self.side, self.core)

    def far(self, step):
        return self.at_pair(self.far_pair(step))

    def mirror(self):
        return self.at_pair(far_count - 1 - self.pair)

    def next_epoch(self):
        return {"epoch": (self.epoch + 1) % 4}

    def last_epoch(self):
        return {"epoch": (self.epoch + 3) % 4}


near_steps = sorted(range(1, near_count), key=lambda k: -(min(k // 4, 4 - k // 4) + k % 2))
far_steps = (4, 3, 5, 2, 6, 1, 7)


class TrainerSum:
    def __init__(self, place, gradient, rounded, near_in, far_in, half_sum, total, sems):
        self.place, self.gradient, self.rounded = place, gradient, rounded
        self.near_in, self.far_in, self.half_sum = near_in, far_in, half_sum
        self.total, self.sems = total, sems
        self.own = pl.ds(pl.multiple_of(place.piece * 16, 16), 16)

    def copy_of(self, src, dst, stage, device):
        return pltpu.make_async_remote_copy(
            src_ref=src,
            dst_ref=dst,
            send_sem=self.sems.at[0, stage],
            recv_sem=self.sems.at[1, stage],
            device_id=device,
            device_id_type=MESH,
        )

    def all_of(self, rows, stage):
        return self.copy_of(rows, rows, stage, self.place.mirror())

    def scatter(self):
        for step in near_steps:
            device, piece = self.place.near(step)
            rows = pl.ds(pl.multiple_of(piece * 16, 16), 16)
            self.copy_of(self.rounded.at[rows], self.near_in.at[step - 1], near_out, device).start()

    def exchange(self, first_pair_first):
        self.all_of(self.near_in, near_out).wait_recv()
        value = self.gradient[self.own, :]
        for slot in range(near_count - 1):
            value = value + self.near_in[slot].astype(f32)
        place = self.place
        self.far_in[place.pair] = value.astype(bf16)
        slot = self.far_in.at[place.pair]
        if first_pair_first:
            targets = [(pair, place.at_pair(pair)) for pair in range(far_count)]
        else:
            targets = [(place.far_pair(step), place.far(step)) for step in far_steps]
        for pair, device in targets:

            @pl.when((place.pair >= half) & (place.pair != pair))
            def _(device=device):
                self.copy_of(slot, slot, late_out, device).start()

            @pl.when((place.pair < half) & (place.pair != pair) & (pair < half))
            def _(device=device):
                self.copy_of(slot, slot, early_out, device).start()

    def bridge_copy(self):
        return self.copy_of(self.half_sum, self.half_sum, bridge_out, self.place.mirror())

    def bridge(self, greeting):
        @pl.when(self.place.pair < half)
        def _():
            self.all_of(self.far_in.at[: half - 1], early_out).wait_recv()
            value = self.far_in[0].astype(f32)
            for slot in range(1, half):
                value = value + self.far_in[slot].astype(f32)
            self.half_sum[...] = value.astype(bf16)
            if greeting is not None:
                pl.semaphore_wait(greeting, 1)
            self.bridge_copy().start()

    def gather(self):
        @pl.when(self.place.pair < half)
        def _():
            self.all_of(self.far_in.at[:half], late_out).wait_recv()

        @pl.when(self.place.pair >= half)
        def _():
            self.all_of(self.far_in.at[: half - 1], late_out).wait_recv()
            self.bridge_copy().wait_recv()

        value = self.half_sum[...].astype(f32)
        for slot in range(half, far_count):
            value = value + self.far_in[slot].astype(f32)
        self.total[self.own, :] = value.astype(bf16)
        rows = self.total.at[self.own]
        for step in near_steps:
            self.copy_of(rows, rows, back_out, self.place.near(step)[0]).start()

    def arrive(self):
        self.all_of(self.near_in, back_out).wait_recv()

    def close(self):
        self.all_of(self.near_in, near_out).wait_send()
        self.all_of(self.near_in, back_out).wait_send()

        @pl.when(self.place.pair < half)
        def _():
            self.all_of(self.far_in.at[: half - 1], early_out).wait_send()
            self.bridge_copy().wait_send()

        @pl.when(self.place.pair >= half)
        def _():
            self.all_of(self.far_in.at[: far_count - 1], late_out).wait_send()


def column_picks(column, count):
    lanes = lax.broadcasted_iota(jnp.int32, (column.shape[0], count), 1).astype(f32)
    return jnp.where(column == lanes, 1.0, 0.0).astype(bf16)


def row_picks(row, count):
    names = lax.broadcasted_iota(jnp.int32, (count, row.shape[1]), 0).astype(f32)
    return jnp.where(row == names, 1.0, 0.0)


def fill_table(table, near_ids, near_times):
    table[...] = jnp.zeros_like(table)
    count = near_ids.shape[0]
    for part, value in enumerate((near_ids, near_ids, near_times, near_times)):
        value = value[...] >> 8 if part % 2 else value[...] & 255
        table[16 * part : 16 * part + count, :] = value.astype(f32).astype(bf16)


def neighbour_weights(found, count, ticks, nodes):
    ids = found[:, 0:count] + 256.0 * found[:, 16 : 16 + count]
    times = found[:, 32 : 32 + count] + 256.0 * found[:, 48 : 48 + count]
    decay = tick_scale / (tick_scale + (ticks - times))
    decay = decay / jnp.sum(decay, axis=1, keepdims=True)
    events = found.shape[0]
    lanes = lax.broadcasted_iota(jnp.int32, (events, nodes), 1).astype(f32)
    weights = jnp.zeros((events, nodes), f32)
    for slot in range(count):
        chosen = ids[:, slot : slot + 1] == lanes
        weights = weights + jnp.where(chosen, decay[:, slot : slot + 1], 0.0)
    return weights


def gather_events(memory, columns, table, count, picks, stacked, target_rows, ready):
    source, target, negative, ticks = columns
    events, nodes = source.shape[0], memory.shape[0]
    target_picks = column_picks(target, nodes)
    found = matmul_nt(target_picks, table[...])
    picks[2 * events :, :] = target_picks
    picks[0:events, :] = column_picks(source, nodes)
    picks[events : 2 * events, :] = column_picks(negative, nodes)
    ready()
    rows = matmul(picks[...], memory[...])
    weights = neighbour_weights(found, count, ticks, nodes).astype(bf16)
    stacked[0:events, :] = rows[0:events].astype(bf16)
    stacked[2 * events :, :] = rows[events : 2 * events].astype(bf16)
    rows = rows[2 * events :]
    target_rows[...] = rows.astype(bf16)
    aggregate = matmul(weights, memory[...])
    stacked[events : 2 * events, :] = (0.5 * (rows + aggregate)).astype(bf16)


def link_gradient(stacked, projection, logits, row, deltas, gradient, rounded):
    events = stacked.shape[0] // 3
    scale = 1.0 / projection.shape[0] ** 0.5
    projected = matmul_nt(projection, stacked[...])
    source = projected[:, :events]
    target = projected[:, events : 2 * events]
    negative = projected[:, 2 * events :]
    positive = jnp.sum(source * target, axis=0, keepdims=True) * scale
    negative_logit = jnp.sum(source * negative, axis=0, keepdims=True) * scale
    logits[row : row + 1, :] = positive
    logits[row + 1 : row + 2, :] = negative_logit
    grad_positive = -jax.nn.sigmoid(-positive) * scale
    grad_negative = jax.nn.sigmoid(negative_logit) * scale
    deltas[:, :events] = (grad_positive * target + grad_negative * negative).astype(bf16)
    deltas[:, events : 2 * events] = (grad_positive * source).astype(bf16)
    deltas[:, 2 * events :] = (grad_negative * source).astype(bf16)
    value = matmul(deltas[...], stacked[...])
    gradient[...] = value
    rounded[...] = value.astype(bf16)


def fresh_rows(source_rows, target_rows, gru_input, gru_state):
    width = source_rows.shape[1]

    def gate(weights, rows, part):
        return matmul(rows, weights[:, part * width : (part + 1) * width])

    reset = jax.nn.sigmoid(gate(gru_input, source_rows, 0) + gate(gru_state, target_rows, 0))
    candidate = jnp.tanh(
        gate(gru_input, source_rows, 2) + reset * gate(gru_state, target_rows, 2)
    )
    update = jax.nn.sigmoid(gate(gru_input, source_rows, 1) + gate(gru_state, target_rows, 1))
    return ((1.0 - update) * candidate + update * target_rows.astype(f32)).astype(bf16)


def replaced(memory, target_row, fresh):
    picks = row_picks(target_row, memory.shape[0])
    hit = jnp.sum(picks, axis=1, keepdims=True)
    placed = matmul(picks.astype(bf16), fresh)
    return jnp.where(hit > 0.5, placed, memory[...].astype(f32)).astype(bf16)


def step_scale(total):
    total = total[...].astype(f32)
    return step_length / jnp.sqrt(jnp.sum(total * total) + epsilon)


def stepped(master, total, scale):
    return master - scale * total.astype(f32)


def window_kernel(
    memory_hbm,
    near_ids_hbm,
    near_times_hbm,
    source_ids_hbm,
    target_ids_hbm,
    negative_ids_hbm,
    event_ticks_hbm,
    gru_input_hbm,
    gru_state_hbm,
    decoder_hbm,
    memory_out,
    master,
    last_total,
    logits_out,
    memory,
    near_ids,
    near_times,
    source_ids,
    target_ids,
    negative_ids,
    event_ticks,
    gru_input,
    gru_state,
    decoder,
    handed_source,
    handed_target,
    handed_memory,
    table,
    picks,
    stacked,
    target_rows,
    deltas,
    gradient,
    rounded,
    near_in,
    far_in,
    half_sums,
    total,
    load_sems,
    hand_sems,
    sum_sems,
    greeting,
):
    place = Place()
    barrier = pltpu.get_barrier_semaphore()
    greeted = [place.near(step)[0] for step in near_steps]
    greeted += [place.next_epoch(), place.last_epoch()]
    loads = [
        pltpu.make_async_copy(stored, held, load_sems.at[slot])
        for slot, (stored, held) in enumerate(
            (
                (source_ids_hbm, source_ids),
                (target_ids_hbm, target_ids),
                (negative_ids_hbm, negative_ids),
                (event_ticks_hbm, event_ticks),
                (near_ids_hbm, near_ids),
                (near_times_hbm, near_times),
                (memory_hbm, memory),
                (decoder_hbm, decoder),
                (gru_input_hbm, gru_input),
                (gru_state_hbm, gru_state),
            )
        )
    ]
    for load in loads[:8]:
        load.start()
    for step in far_steps:

        @pl.when((place.pair < half) | (place.far_pair(step) >= half))
        def _(step=step):
            pl.semaphore_signal(barrier, 1, device_id=place.far(step), device_id_type=MESH)

    for device in greeted:
        pl.semaphore_signal(barrier, 1, device_id=device, device_id_type=MESH)
    for load in loads[:6]:
        load.wait()

    ids = jnp.concatenate(
        [source_ids[0], target_ids[0], negative_ids[0], event_ticks[0]], axis=0
    ).astype(f32)
    columns = ids.T
    first_columns = [columns[:, 2 * kind : 2 * kind + 1] for kind in range(4)]
    second_columns = [columns[:, 2 * kind + 1 : 2 * kind + 2] for kind in range(4)]
    fill_table(table, near_ids, near_times)
    count = near_ids.shape[0]

    def loaded():
        for load in loads[6:8]:
            load.wait()
        for load in loads[8:]:
            load.start()
        master[...] = decoder[...].astype(f32).T

    gather_events(memory, first_columns, table, count, picks, stacked, target_rows, loaded)
    link_gradient(
        stacked, master[...].astype(bf16), logits_out, 0, deltas, gradient, rounded.at[0]
    )
    pl.semaphore_wait(barrier, len(greeted) + half - 1 + half * (place.pair // half))

    @pl.when(place.pair >= half)
    def _():
        pl.semaphore_signal(greeting, 1, device_id=place.mirror(), device_id_type=MESH)


    hands = []
    for slot, (kept, handed) in enumerate(
        ((source_ids, handed_source), (target_ids, handed_target))
    ):
        copy = pltpu.make_async_remote_copy(
            src_ref=kept.at[0],
            dst_ref=handed,
            send_sem=hand_sems.at[0, slot],
            recv_sem=hand_sems.at[1, slot],
            device_id=place.next_epoch(),
            device_id_type=MESH,
        )
        copy.start()
        hands.append(copy)
    sums = [
        TrainerSum(
            place,
            gradient,
            rounded.at[batch],
            near_in.at[batch],
            far_in.at[batch],
            half_sums.at[batch],
            (total, last_total)[batch],
            sum_sems.at[batch],
        )
        for batch in range(2)
    ]
    sums[0].scatter()
    for hand in hands:
        hand.wait_recv()
    for load in loads[8:]:
        load.wait()
    handed_rows = jnp.concatenate(
        [handed_source[...], handed_target[...], handed_source[...], handed_target[...]], axis=0
    ).astype(f32)
    handed_columns = handed_rows.T
    nodes = memory.shape[0]
    source = matmul(column_picks(handed_columns[:, 0:1], nodes), memory[...]).astype(bf16)
    target = matmul(column_picks(handed_columns[:, 2:3], nodes), memory[...]).astype(bf16)
    fresh = fresh_rows(source, target, gru_input, gru_state)
    sums[0].exchange(False)

    handed_memory[...] = replaced(memory, handed_rows[2:3, :], fresh)
    gather_events(
        handed_memory, second_columns, table, count, picks, stacked, target_rows, lambda: None
    )
    sums[0].bridge(greeting)
    sums[0].gather()
    sums[0].arrive()

    master[...] = stepped(master[...], total[...], step_scale(total))
    link_gradient(
        stacked, master[...].astype(bf16), logits_out, 2, deltas, gradient, rounded.at[1]
    )
    sums[1].scatter()
    events = target_rows.shape[0]
    fresh = fresh_rows(stacked[0:events, :], target_rows[...], gru_input, gru_state)
    sums[1].exchange(True)
    sums[0].close()
    for hand in hands:
        hand.wait_send()
    memory_out[...] = replaced(handed_memory, ids[3:4, :], fresh)
    sums[1].bridge(None)
    sums[1].gather()
    sums[1].close()
    sums[1].arrive()


def results_kernel(memory, master, total, logits, memory_out, decoder_out, logits_out, decoder, sems):
    stores = [
        pltpu.make_async_copy(memory, memory_out.at[0], sems.at[0]),
        pltpu.make_async_copy(logits, logits_out.at[0], sems.at[1]),
    ]
    for store in stores:
        store.start()
    scale = step_scale(total)
    parts = decoder.shape[0] // 128
    for part in range(parts):
        rows = slice(128 * part, 128 * (part + 1))
        decoder[rows, :] = stepped(master[:, rows], total[:, rows], scale).T
        stores.append(
            pltpu.make_async_copy(
                decoder.at[rows], decoder_out.at[0, rows], sems.at[2 + part]
            )
        )
        stores[-1].start()
    for store in stores:
        store.wait()


def on_device(*given):
    node_memory, neighbour_ids, neighbour_ticks, source_ids, target_ids, negative_ids = given[:6]
    event_ticks, gru_input, gru_state, decoder_weight = given[6:]
    nodes, width = node_memory.shape
    hidden = decoder_weight.shape[1]
    batches, events = source_ids.shape[1:]
    vmem, dma = pltpu.VMEM, pltpu.SemaphoreType.DMA
    held = pl.BlockSpec(memory_space=vmem)
    kept = pl.pallas_call(
        window_kernel,
        out_shape=(
            vmem((nodes, width), bf16),
            vmem((hidden, width), f32),
            vmem((hidden, width), bf16),
            vmem((2 * batches, events), f32),
        ),
        in_specs=[pl.BlockSpec(memory_space=pltpu.HBM)] * 10,
        out_specs=(held,) * 4,
        scratch_shapes=[
            vmem(node_memory.shape, bf16),
            vmem(neighbour_ids.shape, jnp.int32),
            vmem(neighbour_ticks.shape, jnp.int32),
            vmem(source_ids.shape, jnp.int32),
            vmem(target_ids.shape, jnp.int32),
            vmem(negative_ids.shape, jnp.int32),
            vmem(event_ticks.shape, jnp.int32),
            vmem(gru_input.shape, bf16),
            vmem(gru_state.shape, bf16),
            vmem(decoder_weight.shape, bf16),
            vmem((batches, events), jnp.int32),
            vmem((batches, events), jnp.int32),
            vmem((nodes, width), bf16),
            vmem((64, nodes), bf16),
            vmem((3 * events, nodes), bf16),
            vmem((3 * events, width), bf16),
            vmem((events, width), bf16),
            vmem((hidden, 3 * events), bf16),
            vmem((hidden, width), f32),
            vmem((batches, hidden, width), bf16),
            vmem((batches, near_count - 1, hidden // near_count, width), bf16),
            vmem((batches, far_count, hidden // near_count, width), bf16),
            vmem((batches, hidden // near_count, width), bf16),
            vmem((hidden, width), bf16),
            dma((10,)),
            dma((2, 2)),
            dma((batches, 2, 5)),
            pltpu.SemaphoreType.REGULAR,
        ],
        compiler_params=pltpu.CompilerParams(
            collective_id=0, has_side_effects=True, vmem_limit_bytes=50 * 2**20
        ),
        name="window",
    )(*(pltpu.with_memory_space_constraint(each, pltpu.HBM) for each in given))
    stored = pl.BlockSpec(memory_space=pltpu.HBM)
    return pl.pallas_call(
        results_kernel,
        out_shape=(
            jax.ShapeDtypeStruct((1, nodes, width), bf16),
            jax.ShapeDtypeStruct((1, width, hidden), f32),
            jax.ShapeDtypeStruct((1, 2 * batches, events), f32),
        ),
        in_specs=[held] * 4,
        out_specs=(stored,) * 3,
        scratch_shapes=[vmem((width, hidden), f32), dma((2 + width // 128,))],
        compiler_params=pltpu.CompilerParams(vmem_limit_bytes=8 * 2**20),
        name="results",
    )(*(pltpu.with_memory_space_constraint(each, pltpu.VMEM) for each in kept))


def solution(mesh):
    in_specs = (
        P(("batch", "mem"), None),
        P(None, ("batch", "mem")),
        P(None, ("batch", "mem")),
        P("epoch", None, ("batch", "mem")),
        P("epoch", None, ("batch", "mem")),
        P("epoch", None, ("batch", "mem")),
        P("epoch", None, ("batch", "mem")),
        P(),
        P(),
        P(),
    )
    out_specs = (
        P("epoch", ("batch", "mem"), None),
        P("epoch", None, None),
        P("epoch", None, ("batch", "mem")),
    )
    return jax.shard_map(
        on_device, mesh=mesh, in_specs=in_specs, out_specs=out_specs, check_vma=False
    )
```

```python
import jax
import jax.numpy as jnp
from jax import lax
from jax.experimental import pallas as pl
from jax.experimental.pallas import tpu as pltpu
from jax.sharding import PartitionSpec as P

MESH = pl.DeviceIdType.MESH
bf16, f32 = jnp.bfloat16, jnp.float32
tick_scale = 100.0
step_length = 4.0
epsilon = 1e-06
near_count, far_count = 16, 8
half = far_count // 2
near_out, early_out, late_out, bridge_out, back_out, relay_out = range(6)
relayed = (4, 12, 5, 13)
back_count = near_count - 1 - len(relayed)


def matmul(a, b):
    return jnp.dot(a, b, preferred_element_type=f32)


def matmul_nt(a, b):
    return lax.dot_general(a, b, (((1,), (1,)), ((), ())), preferred_element_type=f32)


def device_at(y, z, core):
    return {"batch": y * 8 + z % 8, "mem": (z // 8) * 2 + core}


class Place:
    def __init__(self):
        self.epoch = lax.axis_index("epoch")
        batch, mem = lax.axis_index("batch"), lax.axis_index("mem")
        self.y, self.core = batch // 8, mem % 2
        z = (mem // 2) * 8 + batch % 8
        self.pair, self.side = z // 2, z % 2
        self.piece = (self.y * 2 + self.core) * 2 + self.side

    def near(self, step):
        y, core = (self.y + step // 4) % 4, (self.core + (step // 2) % 2) % 2
        side = (self.side + step % 2) % 2
        return device_at(y, self.pair * 2 + side, core), (y * 2 + core) * 2 + side

    def far_pair(self, step):
        return (self.pair + step + far_count) % far_count

    def at_pair(self, pair):
        return device_at(self.y, pair * 2 + self.side, self.core)

    def far(self, step):
        return self.at_pair(self.far_pair(step))

    def mirror(self):
        return self.at_pair(far_count - 1 - self.pair)

    def next_epoch(self):
        return {"epoch": (self.epoch + 1) % 4}

    def last_epoch(self):
        return {"epoch": (self.epoch + 3) % 4}


near_steps = sorted(range(1, near_count), key=lambda k: -(min(k // 4, 4 - k // 4) + k % 2))
far_steps = (4, 3, 5, 2, 6, 1, 7)


class TrainerSum:
    def __init__(self, place, gradient, rounded, near_in, far_in, half_sum, total, sems):
        self.place, self.gradient, self.rounded = place, gradient, rounded
        self.near_in, self.far_in, self.half_sum = near_in, far_in, half_sum
        self.total, self.sems = total, sems
        self.own = pl.ds(pl.multiple_of(place.piece * 16, 16), 16)

    def copy_of(self, src, dst, stage, device):
        return pltpu.make_async_remote_copy(
            src_ref=src,
            dst_ref=dst,
            send_sem=self.sems.at[0, stage],
            recv_sem=self.sems.at[1, stage],
            device_id=device,
            device_id_type=MESH,
        )

    def all_of(self, rows, stage):
        return self.copy_of(rows, rows, stage, self.place.mirror())

    def scatter(self):
        for step in near_steps:
            device, piece = self.place.near(step)
            rows = pl.ds(pl.multiple_of(piece * 16, 16), 16)
            self.copy_of(self.rounded.at[rows], self.near_in.at[step - 1], near_out, device).start()

    def exchange(self):
        self.all_of(self.near_in, near_out).wait_recv()
        value = self.gradient[self.own, :]
        for slot in range(near_count - 1):
            value = value + self.near_in[slot].astype(f32)
        place = self.place
        self.far_in[place.pair] = value.astype(bf16)
        slot = self.far_in.at[place.pair]
        for step in far_steps:

            @pl.when(place.pair >= half)
            def _(step=step):
                self.copy_of(slot, slot, late_out, place.far(step)).start()

            @pl.when((place.pair < half) & (place.far_pair(step) < half))
            def _(step=step):
                self.copy_of(slot, slot, early_out, place.far(step)).start()

    def bridge_copy(self):
        return self.copy_of(self.half_sum, self.half_sum, bridge_out, self.place.mirror())

    def bridge(self, greeting):
        @pl.when(self.place.pair < half)
        def _():
            self.all_of(self.far_in.at[: half - 1], early_out).wait_recv()
            value = self.far_in[0].astype(f32)
            for slot in range(1, half):
                value = value + self.far_in[slot].astype(f32)
            self.half_sum[...] = value.astype(bf16)
            if greeting is not None:
                pl.semaphore_wait(greeting, 1)
            self.bridge_copy().start()

    def gather(self):
        @pl.when(self.place.pair < half)
        def _():
            self.all_of(self.far_in.at[:half], late_out).wait_recv()

        @pl.when(self.place.pair >= half)
        def _():
            self.all_of(self.far_in.at[: half - 1], late_out).wait_recv()
            self.bridge_copy().wait_recv()

        value = self.half_sum[...].astype(f32)
        for slot in range(half, far_count):
            value = value + self.far_in[slot].astype(f32)
        self.total[self.own, :] = value.astype(bf16)
        rows = self.total.at[self.own]
        for step in near_steps:
            if step in relayed:
                stage = relay_out + relayed.index(step)
                self.copy_of(rows, rows, stage, self.place.near(step)[0]).start()
            elif step // 4 % 2 == 0:
                self.copy_of(rows, rows, back_out, self.place.near(step)[0]).start()

    def relay(self):
        place = self.place
        other = place.near(2)[0]
        for slot, step in enumerate(relayed):
            y, side = (place.y - step // 4 + 4) % 4, (place.side + step) % 2
            start = pl.multiple_of(((y * 2 + place.core) * 2 + side) * 16, 16)
            rows = self.total.at[pl.ds(start, 16)]
            self.copy_of(rows, rows, relay_out + slot, other).wait_recv()
            self.copy_of(rows, rows, back_out, other).start()

    def arrive(self):
        self.all_of(self.near_in.at[:back_count], back_out).wait_recv()

    def close(self):
        self.all_of(self.near_in, near_out).wait_send()
        self.all_of(self.near_in.at[:back_count], back_out).wait_send()
        for slot in range(len(relayed)):
            self.all_of(self.near_in.at[0], relay_out + slot).wait_send()

        @pl.when(self.place.pair < half)
        def _():
            self.all_of(self.far_in.at[: half - 1], early_out).wait_send()
            self.bridge_copy().wait_send()

        @pl.when(self.place.pair >= half)
        def _():
            self.all_of(self.far_in.at[: far_count - 1], late_out).wait_send()


def column_picks(column, count):
    lanes = lax.broadcasted_iota(jnp.int32, (column.shape[0], count), 1).astype(f32)
    return jnp.where(column == lanes, 1.0, 0.0).astype(bf16)


def row_picks(row, count):
    names = lax.broadcasted_iota(jnp.int32, (count, row.shape[1]), 0).astype(f32)
    return jnp.where(row == names, 1.0, 0.0)


def fill_table(table, near_ids, near_times):
    table[...] = jnp.zeros_like(table)
    count = near_ids.shape[0]
    for part, value in enumerate((near_ids, near_ids, near_times, near_times)):
        value = value[...] >> 8 if part % 2 else value[...] & 255
        table[16 * part : 16 * part + count, :] = value.astype(f32).astype(bf16)


def neighbour_weights(found, count, ticks, nodes):
    ids = found[:, 0:count] + 256.0 * found[:, 16 : 16 + count]
    times = found[:, 32 : 32 + count] + 256.0 * found[:, 48 : 48 + count]
    decay = tick_scale / (tick_scale + (ticks - times))
    decay = decay / jnp.sum(decay, axis=1, keepdims=True)
    events = found.shape[0]
    lanes = lax.broadcasted_iota(jnp.int32, (events, nodes), 1).astype(f32)
    weights = jnp.zeros((events, nodes), f32)
    for slot in range(count):
        chosen = ids[:, slot : slot + 1] == lanes
        weights = weights + jnp.where(chosen, decay[:, slot : slot + 1], 0.0)
    return weights


def gather_events(memory, columns, table, count, picks, stacked, target_rows, ready):
    source, target, negative, ticks = columns
    events, nodes = source.shape[0], memory.shape[0]
    target_picks = column_picks(target, nodes)
    found = matmul_nt(target_picks, table[...])
    picks[2 * events :, :] = target_picks
    picks[0:events, :] = column_picks(source, nodes)
    picks[events : 2 * events, :] = column_picks(negative, nodes)
    ready()
    rows = matmul(picks[...], memory[...])
    weights = neighbour_weights(found, count, ticks, nodes).astype(bf16)
    stacked[0:events, :] = rows[0:events].astype(bf16)
    stacked[2 * events :, :] = rows[events : 2 * events].astype(bf16)
    rows = rows[2 * events :]
    target_rows[...] = rows.astype(bf16)
    aggregate = matmul(weights, memory[...])
    stacked[events : 2 * events, :] = (0.5 * (rows + aggregate)).astype(bf16)


def link_gradient(stacked, projection, logits, row, deltas, gradient, rounded):
    events = stacked.shape[0] // 3
    scale = 1.0 / projection.shape[0] ** 0.5
    projected = matmul_nt(projection, stacked[...])
    source = projected[:, :events]
    target = projected[:, events : 2 * events]
    negative = projected[:, 2 * events :]
    positive = jnp.sum(source * target, axis=0, keepdims=True) * scale
    negative_logit = jnp.sum(source * negative, axis=0, keepdims=True) * scale
    logits[row : row + 1, :] = positive
    logits[row + 1 : row + 2, :] = negative_logit
    grad_positive = -jax.nn.sigmoid(-positive) * scale
    grad_negative = jax.nn.sigmoid(negative_logit) * scale
    deltas[:, :events] = (grad_positive * target + grad_negative * negative).astype(bf16)
    deltas[:, events : 2 * events] = (grad_positive * source).astype(bf16)
    deltas[:, 2 * events :] = (grad_negative * source).astype(bf16)
    value = matmul(deltas[...], stacked[...])
    gradient[...] = value
    rounded[...] = value.astype(bf16)


def fresh_rows(source_rows, target_rows, gru_input, gru_state):
    width = source_rows.shape[1]

    def gate(weights, rows, part):
        return matmul(rows, weights[:, part * width : (part + 1) * width])

    reset = jax.nn.sigmoid(gate(gru_input, source_rows, 0) + gate(gru_state, target_rows, 0))
    candidate = jnp.tanh(
        gate(gru_input, source_rows, 2) + reset * gate(gru_state, target_rows, 2)
    )
    update = jax.nn.sigmoid(gate(gru_input, source_rows, 1) + gate(gru_state, target_rows, 1))
    return ((1.0 - update) * candidate + update * target_rows.astype(f32)).astype(bf16)


def replaced(memory, target_row, fresh):
    picks = row_picks(target_row, memory.shape[0])
    hit = jnp.sum(picks, axis=1, keepdims=True)
    placed = matmul(picks.astype(bf16), fresh)
    return jnp.where(hit > 0.5, placed, memory[...].astype(f32)).astype(bf16)


def step_scale(total):
    total = total[...].astype(f32)
    return step_length / jnp.sqrt(jnp.sum(total * total) + epsilon)


def stepped(master, total, scale):
    return master - scale * total.astype(f32)


def window_kernel(
    memory_hbm,
    near_ids_hbm,
    near_times_hbm,
    source_ids_hbm,
    target_ids_hbm,
    negative_ids_hbm,
    event_ticks_hbm,
    gru_input_hbm,
    gru_state_hbm,
    decoder_hbm,
    memory_out,
    master,
    last_total,
    logits_out,
    memory,
    near_ids,
    near_times,
    source_ids,
    target_ids,
    negative_ids,
    event_ticks,
    gru_input,
    gru_state,
    decoder,
    handed_source,
    handed_target,
    handed_memory,
    table,
    picks,
    stacked,
    target_rows,
    deltas,
    gradient,
    rounded,
    near_in,
    far_in,
    half_sums,
    total,
    load_sems,
    hand_sems,
    sum_sems,
    greeting,
):
    place = Place()
    barrier = pltpu.get_barrier_semaphore()
    greeted = [place.near(step)[0] for step in near_steps]
    greeted += [place.next_epoch(), place.last_epoch()]
    loads = [
        pltpu.make_async_copy(stored, held, load_sems.at[slot])
        for slot, (stored, held) in enumerate(
            (
                (source_ids_hbm, source_ids),
                (target_ids_hbm, target_ids),
                (negative_ids_hbm, negative_ids),
                (event_ticks_hbm, event_ticks),
                (near_ids_hbm, near_ids),
                (near_times_hbm, near_times),
                (memory_hbm, memory),
                (decoder_hbm, decoder),
                (gru_input_hbm, gru_input),
                (gru_state_hbm, gru_state),
            )
        )
    ]
    for load in loads[:8]:
        load.start()
    for step in far_steps:

        @pl.when((place.pair < half) | (place.far_pair(step) >= half))
        def _(step=step):
            pl.semaphore_signal(barrier, 1, device_id=place.far(step), device_id_type=MESH)

    for device in greeted:
        pl.semaphore_signal(barrier, 1, device_id=device, device_id_type=MESH)
    for load in loads[:6]:
        load.wait()

    ids = jnp.concatenate(
        [source_ids[0], target_ids[0], negative_ids[0], event_ticks[0]], axis=0
    ).astype(f32)
    columns = ids.T
    first_columns = [columns[:, 2 * kind : 2 * kind + 1] for kind in range(4)]
    second_columns = [columns[:, 2 * kind + 1 : 2 * kind + 2] for kind in range(4)]
    fill_table(table, near_ids, near_times)
    count = near_ids.shape[0]

    def loaded():
        for load in loads[6:8]:
            load.wait()
        for load in loads[8:]:
            load.start()
        master[...] = decoder[...].astype(f32).T

    gather_events(memory, first_columns, table, count, picks, stacked, target_rows, loaded)
    link_gradient(
        stacked, master[...].astype(bf16), logits_out, 0, deltas, gradient, rounded.at[0]
    )
    pl.semaphore_wait(barrier, len(greeted) + half - 1 + half * (place.pair // half))

    @pl.when(place.pair >= half)
    def _():
        pl.semaphore_signal(greeting, 1, device_id=place.mirror(), device_id_type=MESH)


    hands = []
    for slot, (kept, handed) in enumerate(
        ((source_ids, handed_source), (target_ids, handed_target))
    ):
        copy = pltpu.make_async_remote_copy(
            src_ref=kept.at[0],
            dst_ref=handed,
            send_sem=hand_sems.at[0, slot],
            recv_sem=hand_sems.at[1, slot],
            device_id=place.next_epoch(),
            device_id_type=MESH,
        )
        copy.start()
        hands.append(copy)
    sums = [
        TrainerSum(
            place,
            gradient,
            rounded.at[batch],
            near_in.at[batch],
            far_in.at[batch],
            half_sums.at[batch],
            (total, last_total)[batch],
            sum_sems.at[batch],
        )
        for batch in range(2)
    ]
    sums[0].scatter()
    for hand in hands:
        hand.wait_recv()
    for load in loads[8:]:
        load.wait()
    handed_rows = jnp.concatenate(
        [handed_source[...], handed_target[...], handed_source[...], handed_target[...]], axis=0
    ).astype(f32)
    handed_columns = handed_rows.T
    nodes = memory.shape[0]
    source = matmul(column_picks(handed_columns[:, 0:1], nodes), memory[...]).astype(bf16)
    target = matmul(column_picks(handed_columns[:, 2:3], nodes), memory[...]).astype(bf16)
    fresh = fresh_rows(source, target, gru_input, gru_state)
    sums[0].exchange()

    handed_memory[...] = replaced(memory, handed_rows[2:3, :], fresh)
    gather_events(
        handed_memory, second_columns, table, count, picks, stacked, target_rows, lambda: None
    )
    sums[0].bridge(greeting)
    sums[0].gather()
    sums[0].relay()
    sums[0].arrive()

    master[...] = stepped(master[...], total[...], step_scale(total))
    link_gradient(
        stacked, master[...].astype(bf16), logits_out, 2, deltas, gradient, rounded.at[1]
    )
    sums[1].scatter()
    events = target_rows.shape[0]
    fresh = fresh_rows(stacked[0:events, :], target_rows[...], gru_input, gru_state)
    sums[1].exchange()
    sums[0].close()
    for hand in hands:
        hand.wait_send()
    memory_out[...] = replaced(handed_memory, ids[3:4, :], fresh)
    sums[1].bridge(None)
    sums[1].gather()
    sums[1].relay()
    sums[1].close()
    sums[1].arrive()


def results_kernel(memory, master, total, logits, memory_out, decoder_out, logits_out, decoder, sems):
    stores = [
        pltpu.make_async_copy(memory, memory_out.at[0], sems.at[0]),
        pltpu.make_async_copy(logits, logits_out.at[0], sems.at[1]),
    ]
    for store in stores:
        store.start()
    scale = step_scale(total)
    parts = decoder.shape[0] // 128
    for part in range(parts):
        rows = slice(128 * part, 128 * (part + 1))
        decoder[rows, :] = stepped(master[:, rows], total[:, rows], scale).T
        stores.append(
            pltpu.make_async_copy(
                decoder.at[rows], decoder_out.at[0, rows], sems.at[2 + part]
            )
        )
        stores[-1].start()
    for store in stores:
        store.wait()


def on_device(*given):
    node_memory, neighbour_ids, neighbour_ticks, source_ids, target_ids, negative_ids = given[:6]
    event_ticks, gru_input, gru_state, decoder_weight = given[6:]
    nodes, width = node_memory.shape
    hidden = decoder_weight.shape[1]
    batches, events = source_ids.shape[1:]
    vmem, dma = pltpu.VMEM, pltpu.SemaphoreType.DMA
    held = pl.BlockSpec(memory_space=vmem)
    kept = pl.pallas_call(
        window_kernel,
        out_shape=(
            vmem((nodes, width), bf16),
            vmem((hidden, width), f32),
            vmem((hidden, width), bf16),
            vmem((2 * batches, events), f32),
        ),
        in_specs=[pl.BlockSpec(memory_space=pltpu.HBM)] * 10,
        out_specs=(held,) * 4,
        scratch_shapes=[
            vmem(node_memory.shape, bf16),
            vmem(neighbour_ids.shape, jnp.int32),
            vmem(neighbour_ticks.shape, jnp.int32),
            vmem(source_ids.shape, jnp.int32),
            vmem(target_ids.shape, jnp.int32),
            vmem(negative_ids.shape, jnp.int32),
            vmem(event_ticks.shape, jnp.int32),
            vmem(gru_input.shape, bf16),
            vmem(gru_state.shape, bf16),
            vmem(decoder_weight.shape, bf16),
            vmem((batches, events), jnp.int32),
            vmem((batches, events), jnp.int32),
            vmem((nodes, width), bf16),
            vmem((64, nodes), bf16),
            vmem((3 * events, nodes), bf16),
            vmem((3 * events, width), bf16),
            vmem((events, width), bf16),
            vmem((hidden, 3 * events), bf16),
            vmem((hidden, width), f32),
            vmem((batches, hidden, width), bf16),
            vmem((batches, near_count - 1, hidden // near_count, width), bf16),
            vmem((batches, far_count, hidden // near_count, width), bf16),
            vmem((batches, hidden // near_count, width), bf16),
            vmem((hidden, width), bf16),
            dma((10,)),
            dma((2, 2)),
            dma((batches, 2, relay_out + len(relayed))),
            pltpu.SemaphoreType.REGULAR,
        ],
        compiler_params=pltpu.CompilerParams(
            collective_id=0, has_side_effects=True, vmem_limit_bytes=50 * 2**20
        ),
        name="window",
    )(*(pltpu.with_memory_space_constraint(each, pltpu.HBM) for each in given))
    stored = pl.BlockSpec(memory_space=pltpu.HBM)
    return pl.pallas_call(
        results_kernel,
        out_shape=(
            jax.ShapeDtypeStruct((1, nodes, width), bf16),
            jax.ShapeDtypeStruct((1, width, hidden), f32),
            jax.ShapeDtypeStruct((1, 2 * batches, events), f32),
        ),
        in_specs=[held] * 4,
        out_specs=(stored,) * 3,
        scratch_shapes=[vmem((width, hidden), f32), dma((2 + width // 128,))],
        compiler_params=pltpu.CompilerParams(vmem_limit_bytes=8 * 2**20),
        name="results",
    )(*(pltpu.with_memory_space_constraint(each, pltpu.VMEM) for each in kept))


def solution(mesh):
    in_specs = (
        P(("batch", "mem"), None),
        P(None, ("batch", "mem")),
        P(None, ("batch", "mem")),
        P("epoch", None, ("batch", "mem")),
        P("epoch", None, ("batch", "mem")),
        P("epoch", None, ("batch", "mem")),
        P("epoch", None, ("batch", "mem")),
        P(),
        P(),
        P(),
    )
    out_specs = (
        P("epoch", ("batch", "mem"), None),
        P("epoch", None, None),
        P("epoch", None, ("batch", "mem")),
    )
    return jax.shard_map(
        on_device, mesh=mesh, in_specs=in_specs, out_specs=out_specs, check_vma=False
    )
```

```python
import jax
import jax.numpy as jnp
from jax import lax
from jax.experimental import pallas as pl
from jax.experimental.pallas import tpu as pltpu
from jax.sharding import PartitionSpec as P

MESH = pl.DeviceIdType.MESH
bf16, f32 = jnp.bfloat16, jnp.float32
tick_scale = 100.0
step_length = 4.0
epsilon = 1e-06
near_count, far_count = 16, 8
half = far_count // 2
near_out, early_out, late_out, bridge_out, back_out = range(5)


def matmul(a, b):
    return jnp.dot(a, b, preferred_element_type=f32)


def matmul_nt(a, b):
    return lax.dot_general(a, b, (((1,), (1,)), ((), ())), preferred_element_type=f32)


def device_at(y, z, core):
    return {"batch": y * 8 + z % 8, "mem": (z // 8) * 2 + core}


class Place:
    def __init__(self):
        self.epoch = lax.axis_index("epoch")
        batch, mem = lax.axis_index("batch"), lax.axis_index("mem")
        self.y, self.core = batch // 8, mem % 2
        z = (mem // 2) * 8 + batch % 8
        self.pair, self.side = z // 2, z % 2
        self.piece = (self.y * 2 + self.core) * 2 + self.side

    def near(self, step):
        y, core = (self.y + step // 4) % 4, (self.core + (step // 2) % 2) % 2
        side = (self.side + step % 2) % 2
        return device_at(y, self.pair * 2 + side, core), (y * 2 + core) * 2 + side

    def far_pair(self, step):
        return (self.pair + step + far_count) % far_count

    def far(self, step):
        return device_at(self.y, self.far_pair(step) * 2 + self.side, self.core)

    def mirror(self):
        return device_at(self.y, (far_count - 1 - self.pair) * 2 + self.side, self.core)

    def next_epoch(self):
        return {"epoch": (self.epoch + 1) % 4}

    def last_epoch(self):
        return {"epoch": (self.epoch + 3) % 4}


near_steps = sorted(range(1, near_count), key=lambda k: -(min(k // 4, 4 - k // 4) + k % 2))
far_steps = (4, 3, 5, 2, 6, 1, 7)


class TrainerSum:
    def __init__(self, place, gradient, rounded, near_in, far_in, half_sum, total, sems):
        self.place, self.gradient, self.rounded = place, gradient, rounded
        self.near_in, self.far_in, self.half_sum = near_in, far_in, half_sum
        self.total, self.sems = total, sems
        self.own = pl.ds(pl.multiple_of(place.piece * 16, 16), 16)

    def copy_of(self, src, dst, stage, device):
        return pltpu.make_async_remote_copy(
            src_ref=src,
            dst_ref=dst,
            send_sem=self.sems.at[0, stage],
            recv_sem=self.sems.at[1, stage],
            device_id=device,
            device_id_type=MESH,
        )

    def all_of(self, rows, stage):
        return self.copy_of(rows, rows, stage, self.place.mirror())

    def scatter(self):
        for step in near_steps:
            device, piece = self.place.near(step)
            rows = pl.ds(pl.multiple_of(piece * 16, 16), 16)
            self.copy_of(self.rounded.at[rows], self.near_in.at[step - 1], near_out, device).start()

    def exchange(self):
        self.all_of(self.near_in, near_out).wait_recv()
        value = self.gradient[self.own, :]
        for slot in range(near_count - 1):
            value = value + self.near_in[slot].astype(f32)
        place = self.place
        self.far_in[place.pair] = value.astype(bf16)
        slot = self.far_in.at[place.pair]
        for step in far_steps:

            @pl.when(place.pair >= half)
            def _(step=step):
                self.copy_of(slot, slot, late_out, place.far(step)).start()

            @pl.when((place.pair < half) & (place.far_pair(step) < half))
            def _(step=step):
                self.copy_of(slot, slot, early_out, place.far(step)).start()

    def bridge_copy(self):
        return self.copy_of(self.half_sum, self.half_sum, bridge_out, self.place.mirror())

    def bridge(self, greeting):
        @pl.when(self.place.pair < half)
        def _():
            self.all_of(self.far_in.at[: half - 1], early_out).wait_recv()
            value = self.far_in[0].astype(f32)
            for slot in range(1, half):
                value = value + self.far_in[slot].astype(f32)
            self.half_sum[...] = value.astype(bf16)
            if greeting is not None:
                pl.semaphore_wait(greeting, 1)
            self.bridge_copy().start()

    def gather(self):
        @pl.when(self.place.pair < half)
        def _():
            self.all_of(self.far_in.at[:half], late_out).wait_recv()

        @pl.when(self.place.pair >= half)
        def _():
            self.all_of(self.far_in.at[: half - 1], late_out).wait_recv()
            self.bridge_copy().wait_recv()

        value = self.half_sum[...].astype(f32)
        for slot in range(half, far_count):
            value = value + self.far_in[slot].astype(f32)
        self.total[self.own, :] = value.astype(bf16)
        rows = self.total.at[self.own]
        for step in near_steps:
            self.copy_of(rows, rows, back_out, self.place.near(step)[0]).start()

    def arrive(self):
        self.all_of(self.near_in, back_out).wait_recv()

    def close(self):
        self.all_of(self.near_in, near_out).wait_send()
        self.all_of(self.near_in, back_out).wait_send()

        @pl.when(self.place.pair < half)
        def _():
            self.all_of(self.far_in.at[: half - 1], early_out).wait_send()
            self.bridge_copy().wait_send()

        @pl.when(self.place.pair >= half)
        def _():
            self.all_of(self.far_in.at[: far_count - 1], late_out).wait_send()


def column_picks(column, count):
    lanes = lax.broadcasted_iota(jnp.int32, (column.shape[0], count), 1).astype(f32)
    return jnp.where(column == lanes, 1.0, 0.0).astype(bf16)


def row_picks(row, count):
    names = lax.broadcasted_iota(jnp.int32, (count, row.shape[1]), 0).astype(f32)
    return jnp.where(row == names, 1.0, 0.0)


def fill_table(table, near_ids, near_times):
    table[...] = jnp.zeros_like(table)
    count = near_ids.shape[0]
    for part, value in enumerate((near_ids, near_ids, near_times, near_times)):
        value = value[...] >> 8 if part % 2 else value[...] & 255
        table[16 * part : 16 * part + count, :] = value.astype(f32).astype(bf16)


def neighbour_weights(found, count, ticks, nodes):
    ids = found[:, 0:count] + 256.0 * found[:, 16 : 16 + count]
    times = found[:, 32 : 32 + count] + 256.0 * found[:, 48 : 48 + count]
    decay = tick_scale / (tick_scale + (ticks - times))
    decay = decay / jnp.sum(decay, axis=1, keepdims=True)
    events = found.shape[0]
    lanes = lax.broadcasted_iota(jnp.int32, (events, nodes), 1).astype(f32)
    weights = jnp.zeros((events, nodes), f32)
    for slot in range(count):
        chosen = ids[:, slot : slot + 1] == lanes
        weights = weights + jnp.where(chosen, decay[:, slot : slot + 1], 0.0)
    return weights


def gather_events(memory, columns, table, count, picks, stacked, target_rows, ready):
    source, target, negative, ticks = columns
    events, nodes = source.shape[0], memory.shape[0]
    target_picks = column_picks(target, nodes)
    found = matmul_nt(target_picks, table[...])
    picks[2 * events :, :] = target_picks
    picks[0:events, :] = column_picks(source, nodes)
    picks[events : 2 * events, :] = column_picks(negative, nodes)
    ready()
    rows = matmul(picks[...], memory[...])
    weights = neighbour_weights(found, count, ticks, nodes).astype(bf16)
    stacked[0:events, :] = rows[0:events].astype(bf16)
    stacked[2 * events :, :] = rows[events : 2 * events].astype(bf16)
    rows = rows[2 * events :]
    target_rows[...] = rows.astype(bf16)
    aggregate = matmul(weights, memory[...])
    stacked[events : 2 * events, :] = (0.5 * (rows + aggregate)).astype(bf16)


def link_gradient(stacked, projected, logits, row, deltas, gradient, rounded):
    events = stacked.shape[0] // 3
    scale = 1.0 / projected.shape[0] ** 0.5
    source = projected[:, :events]
    target = projected[:, events : 2 * events]
    negative = projected[:, 2 * events :]
    positive = jnp.sum(source * target, axis=0, keepdims=True) * scale
    negative_logit = jnp.sum(source * negative, axis=0, keepdims=True) * scale
    logits[row : row + 1, :] = positive
    logits[row + 1 : row + 2, :] = negative_logit
    grad_positive = -jax.nn.sigmoid(-positive) * scale
    grad_negative = jax.nn.sigmoid(negative_logit) * scale
    deltas[:, :events] = (grad_positive * target + grad_negative * negative).astype(bf16)
    deltas[:, events : 2 * events] = (grad_positive * source).astype(bf16)
    deltas[:, 2 * events :] = (grad_negative * source).astype(bf16)
    value = matmul(deltas[...], stacked[...])
    gradient[...] = value
    rounded[...] = value.astype(bf16)


def fresh_rows(source_rows, target_rows, gru_input, gru_state):
    width = source_rows.shape[1]

    def gate(weights, rows, part):
        return matmul(rows, weights[:, part * width : (part + 1) * width])

    reset = jax.nn.sigmoid(gate(gru_input, source_rows, 0) + gate(gru_state, target_rows, 0))
    candidate = jnp.tanh(
        gate(gru_input, source_rows, 2) + reset * gate(gru_state, target_rows, 2)
    )
    update = jax.nn.sigmoid(gate(gru_input, source_rows, 1) + gate(gru_state, target_rows, 1))
    return ((1.0 - update) * candidate + update * target_rows.astype(f32)).astype(bf16)


def replaced(memory, target_row, fresh):
    picks = row_picks(target_row, memory.shape[0])
    hit = jnp.sum(picks, axis=1, keepdims=True)
    placed = matmul(picks.astype(bf16), fresh)
    return jnp.where(hit > 0.5, placed, memory[...].astype(f32)).astype(bf16)


def step_scale(total):
    total = total[...].astype(f32)
    return step_length / jnp.sqrt(jnp.sum(total * total) + epsilon)


def stepped(master, total, scale):
    return master - scale * total.astype(f32)


def window_kernel(
    memory_hbm,
    near_ids_hbm,
    near_times_hbm,
    source_ids_hbm,
    target_ids_hbm,
    negative_ids_hbm,
    event_ticks_hbm,
    gru_input_hbm,
    gru_state_hbm,
    decoder_hbm,
    memory_out,
    master,
    last_total,
    logits_out,
    memory,
    near_ids,
    near_times,
    source_ids,
    target_ids,
    negative_ids,
    event_ticks,
    gru_input,
    gru_state,
    decoder,
    handed_source,
    handed_target,
    handed_memory,
    table,
    picks,
    stacked,
    target_rows,
    first_part,
    deltas,
    gradient,
    rounded,
    near_in,
    far_in,
    half_sums,
    total,
    load_sems,
    hand_sems,
    sum_sems,
    greeting,
):
    place = Place()
    barrier = pltpu.get_barrier_semaphore()
    greeted = [place.near(step)[0] for step in near_steps]
    greeted += [place.next_epoch(), place.last_epoch()]
    loads = [
        pltpu.make_async_copy(stored, held, load_sems.at[slot])
        for slot, (stored, held) in enumerate(
            (
                (source_ids_hbm, source_ids),
                (target_ids_hbm, target_ids),
                (negative_ids_hbm, negative_ids),
                (event_ticks_hbm, event_ticks),
                (near_ids_hbm, near_ids),
                (near_times_hbm, near_times),
                (memory_hbm, memory),
                (decoder_hbm, decoder),
                (gru_input_hbm, gru_input),
                (gru_state_hbm, gru_state),
            )
        )
    ]
    for load in loads[:8]:
        load.start()
    for step in far_steps:

        @pl.when((place.pair < half) | (place.far_pair(step) >= half))
        def _(step=step):
            pl.semaphore_signal(barrier, 1, device_id=place.far(step), device_id_type=MESH)

    for device in greeted:
        pl.semaphore_signal(barrier, 1, device_id=device, device_id_type=MESH)
    for load in loads[:6]:
        load.wait()

    ids = jnp.concatenate(
        [source_ids[0], target_ids[0], negative_ids[0], event_ticks[0]], axis=0
    ).astype(f32)
    columns = ids.T
    first_columns = [columns[:, 2 * kind : 2 * kind + 1] for kind in range(4)]
    second_columns = [columns[:, 2 * kind + 1 : 2 * kind + 2] for kind in range(4)]
    fill_table(table, near_ids, near_times)
    count = near_ids.shape[0]

    def loaded():
        for load in loads[6:8]:
            load.wait()
        for load in loads[8:]:
            load.start()
        master[...] = decoder[...].astype(f32).T

    gather_events(memory, first_columns, table, count, picks, stacked, target_rows, loaded)
    start = master[...].astype(bf16)
    projected = matmul_nt(start, stacked[...])
    link_gradient(stacked, projected, logits_out, 0, deltas, gradient, rounded.at[0])
    pl.semaphore_wait(barrier, len(greeted) + half - 1 + half * (place.pair // half))

    @pl.when(place.pair >= half)
    def _():
        pl.semaphore_signal(greeting, 1, device_id=place.mirror(), device_id_type=MESH)


    hands = []
    for slot, (kept, handed) in enumerate(
        ((source_ids, handed_source), (target_ids, handed_target))
    ):
        copy = pltpu.make_async_remote_copy(
            src_ref=kept.at[0],
            dst_ref=handed,
            send_sem=hand_sems.at[0, slot],
            recv_sem=hand_sems.at[1, slot],
            device_id=place.next_epoch(),
            device_id_type=MESH,
        )
        copy.start()
        hands.append(copy)
    sums = [
        TrainerSum(
            place,
            gradient,
            rounded.at[batch],
            near_in.at[batch],
            far_in.at[batch],
            half_sums.at[batch],
            (total, last_total)[batch],
            sum_sems.at[batch],
        )
        for batch in range(2)
    ]
    sums[0].scatter()
    for hand in hands:
        hand.wait_recv()
    for load in loads[8:]:
        load.wait()
    handed_rows = jnp.concatenate(
        [handed_source[...], handed_target[...], handed_source[...], handed_target[...]], axis=0
    ).astype(f32)
    handed_columns = handed_rows.T
    nodes = memory.shape[0]
    source = matmul(column_picks(handed_columns[:, 0:1], nodes), memory[...]).astype(bf16)
    target = matmul(column_picks(handed_columns[:, 2:3], nodes), memory[...]).astype(bf16)
    fresh = fresh_rows(source, target, gru_input, gru_state)
    sums[0].exchange()

    handed_memory[...] = replaced(memory, handed_rows[2:3, :], fresh)
    gather_events(
        handed_memory, second_columns, table, count, picks, stacked, target_rows, lambda: None
    )
    first_part[...] = matmul_nt(start, stacked[...])
    sums[0].bridge(greeting)
    sums[0].gather()
    sums[0].arrive()

    scale = step_scale(total)
    projected = first_part[...] - scale * matmul_nt(total[...], stacked[...])
    link_gradient(stacked, projected, logits_out, 2, deltas, gradient, rounded.at[1])
    sums[1].scatter()
    master[...] = stepped(master[...], total[...], scale)
    events = target_rows.shape[0]
    fresh = fresh_rows(stacked[0:events, :], target_rows[...], gru_input, gru_state)
    sums[1].exchange()
    sums[0].close()
    for hand in hands:
        hand.wait_send()
    memory_out[...] = replaced(handed_memory, ids[3:4, :], fresh)
    sums[1].bridge(None)
    sums[1].gather()
    sums[1].close()
    sums[1].arrive()


def results_kernel(memory, master, total, logits, memory_out, decoder_out, logits_out, decoder, sems):
    stores = [
        pltpu.make_async_copy(memory, memory_out.at[0], sems.at[0]),
        pltpu.make_async_copy(logits, logits_out.at[0], sems.at[1]),
    ]
    for store in stores:
        store.start()
    scale = step_scale(total)
    parts = decoder.shape[0] // 128
    for part in range(parts):
        rows = slice(128 * part, 128 * (part + 1))
        decoder[rows, :] = stepped(master[:, rows], total[:, rows], scale).T
        stores.append(
            pltpu.make_async_copy(
                decoder.at[rows], decoder_out.at[0, rows], sems.at[2 + part]
            )
        )
        stores[-1].start()
    for store in stores:
        store.wait()


def on_device(*given):
    node_memory, neighbour_ids, neighbour_ticks, source_ids, target_ids, negative_ids = given[:6]
    event_ticks, gru_input, gru_state, decoder_weight = given[6:]
    nodes, width = node_memory.shape
    hidden = decoder_weight.shape[1]
    batches, events = source_ids.shape[1:]
    vmem, dma = pltpu.VMEM, pltpu.SemaphoreType.DMA
    held = pl.BlockSpec(memory_space=vmem)
    kept = pl.pallas_call(
        window_kernel,
        out_shape=(
            vmem((nodes, width), bf16),
            vmem((hidden, width), f32),
            vmem((hidden, width), bf16),
            vmem((2 * batches, events), f32),
        ),
        in_specs=[pl.BlockSpec(memory_space=pltpu.HBM)] * 10,
        out_specs=(held,) * 4,
        scratch_shapes=[
            vmem(node_memory.shape, bf16),
            vmem(neighbour_ids.shape, jnp.int32),
            vmem(neighbour_ticks.shape, jnp.int32),
            vmem(source_ids.shape, jnp.int32),
            vmem(target_ids.shape, jnp.int32),
            vmem(negative_ids.shape, jnp.int32),
            vmem(event_ticks.shape, jnp.int32),
            vmem(gru_input.shape, bf16),
            vmem(gru_state.shape, bf16),
            vmem(decoder_weight.shape, bf16),
            vmem((batches, events), jnp.int32),
            vmem((batches, events), jnp.int32),
            vmem((nodes, width), bf16),
            vmem((64, nodes), bf16),
            vmem((3 * events, nodes), bf16),
            vmem((3 * events, width), bf16),
            vmem((events, width), bf16),
            vmem((hidden, 3 * events), f32),
            vmem((hidden, 3 * events), bf16),
            vmem((hidden, width), f32),
            vmem((batches, hidden, width), bf16),
            vmem((batches, near_count - 1, hidden // near_count, width), bf16),
            vmem((batches, far_count, hidden // near_count, width), bf16),
            vmem((batches, hidden // near_count, width), bf16),
            vmem((hidden, width), bf16),
            dma((10,)),
            dma((2, 2)),
            dma((batches, 2, 5)),
            pltpu.SemaphoreType.REGULAR,
        ],
        compiler_params=pltpu.CompilerParams(
            collective_id=0, has_side_effects=True, vmem_limit_bytes=50 * 2**20
        ),
        name="window",
    )(*(pltpu.with_memory_space_constraint(each, pltpu.HBM) for each in given))
    stored = pl.BlockSpec(memory_space=pltpu.HBM)
    return pl.pallas_call(
        results_kernel,
        out_shape=(
            jax.ShapeDtypeStruct((1, nodes, width), bf16),
            jax.ShapeDtypeStruct((1, width, hidden), f32),
            jax.ShapeDtypeStruct((1, 2 * batches, events), f32),
        ),
        in_specs=[held] * 4,
        out_specs=(stored,) * 3,
        scratch_shapes=[vmem((width, hidden), f32), dma((2 + width // 128,))],
        compiler_params=pltpu.CompilerParams(vmem_limit_bytes=8 * 2**20),
        name="results",
    )(*(pltpu.with_memory_space_constraint(each, pltpu.VMEM) for each in kept))


def solution(mesh):
    in_specs = (
        P(("batch", "mem"), None),
        P(None, ("batch", "mem")),
        P(None, ("batch", "mem")),
        P("epoch", None, ("batch", "mem")),
        P("epoch", None, ("batch", "mem")),
        P("epoch", None, ("batch", "mem")),
        P("epoch", None, ("batch", "mem")),
        P(),
        P(),
        P(),
    )
    out_specs = (
        P("epoch", ("batch", "mem"), None),
        P("epoch", None, None),
        P("epoch", None, ("batch", "mem")),
    )
    return jax.shard_map(
        on_device, mesh=mesh, in_specs=in_specs, out_specs=out_specs, check_vma=False
    )
```
